32 devices in a mesh: ctx: 16 (over z, x, core), tp: 2 (over y).
Axes of the slice: x: 2, y: 2, z: 4, core: 2. Of those that a mesh axis runs over, the one named last changes fastest.
Arguments:
- post_gate: bfloat16 [2048, 2048], P('ctx', 'tp'), may hold values from -6 to 6
- pre_gate: bfloat16 [2048, 2048], P('ctx', 'tp'), may hold values from -6 to 6
- features: bfloat16 [2048, 2048], P('ctx', 'tp'), may hold values from -6 to 6
- filters: float32 [2048, 2048], P('ctx', 'tp'), may hold values from -1.1 to 1.1
- token_ids: int32 [2048], P('ctx'), may hold values from 0 to 5
- out_weight: bfloat16 [2048, 2048], P('tp'), may hold values from -0.125 to 0.125
- out_grad: bfloat16 [2048, 2048], P('ctx', 'tp'), may hold values from -6 to 6
Outputs:
- output: bfloat16 [2048, 2048], P('ctx', 'tp')
- grad_post: bfloat16 [2048, 2048], P('ctx', 'tp')
- grad_pre: bfloat16 [2048, 2048], P('ctx', 'tp')
- grad_features: bfloat16 [2048, 2048], P('ctx', 'tp')
The draws below stay inside these ranges and needn't reach their ends.
All inputs are finite; a program needn't handle non-finite values.
Results may differ from the reference program's by a relative error of at most 0.022.
Values may be sent and summed in bfloat16 or wider, within the bound.
No kernel may reach another device: no remote copies, remote signals or barrier semaphores. Data moves between devices by JAX's collectives and lax.ppermute only.
A program may use at most 128 MiB of HBM per device.

```python
import math
import jax
import jax.numpy as jnp
from jax import lax

FEATURE_HALF = 2048
DOUT = 2048
BASES = 4
SEQUENCE_LENGTH = 2048


def draw_filters(key, part):
    key = jax.random.fold_in(key, 7)
    generator_seeds = jax.random.split(key, 6)
    lag_shifts = jnp.arange(SEQUENCE_LENGTH, dtype=jnp.float32)[:, None]
    slow_share = 0.5
    slow_mask = jax.random.bernoulli(generator_seeds[0], slow_share, (FEATURE_HALF,))
    slow_rate = jnp.exp(jax.random.uniform(generator_seeds[1], (FEATURE_HALF,), jnp.float32, math.log(0.1 / SEQUENCE_LENGTH), math.log(1.0 / SEQUENCE_LENGTH)))
    fast_rate = jnp.exp(jax.random.uniform(generator_seeds[2], (FEATURE_HALF,), jnp.float32, math.log(1.0 / 50.0), math.log(1.0 / 30.0)))
    falloff_speed = jnp.where(slow_mask, slow_rate, fast_rate)[None, :]
    impulse_sites = jax.random.randint(generator_seeds[3], (2,), 1, SEQUENCE_LENGTH).astype(jnp.float32)
    impulse_weights = jax.random.uniform(generator_seeds[4], (2, FEATURE_HALF), jnp.float32, math.log(0.55), math.log(0.8))
    impulse_omission = jnp.where(lag_shifts >= impulse_sites[0], impulse_weights[0][None, :], 0.0)
    impulse_omission = impulse_omission + jnp.where(lag_shifts >= impulse_sites[1], impulse_weights[1][None, :], 0.0)
    filter_magnitude = jnp.sqrt(jnp.expm1(-2.0 * falloff_speed) / jnp.expm1(-2.0 * falloff_speed * SEQUENCE_LENGTH))
    noisy_component = jnp.clip(jax.random.normal(generator_seeds[5], (SEQUENCE_LENGTH, FEATURE_HALF), jnp.float32), -4.0, 4.0)
    return filter_magnitude * jnp.exp(impulse_omission - falloff_speed * lag_shifts) * noisy_component


def with_ends(array, key, least, high):
    longest = array.shape.index(max(array.shape))
    spots = []
    for shift in (0, 1):
        where = [jax.random.randint(jax.random.fold_in(key, axis), (), 0, length) for axis, length in enumerate(array.shape)]
        where[longest] = (where[longest] + shift) % array.shape[longest]
        spots.append(tuple(where))
    return array.at[spots[0]].set(least).at[spots[1]].set(high)


def steps_of(own_key, extent, shards, least, high):
    def one(axis_at, parts):
        steps = jax.random.uniform(jax.random.fold_in(jax.random.fold_in(own_key, 6), axis_at), (parts,), jnp.float32, least / len(shards), high / len(shards))
        return jnp.repeat(jnp.exp(steps), extent[axis_at] // parts).reshape((-1,) + (1,) * (len(extent) - axis_at - 1))

    loudness = one(*shards[0])
    for cut in shards[1:]:
        loudness = loudness * one(*cut)
    return loudness


def scatter_about(rng, dims, scale, bound, cuts=(), held_as=jnp.bfloat16):
    result = scale * jax.random.normal(rng, dims, jnp.float32)
    if cuts:
        result = result * steps_of(rng, dims, cuts, -0.22, 0.18)
    return jnp.clip(result, -bound, bound).astype(held_as)


def setup_inputs(seed: int = 0) -> dict:
    key_of = jax.random.split(jax.random.key(seed), 8)
    return {
        "post_gate": scatter_about(key_of[0], (SEQUENCE_LENGTH, FEATURE_HALF), 1.0, 6.0, ((0, 16), (1, 2))),
        "pre_gate": scatter_about(key_of[1], (SEQUENCE_LENGTH, FEATURE_HALF), 1.0, 6.0, ((0, 16), (1, 2))),
        "features": scatter_about(key_of[2], (SEQUENCE_LENGTH, FEATURE_HALF), 1.0, 6.0, ((0, 16), (1, 2))),
        "filters": draw_filters(jax.random.fold_in(key_of[7], 71), 0),
        "token_ids": with_ends(jax.random.randint(key_of[4], (SEQUENCE_LENGTH,), 0, BASES + 2), jax.random.fold_in(key_of[4], 1), 0, (BASES + 2) - 1).astype(jnp.int32),
        "out_weight": scatter_about(key_of[5], (FEATURE_HALF, DOUT), FEATURE_HALF ** -0.5, 0.125, ((0, 2),)),
        "out_grad": scatter_about(key_of[6], (SEQUENCE_LENGTH, DOUT), 1.0, 6.0, ((0, 16), (1, 2))),
    }


def causal_mix(signal, kernel, backward):
    length = 2 * signal.shape[0]
    signal_spec = jnp.fft.rfft(signal, n=length, axis=0)
    kernel_spec = jnp.fft.rfft(kernel, n=length, axis=0)
    if backward:
        kernel_spec = jnp.conj(kernel_spec)
    return jnp.fft.irfft(signal_spec * kernel_spec, n=length, axis=0)[: signal.shape[0]]


def grouped_mix(signal, kernel, backward):
    seq_len, channel_count = signal.shape
    group_width = math.gcd(channel_count, 256)
    group_count = channel_count // group_width
    signal_groups = signal.reshape(seq_len, group_count, group_width).transpose(1, 0, 2)
    kernel_groups = kernel.reshape(seq_len, group_count, group_width).transpose(1, 0, 2)

    def one_group(pair_args):
        return causal_mix(pair_args[0], pair_args[1], backward)

    mixed_groups = lax.map(one_group, (signal_groups, kernel_groups))
    return mixed_groups.transpose(1, 0, 2).reshape(seq_len, channel_count)


def reference(post_gate, pre_gate, features, filters, token_ids, out_weight, out_grad):
    keep_mask = (token_ids < BASES).astype(jnp.float32)[:, None]
    post_wide = post_gate.astype(jnp.float32)
    pre_wide = pre_gate.astype(jnp.float32)
    feat_wide = features.astype(jnp.float32)
    mixer_input = pre_wide * feat_wide * keep_mask
    mixed_signal = grouped_mix(mixer_input, filters, False)
    gated_out = (post_wide * mixed_signal).astype(jnp.bfloat16)
    output = jnp.dot(gated_out, out_weight, preferred_element_type=jnp.float32).astype(jnp.bfloat16)
    grad_gated = jnp.dot(out_grad, out_weight.T, preferred_element_type=jnp.float32)
    grad_post = (grad_gated * mixed_signal).astype(jnp.bfloat16)
    grad_mixed = grad_gated * post_wide
    grad_input = grouped_mix(grad_mixed, filters, True)
    grad_pre = (grad_input * feat_wide * keep_mask).astype(jnp.bfloat16)
    grad_features = (grad_input * pre_wide * keep_mask).astype(jnp.bfloat16)
    return output, grad_post, grad_pre, grad_features
```

```python
import functools
import math

import jax
import jax.numpy as jnp
import numpy as np
from jax import lax
from jax.experimental import pallas as pl
from jax.experimental.pallas import tpu as pltpu
from jax.sharding import PartitionSpec as P

BASES = 4
LANES = 128
F32 = jnp.float32
BF16 = jnp.bfloat16


def complex_dft(values, sign):
    length = len(values)
    if length == 1:
        return values
    half = length // 2
    even = [
        (values[b][0] + values[b + half][0], values[b][1] + values[b + half][1])
        for b in range(half)
    ]
    odd = [
        twist(
            (values[b][0] - values[b + half][0], values[b][1] - values[b + half][1]),
            sign * b,
            length,
        )
        for b in range(half)
    ]
    even = complex_dft(even, sign)
    odd = complex_dft(odd, sign)
    return [part for pair in zip(even, odd) for part in pair]


def twist(value, step, length):
    real, imag = value
    step = step % length
    if step == 0:
        return real, imag
    if 4 * step == length:
        return -imag, real
    if 2 * step == length:
        return -real, -imag
    if 4 * step == 3 * length:
        return imag, -real
    cos = math.cos(2.0 * math.pi * step / length)
    sin = math.sin(2.0 * math.pi * step / length)
    if 8 * step % length == 0:
        root = math.sqrt(0.5)
        signed_cos = 1.0 if cos > 0 else -1.0
        signed_sin = 1.0 if sin > 0 else -1.0
        a = real * root
        b = imag * root
        if signed_cos == signed_sin:
            return (a - b, a + b) if signed_cos > 0 else (b - a, -a - b)
        return (a + b, b - a) if signed_cos > 0 else (-a - b, a - b)
    return real * cos - imag * sin, real * sin + imag * cos


def real_dft(values, length):
    if length == 2:
        if len(values) == 1:
            return [(values[0], None), (values[0], None)]
        return [(values[0] + values[1], None), (values[0] - values[1], None)]
    half, quarter = length // 2, length // 4
    if len(values) == length:
        total = [values[b] + values[b + half] for b in range(half)]
        rest = [values[b] - values[b + half] for b in range(half)]
    else:
        total = values
        rest = values
    out = [None] * (half + 1)
    for index, value in enumerate(real_dft(total, half)):
        out[2 * index] = value
    turned = [
        twist((rest[b], -rest[b + quarter]), -b, length) for b in range(quarter)
    ]
    for index, (real, imag) in enumerate(complex_dft(turned, -1)):
        place = 4 * index + 1
        if place <= half:
            out[place] = (real, imag)
        else:
            out[length - place] = (real, -imag)
    return out


def real_dft_transposed(spectrum, length, padded):
    if length == 2:
        first, second = spectrum[0][0], spectrum[1][0]
        return [first + second] if padded else [first + second, first - second]
    half, quarter = length // 2, length // 4
    total = real_dft_transposed(
        [spectrum[2 * index] for index in range(quarter + 1)], half, False
    )
    odd = []
    for index in range(quarter):
        place = 4 * index + 1
        if place <= half:
            odd.append(spectrum[place])
        else:
            real, imag = spectrum[length - place]
            odd.append((real, -imag))
    rest = [None] * half
    for b, value in enumerate(complex_dft(odd, 1)):
        real, imag = twist(value, b, length)
        rest[b] = real
        rest[b + quarter] = -imag
    low = [total[b] + rest[b] for b in range(half)]
    if padded:
        return low
    return low + [total[b] - rest[b] for b in range(half)]


def pack_rows(block, pieces):
    if pieces == 1:
        return block
    rows = block.shape[0] // pieces
    return jnp.concatenate(
        [block[i * rows : (i + 1) * rows] for i in range(pieces)], axis=1
    )


def unpack_rows(block, pieces):
    if pieces == 1:
        return block
    width = block.shape[1] // pieces
    return jnp.concatenate(
        [block[:, i * width : (i + 1) * width] for i in range(pieces)], axis=0
    )


def keep_rows(token_ref, width):
    keep = (token_ref[...] < BASES).astype(F32)
    length = keep.shape[1]
    return jnp.broadcast_to(keep, (length, length)).T[:, :1] * jnp.ones((1, width), F32)


def pack_inputs(n, token_ref, pre_ref, feat_ref, filt_ref, out_ref):
    width = pre_ref.shape[1] // n
    pieces = max(1, LANES // (2 * width))
    keep = keep_rows(token_ref, pre_ref.shape[1])
    mixer = pre_ref[...].astype(F32) * feat_ref[...].astype(F32) * keep
    filt = filt_ref[...]
    for k in range(n):
        cols = slice(k * width, (k + 1) * width)
        pair = jnp.concatenate([mixer[:, cols], filt[:, cols]], axis=1)
        out_ref[k] = pack_rows(pair, pieces).astype(BF16)


def pack_grad(n, rank_ref, own_ref, other_ref, weight_ref, post_ref, gated_ref, out_ref):
    width = post_ref.shape[1] // n
    pieces = max(1, LANES // width)
    columns = own_ref.shape[1]
    first = rank_ref[0] == 0
    own, other = own_ref[...], other_ref[...]
    left = jnp.where(first, own, other)
    right = jnp.where(first, other, own)
    dims = (((1,), (1,)), ((), ()))
    grad_gated = lax.dot_general(
        left, weight_ref[:, :columns], dims, preferred_element_type=F32
    ) + lax.dot_general(right, weight_ref[:, columns:], dims, preferred_element_type=F32)
    gated_ref[...] = grad_gated
    mixed = grad_gated * post_ref[...].astype(F32)
    for k in range(n):
        out_ref[k] = pack_rows(mixed[:, k * width : (k + 1) * width], pieces).astype(BF16)


def row_chunk(rows):
    return min(rows, 16)


def forward_blocks(n, blocks_ref, store):
    rows = blocks_ref.shape[1]
    chunk = row_chunk(rows)

    def body(index, carry):
        at = pl.ds(pl.multiple_of(index * chunk, chunk), chunk)
        spectrum = real_dft([blocks_ref[b, at].astype(F32) for b in range(n)], 2 * n)
        for m, (real, imag) in enumerate(spectrum):
            store(m, 0, at, real)
            store(m, 1, at, jnp.zeros_like(real) if imag is None else imag)
        return carry

    lax.fori_loop(0, rows // chunk, body, 0)


def inverse_blocks(n, spec_ref, out_ref):
    rows = out_ref.shape[1]
    chunk = row_chunk(rows)

    def body(index, carry):
        at = pl.ds(pl.multiple_of(index * chunk, chunk), chunk)
        spectrum = [(spec_ref[m, 0, at], spec_ref[m, 1, at]) for m in range(n + 1)]
        for b, value in enumerate(real_dft_transposed(spectrum, 2 * n, True)):
            out_ref[b, at] = value.astype(BF16)
        return carry

    lax.fori_loop(0, rows // chunk, body, 0)


def inverse_scale(m, n, length):
    edge = jnp.logical_or(m == 0, m == n)
    return jnp.where(edge, 0.5 / (n * length), 1.0 / (n * length))


def mix_forward(n, pair_ref, table_ref, back_ref, out_ref, filt_ref, mid_ref, spec_ref):
    length = table_ref.shape[1] // 2
    width = filt_ref.shape[2]
    pieces = max(1, LANES // width)
    pair_pieces = max(1, LANES // (2 * width))

    if pair_pieces == 1:

        def store(m, part, at, value):
            mid_ref[m, pl.ds(pl.multiple_of(part * length + at.start, at.size), at.size)] = (
                value.astype(BF16)
            )
    else:

        def store(m, part, at, value):
            for i in range(pair_pieces):
                start = part * length + i * (length // pair_pieces) + at.start
                mid_ref[m, pl.ds(pl.multiple_of(start, at.size), at.size)] = value[
                    :, i * 2 * width : (i + 1) * 2 * width
                ].astype(BF16)

    forward_blocks(n, pair_ref, store)

    def body(m, carry):
        spec = jnp.dot(table_ref[m], mid_ref[m], preferred_element_type=F32)
        real, imag = spec[:length, :width], spec[length:, :width]
        filt = spec[:, width:]
        filt_ref[m] = filt.astype(filt_ref.dtype)
        filt_real, filt_imag = filt[:length], filt[length:]
        scale = inverse_scale(m, n, length)
        product = jnp.concatenate(
            [
                (real * filt_real - imag * filt_imag) * scale,
                (real * filt_imag + imag * filt_real) * scale,
            ],
            axis=0,
        ).astype(BF16)
        mid = jnp.dot(back_ref[m], product, preferred_element_type=F32)
        spec_ref[m, 0] = pack_rows(mid[:length], pieces)
        spec_ref[m, 1] = pack_rows(mid[length:], pieces)
        return carry

    lax.fori_loop(0, n + 1, body, 0)
    inverse_blocks(n, spec_ref, out_ref)


def mix_backward(n, grad_ref, filt_ref, table_ref, back_ref, out_ref, spec_ref):
    length = table_ref.shape[1] // 2
    width = filt_ref.shape[2]
    pieces = max(1, LANES // width)

    def store(m, part, at, value):
        spec_ref[m, part, at] = value

    forward_blocks(n, grad_ref, store)

    def body(m, carry):
        mid = jnp.concatenate(
            [unpack_rows(spec_ref[m, 0], pieces), unpack_rows(spec_ref[m, 1], pieces)], axis=0
        ).astype(BF16)
        spec = jnp.dot(table_ref[m], mid, preferred_element_type=F32)
        real, imag = spec[:length], spec[length:]
        filt = filt_ref[m].astype(F32)
        filt_real, filt_imag = filt[:length], filt[length:]
        scale = inverse_scale(m, n, length)
        product = jnp.concatenate(
            [
                (filt_real * real + filt_imag * imag) * scale,
                (filt_real * imag - filt_imag * real) * scale,
            ],
            axis=0,
        ).astype(BF16)
        back = jnp.dot(back_ref[m], product, preferred_element_type=F32)
        spec_ref[m, 0] = pack_rows(back[:length], pieces)
        spec_ref[m, 1] = pack_rows(back[length:], pieces)
        return carry

    lax.fori_loop(0, n + 1, body, 0)
    inverse_blocks(n, spec_ref, out_ref)


def unpack_channels(n, packed_ref, pieces):
    return jnp.concatenate(
        [unpack_rows(packed_ref[k].astype(F32), pieces) for k in range(n)], axis=1
    )


def project(
    n, rank_ref, mixed_ref, post_ref, grad_ref, weight_ref, away_ref, home_ref, post_grad_ref
):
    channels = post_ref.shape[1]
    pieces = max(1, LANES // (channels // n))
    columns = home_ref.shape[1]
    mixed = unpack_channels(n, mixed_ref, pieces)
    gated = (post_ref[...].astype(F32) * mixed).astype(BF16)
    left = jnp.dot(gated, weight_ref[:, :columns], preferred_element_type=F32)
    right = jnp.dot(gated, weight_ref[:, columns:], preferred_element_type=F32)
    first = rank_ref[0] == 0
    home_ref[...] = jnp.where(first, left, right)
    away_ref[...] = jnp.where(first, right, left).astype(BF16)
    post_grad_ref[...] = (grad_ref[...] * mixed).astype(BF16)


def add_halves(home_ref, other_ref, out_ref):
    out_ref[...] = (home_ref[...] + other_ref[...].astype(F32)).astype(BF16)


def input_grads(n, packed_ref, token_ref, pre_ref, feat_ref, pre_grad_ref, feat_grad_ref):
    channels = pre_ref.shape[1]
    pieces = max(1, LANES // (channels // n))
    grad = unpack_channels(n, packed_ref, pieces) * keep_rows(token_ref, channels)
    pre_grad_ref[...] = (grad * feat_ref[...].astype(F32)).astype(BF16)
    feat_grad_ref[...] = (grad * pre_ref[...].astype(F32)).astype(BF16)


def dft_tables(n, length):
    full = 2 * n * length
    m = np.arange(n + 1)[:, None, None]
    q = np.arange(length)[None, :, None]
    p = np.arange(length)[None, None, :]
    angle = (2 * n * q + m) * p % full * (2.0 * math.pi / full)
    cos, sin = np.cos(angle), np.sin(angle)
    table = np.concatenate(
        [np.concatenate([cos, sin], axis=2), np.concatenate([-sin, cos], axis=2)], axis=1
    )
    return table.astype(jnp.bfloat16)


def call(kernel, outs, args, flops=0, scratch=(), scalars=0, limit=56):
    def size(x):
        return math.prod(x.shape) * np.dtype(x.dtype).itemsize

    return pl.pallas_call(
        kernel,
        out_shape=outs,
        in_specs=[pl.BlockSpec(memory_space=pltpu.SMEM)] * scalars
        + [pl.BlockSpec(memory_space=pltpu.VMEM)] * (len(args) - scalars),
        out_specs=jax.tree.map(lambda _: pl.BlockSpec(memory_space=pltpu.VMEM), outs),
        scratch_shapes=list(scratch),
        compiler_params=pltpu.CompilerParams(vmem_limit_bytes=limit * 2**20),
        cost_estimate=pl.CostEstimate(
            flops=flops,
            bytes_accessed=sum(size(x) for x in [*args, *jax.tree.leaves(outs)]),
            transcendentals=0,
        ),
    )(*args)


def exchange(block):
    return lax.all_to_all(block, "ctx", split_axis=0, concat_axis=0, tiled=True)


def swap_tp(block):
    count = lax.axis_size("tp")
    assert count == 2
    return lax.ppermute(block, "tp", [(0, 1), (1, 0)])


def on_device(
    tables, post_gate, pre_gate, features, filters, token_ids, out_weight, out_grad
):
    n = lax.axis_size("ctx")
    length, channels = post_gate.shape
    columns = out_grad.shape[1]
    width = channels // n
    pieces = max(1, LANES // width)
    pair_pieces = max(1, LANES // (2 * width))
    shape = jax.ShapeDtypeStruct
    one = shape((n, length // pieces, pieces * width), BF16)
    pair = shape((n, length // pair_pieces, pair_pieces * 2 * width), BF16)
    table, back = tables
    tokens = token_ids.reshape(1, length)
    rank = lax.axis_index("tp").astype(jnp.int32).reshape(1)
    filt_type = F32 if n <= 32 else BF16
    inner_flops = 2 * (n + 1) * (2 * length) ** 2 * width

    other_grad = swap_tp(out_grad)
    pair_out = call(
        functools.partial(pack_inputs, n), pair, (tokens, pre_gate, features, filters)
    )
    pair_in = exchange(pair_out)
    grad_gated, grad_out = call(
        functools.partial(pack_grad, n),
        (shape((length, channels), F32), one),
        (rank, out_grad, other_grad, out_weight, post_gate),
        flops=4 * length * channels * columns,
        scalars=1,
    )
    grad_in = exchange(grad_out)
    spec_scratch = pltpu.VMEM((n + 1, 2, length // pieces, pieces * width), F32)
    mixed_out, filt_spec = call(
        functools.partial(mix_forward, n),
        (one, shape((n + 1, 2 * length, width), filt_type)),
        (pair_in, table, back),
        flops=3 * inner_flops,
        scratch=[pltpu.VMEM((n + 1, 2 * length, 2 * width), BF16), spec_scratch],
    )
    mixed_in = exchange(mixed_out)
    grad_back_out = call(
        functools.partial(mix_backward, n),
        one,
        (grad_in, filt_spec, table, back),
        flops=2 * inner_flops,
        scratch=[spec_scratch],
    )
    grad_back_in = exchange(grad_back_out)
    away, home, grad_post = call(
        functools.partial(project, n),
        (
            shape((length, columns), BF16),
            shape((length, columns), F32),
            shape((length, channels), BF16),
        ),
        (rank, mixed_in, post_gate, grad_gated, out_weight),
        flops=4 * length * channels * columns,
        scalars=1,
    )
    output = call(add_halves, shape((length, columns), BF16), (home, swap_tp(away)))
    grad_pre, grad_features = call(
        functools.partial(input_grads, n),
        (shape((length, channels), BF16), shape((length, channels), BF16)),
        (grad_back_in, tokens, pre_gate, features),
    )
    return (output, grad_post, grad_pre, grad_features)


def solution(mesh):
    in_specs = (
        P("ctx", "tp"),
        P("ctx", "tp"),
        P("ctx", "tp"),
        P("ctx", "tp"),
        P("ctx"),
        P("tp", None),
        P("ctx", "tp"),
    )
    out_specs = (P("ctx", "tp"), P("ctx", "tp"), P("ctx", "tp"), P("ctx", "tp"))

    def run(*args):
        n = mesh.shape["ctx"]
        table = dft_tables(n, args[0].shape[0] // n)
        tables = (jnp.asarray(table), jnp.asarray(np.swapaxes(table, 1, 2)))
        return jax.shard_map(
            functools.partial(on_device, tables),
            mesh=mesh,
            in_specs=in_specs,
            out_specs=out_specs,
            check_vma=False,
        )(*args)

    return run
```

```python
import functools
import math

import jax
import jax.numpy as jnp
import numpy as np
from jax import lax
from jax.experimental import pallas as pl
from jax.experimental.pallas import tpu as pltpu
from jax.sharding import PartitionSpec as P

BASES = 4
LANES = 128
VMEM_MOST = 60 * 2**20
F32 = jnp.float32
BF16 = jnp.bfloat16


def complex_dft(values, sign):
    length = len(values)
    if length == 1:
        return values
    half = length // 2
    even = [
        (values[b][0] + values[b + half][0], values[b][1] + values[b + half][1])
        for b in range(half)
    ]
    odd = [
        twist(
            (values[b][0] - values[b + half][0], values[b][1] - values[b + half][1]),
            sign * b,
            length,
        )
        for b in range(half)
    ]
    even = complex_dft(even, sign)
    odd = complex_dft(odd, sign)
    return [part for pair in zip(even, odd) for part in pair]


def twist(value, step, length):
    real, imag = value
    step = step % length
    if step == 0:
        return real, imag
    if 4 * step == length:
        return -imag, real
    if 2 * step == length:
        return -real, -imag
    if 4 * step == 3 * length:
        return imag, -real
    cos = math.cos(2.0 * math.pi * step / length)
    sin = math.sin(2.0 * math.pi * step / length)
    if 8 * step % length == 0:
        root = math.sqrt(0.5)
        signed_cos = 1.0 if cos > 0 else -1.0
        signed_sin = 1.0 if sin > 0 else -1.0
        a = real * root
        b = imag * root
        if signed_cos == signed_sin:
            return (a - b, a + b) if signed_cos > 0 else (b - a, -a - b)
        return (a + b, b - a) if signed_cos > 0 else (-a - b, a - b)
    return real * cos - imag * sin, real * sin + imag * cos


def real_dft(values, length):
    if length == 2:
        if len(values) == 1:
            return [(values[0], None), (values[0], None)]
        return [(values[0] + values[1], None), (values[0] - values[1], None)]
    half, quarter = length // 2, length // 4
    if len(values) == length:
        total = [values[b] + values[b + half] for b in range(half)]
        rest = [values[b] - values[b + half] for b in range(half)]
    else:
        total = values
        rest = values
    out = [None] * (half + 1)
    for index, value in enumerate(real_dft(total, half)):
        out[2 * index] = value
    turned = [
        twist((rest[b], -rest[b + quarter]), -b, length) for b in range(quarter)
    ]
    for index, (real, imag) in enumerate(complex_dft(turned, -1)):
        place = 4 * index + 1
        if place <= half:
            out[place] = (real, imag)
        else:
            out[length - place] = (real, -imag)
    return out


def real_dft_transposed(spectrum, length, padded):
    if length == 2:
        first, second = spectrum[0][0], spectrum[1][0]
        return [first + second] if padded else [first + second, first - second]
    half, quarter = length // 2, length // 4
    total = real_dft_transposed(
        [spectrum[2 * index] for index in range(quarter + 1)], half, False
    )
    odd = []
    for index in range(quarter):
        place = 4 * index + 1
        if place <= half:
            odd.append(spectrum[place])
        else:
            real, imag = spectrum[length - place]
            odd.append((real, -imag))
    rest = [None] * half
    for b, value in enumerate(complex_dft(odd, 1)):
        real, imag = twist(value, b, length)
        rest[b] = real
        rest[b + quarter] = -imag
    low = [total[b] + rest[b] for b in range(half)]
    if padded:
        return low
    return low + [total[b] - rest[b] for b in range(half)]


def pack_rows(block, pieces):
    if pieces == 1:
        return block
    rows = block.shape[0] // pieces
    return jnp.concatenate(
        [block[i * rows : (i + 1) * rows] for i in range(pieces)], axis=1
    )


def unpack_rows(block, pieces):
    if pieces == 1:
        return block
    width = block.shape[1] // pieces
    return jnp.concatenate(
        [block[:, i * width : (i + 1) * width] for i in range(pieces)], axis=0
    )


def keep_rows(token_ref, width):
    keep = (token_ref[...] < BASES).astype(F32)
    length = keep.shape[1]
    return jnp.broadcast_to(keep, (length, length)).T[:, :1] * jnp.ones((1, width), F32)


def pack_inputs(dests, token_ref, pre_ref, feat_ref, filt_ref, out_ref):
    width = pre_ref.shape[1] // dests
    pieces = max(1, LANES // (2 * width))
    keep = keep_rows(token_ref, pre_ref.shape[1])
    mixer = pre_ref[...].astype(F32) * feat_ref[...].astype(F32) * keep
    filt = filt_ref[...]
    for k in range(dests):
        cols = slice(k * width, (k + 1) * width)
        pair = jnp.concatenate([mixer[:, cols], filt[:, cols]], axis=1)
        out_ref[k] = pack_rows(pair, pieces).astype(BF16)


def pack_grad(dests, rank_ref, own_ref, other_ref, weight_ref, post_ref, gated_ref, out_ref):
    width = post_ref.shape[1] // dests
    pieces = max(1, LANES // width)
    columns = own_ref.shape[1]
    first = rank_ref[0] == 0
    own, other = own_ref[...], other_ref[...]
    left = jnp.where(first, own, other)
    right = jnp.where(first, other, own)
    dims = (((1,), (1,)), ((), ()))
    grad_gated = lax.dot_general(
        left, weight_ref[:, :columns], dims, preferred_element_type=F32
    ) + lax.dot_general(right, weight_ref[:, columns:], dims, preferred_element_type=F32)
    gated_ref[...] = grad_gated
    mixed = grad_gated * post_ref[...].astype(F32)
    for k in range(dests):
        out_ref[k] = pack_rows(mixed[:, k * width : (k + 1) * width], pieces).astype(BF16)


def each(count, body):
    if count <= 32:
        for index in range(count):
            body(index)
    else:
        lax.fori_loop(0, count, lambda index, carry: (body(index), carry)[1], 0)


def row_chunk(rows):
    return min(rows, 16)


def forward_blocks(n, blocks_ref, store):
    rows = blocks_ref.shape[1]
    chunk = row_chunk(rows)

    def body(index, carry):
        at = pl.ds(pl.multiple_of(index * chunk, chunk), chunk)
        spectrum = real_dft([blocks_ref[b, at].astype(F32) for b in range(n)], 2 * n)
        for m, (real, imag) in enumerate(spectrum):
            store(m, 0, at, real)
            if imag is not None:
                store(m, 1, at, imag)
            elif n > 31:
                store(m, 1, at, jnp.zeros_like(real))
        return carry

    lax.fori_loop(0, rows // chunk, body, 0)


def inverse_blocks(n, spec_ref, out_ref, rows):
    chunk = row_chunk(rows)

    def body(index, carry):
        at = pl.ds(pl.multiple_of(index * chunk, chunk), chunk)
        spectrum = [
            (spec_ref[m, 0, at], spec_ref[m, 1, at] if 0 < m < n else None)
            for m in range(n + 1)
        ]
        for b, value in enumerate(real_dft_transposed(spectrum, 2 * n, True)):
            out_ref[b, at] = value.astype(BF16)
        return carry

    lax.fori_loop(0, rows // chunk, body, 0)


def is_edge(m, n):
    return isinstance(m, int) and m in (0, n)


def inverse_scale(m, n, length):
    if isinstance(m, int):
        return (0.5 if m in (0, n) else 1.0) / (n * length)
    edge = jnp.logical_or(m == 0, m == n)
    return jnp.where(edge, 0.5 / (n * length), 1.0 / (n * length))


def inner_dft(m, n, table_ref, mid):
    length = table_ref.shape[1] // 2
    if is_edge(m, n):
        return jnp.dot(table_ref[m, :, :length], mid[:length], preferred_element_type=F32)
    return jnp.dot(table_ref[m], mid, preferred_element_type=F32)


def inner_back(m, n, back_ref, real, imag, spec_ref, pieces):
    length = real.shape[0]
    scale = inverse_scale(m, n, length)
    product = jnp.concatenate([real * scale, imag * scale], axis=0).astype(BF16)
    if is_edge(m, n):
        back = jnp.dot(back_ref[m, :length], product, preferred_element_type=F32)
    else:
        back = jnp.dot(back_ref[m], product, preferred_element_type=F32)
        spec_ref[m, 1] = pack_rows(back[length:], pieces)
    spec_ref[m, 0] = pack_rows(back[:length], pieces)


def started(*copies):
    made = [pltpu.make_async_copy(*copy) for copy in copies]
    for copy in made:
        copy.start()
    return made


def mix_forward(
    n,
    pair_ref,
    grad_ref,
    table_hbm,
    back_hbm,
    out_ref,
    filt_hbm,
    table_ref,
    back_ref,
    filt_ref,
    mid_ref,
    spec_ref,
    sems,
):
    length = table_ref.shape[1] // 2
    width = filt_ref.shape[2] // 2
    pieces = max(1, LANES // width)
    pair_pieces = max(1, LANES // (2 * width))
    rows = length // pieces
    table_copy, back_copy = started(
        (table_hbm, table_ref, sems.at[0]), (back_hbm, back_ref, sems.at[1])
    )

    def store(m, part, at, value):
        for i in range(pair_pieces):
            start = part * length + i * (length // pair_pieces) + at.start
            mid_ref[m, pl.ds(pl.multiple_of(start, at.size), at.size)] = value[
                :, i * 2 * width : (i + 1) * 2 * width
            ].astype(BF16)

    forward_blocks(n, pair_ref, store)
    out_ref[:, rows:] = grad_ref[...]
    table_copy.wait()
    back_copy.wait()

    def body(m):
        spec = inner_dft(m, n, table_ref, mid_ref[m])
        real, imag = spec[:length, :width], spec[length:, :width]
        filt_real, filt_imag = spec[:length, width:], spec[length:, width:]
        filt_ref[m] = jnp.concatenate([filt_real, filt_imag], axis=1).astype(BF16)
        inner_back(
            m,
            n,
            back_ref,
            real * filt_real - imag * filt_imag,
            real * filt_imag + imag * filt_real,
            spec_ref,
            pieces,
        )

    each(n + 1, body)
    (filt_copy,) = started((filt_ref, filt_hbm, sems.at[2]))
    inverse_blocks(n, spec_ref, out_ref, rows)
    filt_copy.wait()


def mix_backward(
    n,
    both_ref,
    filt_hbm,
    table_hbm,
    back_hbm,
    out_ref,
    table_ref,
    back_ref,
    filt_ref,
    spec_ref,
    sems,
):
    length = table_ref.shape[1] // 2
    width = filt_ref.shape[2] // 2
    pieces = max(1, LANES // width)
    rows = length // pieces
    copies = started(
        (table_hbm, table_ref, sems.at[0]),
        (filt_hbm, filt_ref, sems.at[1]),
        (back_hbm, back_ref, sems.at[2]),
    )

    def store(m, part, at, value):
        spec_ref[m, part, at] = value

    forward_blocks(n, both_ref.at[:, rows:], store)
    for copy in copies:
        copy.wait()

    def body(m):
        mid = unpack_rows(spec_ref[m, 0], pieces)
        if not is_edge(m, n):
            mid = jnp.concatenate([mid, unpack_rows(spec_ref[m, 1], pieces)], axis=0)
        spec = inner_dft(m, n, table_ref, mid.astype(BF16))
        real, imag = spec[:length], spec[length:]
        filt = filt_ref[m].astype(F32)
        filt_real, filt_imag = filt[:, :width], filt[:, width:]
        inner_back(
            m,
            n,
            back_ref,
            filt_real * real + filt_imag * imag,
            filt_real * imag - filt_imag * real,
            spec_ref,
            pieces,
        )

    each(n + 1, body)
    inverse_blocks(n, spec_ref, out_ref, rows)


def unpack_channels(packed_ref, pieces):
    return jnp.concatenate(
        [unpack_rows(packed_ref[k].astype(F32), pieces) for k in range(packed_ref.shape[0])],
        axis=1,
    )


def project(
    pieces, rank_ref, both_ref, post_ref, grad_ref, weight_hbm, away_ref, home_ref, post_grad_ref,
    weight_ref, sems,
):
    rows = both_ref.shape[1] // 2
    channels, columns = post_ref.shape[1], home_ref.shape[1]
    rank = rank_ref[0]
    half = channels // 2
    copies = started(
        *(
            (
                weight_hbm.at[
                    pl.ds(k * half, half),
                    pl.ds(pl.multiple_of((1 - rank if side == 0 else rank) * columns, LANES), columns),
                ],
                weight_ref.at[side, pl.ds(k * half, half)],
                sems.at[side, k],
            )
            for side in range(2)
            for k in range(2)
        )
    )
    mixed = unpack_channels(both_ref.at[:, :rows], pieces)
    gated = (post_ref[...].astype(F32) * mixed).astype(BF16)
    post_grad_ref[...] = (grad_ref[...] * mixed).astype(BF16)

    def part(side, k):
        copies[2 * side + k].wait()
        return jnp.dot(
            gated[:, k * half : (k + 1) * half],
            weight_ref[side, k * half : (k + 1) * half],
            preferred_element_type=F32,
        )

    away_ref[...] = (part(0, 0) + part(0, 1)).astype(BF16)
    home_ref[...] = part(1, 0) + part(1, 1)


def add_halves(home_ref, other_ref, out_ref):
    out_ref[...] = (home_ref[...] + other_ref[...].astype(F32)).astype(BF16)


def input_grads(pieces, packed_ref, token_ref, pre_ref, feat_ref, pre_grad_ref, feat_grad_ref):
    grad = unpack_channels(packed_ref, pieces) * keep_rows(token_ref, pre_ref.shape[1])
    pre_grad_ref[...] = (grad * feat_ref[...].astype(F32)).astype(BF16)
    feat_grad_ref[...] = (grad * pre_ref[...].astype(F32)).astype(BF16)


def dft_tables(n, length):
    full = 2 * n * length
    m = np.arange(n + 1)[:, None, None]
    q = np.arange(length)[None, :, None]
    p = np.arange(length)[None, None, :]
    angle = (2 * n * q + m) * p % full * (2.0 * math.pi / full)
    cos, sin = np.cos(angle), np.sin(angle)
    table = np.concatenate(
        [np.concatenate([cos, sin], axis=2), np.concatenate([-sin, cos], axis=2)], axis=1
    )
    return table.astype(jnp.bfloat16)


def padded_bytes(shape, dtype):
    *rest, rows, lanes = (1, *shape)
    item = np.dtype(dtype).itemsize
    rows = -(-rows // 8) * 8
    return math.prod(rest) * rows * -(-lanes // LANES) * LANES * item


def call(kernel, outs, args, grid=None, blocks=None, out_blocks=None, flops=0, scratch=(), prefetch=0, limit=0):
    leaves = jax.tree.leaves(outs)
    tensors = args[prefetch:]

    def spec(array, block):
        if block == "hbm":
            return pl.BlockSpec(memory_space=pltpu.HBM)
        if block is None:
            rank = len(array.shape)
            if grid is None:
                return pl.BlockSpec(memory_space=pltpu.VMEM)
            return pl.BlockSpec(array.shape, lambda *_: (0,) * rank)
        return pl.BlockSpec(*block)

    blocks = blocks or [None] * len(tensors)
    out_blocks = out_blocks or [None] * len(leaves)
    in_specs = [spec(x, b) for x, b in zip(tensors, blocks)]
    out_specs = [spec(x, b) for x, b in zip(leaves, out_blocks)]
    held = sum(
        padded_bytes(b[0] if b else x.shape, x.dtype) * (1 if grid is None else 2)
        for x, b in [*zip(tensors, blocks), *zip(leaves, out_blocks)]
        if b != "hbm"
    ) + sum(padded_bytes(x.shape, x.dtype) for x in scratch if "sem" not in str(x.dtype))
    moved = sum(math.prod(x.shape) * np.dtype(x.dtype).itemsize for x in [*tensors, *leaves])
    return pl.pallas_call(
        kernel,
        out_shape=outs,
        grid_spec=pltpu.PrefetchScalarGridSpec(
            num_scalar_prefetch=prefetch,
            grid=grid or (),
            in_specs=in_specs,
            out_specs=out_specs if isinstance(outs, tuple) else out_specs[0],
            scratch_shapes=list(scratch),
        ),
        compiler_params=pltpu.CompilerParams(
            vmem_limit_bytes=min(max(held + 6 * 2**20, limit), VMEM_MOST)
        ),
        cost_estimate=pl.CostEstimate(flops=flops, bytes_accessed=moved, transcendentals=0),
    )(*args)


def exchange(block):
    return lax.all_to_all(block, "ctx", split_axis=0, concat_axis=0, tiled=True)


def swap_tp(block):
    count = lax.axis_size("tp")
    assert count == 2
    return lax.ppermute(block, "tp", [(0, 1), (1, 0)])


def on_device(
    tables, post_gate, pre_gate, features, filters, token_ids, out_weight, out_grad
):
    n = lax.axis_size("ctx")
    length, channels = post_gate.shape
    columns = out_grad.shape[1]
    width = channels // n
    pieces = max(1, LANES // width)
    pair_pieces = max(1, LANES // (2 * width))
    shape = jax.ShapeDtypeStruct
    one = shape((n, length // pieces, pieces * width), BF16)
    pair = shape((n, length // pair_pieces, pair_pieces * 2 * width), BF16)
    table, back = tables
    tokens = token_ids.reshape(1, length)
    rank = lax.axis_index("tp").astype(jnp.int32).reshape(1)
    inner_flops = 2 * (n + 1) * (2 * length) ** 2 * width
    spec_scratch = pltpu.VMEM((n + 1, 2, length // pieces, pieces * width), F32)

    def by_channels(steps):
        cut, dests = channels // steps, n // steps
        return (
            ((length, cut), lambda i, *_: (0, i)),
            ((dests, *one.shape[1:]), lambda i, *_: (i, 0, 0)),
            ((dests, *pair.shape[1:]), lambda i, *_: (i, 0, 0)),
        )

    other_grad = swap_tp(out_grad)
    steps = 2
    flat, packed, pair_block = by_channels(steps)
    pair_out = call(
        functools.partial(pack_inputs, n // steps),
        pair,
        (tokens, pre_gate, features, filters),
        grid=(steps,),
        blocks=[None, flat, flat, flat],
        out_blocks=[pair_block],
        limit=VMEM_MOST,
    )
    pair_in = exchange(pair_out)
    steps = 4
    flat, packed, _ = by_channels(steps)
    grad_gated, grad_out = call(
        functools.partial(pack_grad, n // steps),
        (shape((length, channels), F32), one),
        (rank, out_grad, other_grad, out_weight, post_gate),
        grid=(steps,),
        blocks=[
            None,
            None,
            ((channels // steps, 2 * columns), lambda i, *_: (i, 0)),
            flat,
        ],
        out_blocks=[flat, packed],
        flops=4 * length * channels * columns,
        prefetch=1,
        limit=57 * 2**20,
    )
    tables_scratch = [pltpu.VMEM(table.shape, BF16), pltpu.VMEM(back.shape, BF16)]
    filt_shape = shape((n + 1, length, 2 * width), BF16)
    both = shape((n, 2 * one.shape[1], one.shape[2]), BF16)
    both_out, filt_spec = call(
        functools.partial(mix_forward, n),
        (both, filt_shape),
        (pair_in, grad_out, table, back),
        blocks=[None, None, "hbm", "hbm"],
        out_blocks=[None, "hbm"],
        flops=3 * inner_flops,
        scratch=[
            *tables_scratch,
            pltpu.VMEM(filt_shape.shape, BF16),
            pltpu.VMEM((n + 1, 2 * length, 2 * width), BF16),
            spec_scratch,
            pltpu.SemaphoreType.DMA((3,)),
        ],
    )
    both_in = exchange(both_out)
    grad_back_out = call(
        functools.partial(mix_backward, n),
        one,
        (both_in, filt_spec, table, back),
        blocks=[None, "hbm", "hbm", "hbm"],
        flops=2 * inner_flops,
        scratch=[
            *tables_scratch,
            pltpu.VMEM(filt_shape.shape, BF16),
            spec_scratch,
            pltpu.SemaphoreType.DMA((3,)),
        ],
    )
    grad_back_in = exchange(grad_back_out)
    away, home, grad_post = call(
        functools.partial(project, pieces),
        (
            shape((length, columns), BF16),
            shape((length, columns), F32),
            shape((length, channels), BF16),
        ),
        (rank, both_in, post_gate, grad_gated, out_weight),
        blocks=[None, None, None, "hbm"],
        flops=4 * length * channels * columns,
        scratch=[
            pltpu.VMEM((2, channels, columns), BF16),
            pltpu.SemaphoreType.DMA((2, 2)),
        ],
        prefetch=1,
    )
    output = call(add_halves, shape((length, columns), BF16), (home, swap_tp(away)))
    steps = 2
    flat, packed, _ = by_channels(steps)
    grad_pre, grad_features = call(
        functools.partial(input_grads, pieces),
        (shape((length, channels), BF16), shape((length, channels), BF16)),
        (grad_back_in, tokens, pre_gate, features),
        grid=(steps,),
        blocks=[packed, None, flat, flat],
        out_blocks=[flat, flat],
    )
    return (output, grad_post, grad_pre, grad_features)


def solution(mesh):
    in_specs = (
        P("ctx", "tp"),
        P("ctx", "tp"),
        P("ctx", "tp"),
        P("ctx", "tp"),
        P("ctx"),
        P("tp", None),
        P("ctx", "tp"),
    )
    out_specs = (P("ctx", "tp"), P("ctx", "tp"), P("ctx", "tp"), P("ctx", "tp"))

    def run(*args):
        n = mesh.shape["ctx"]
        table = dft_tables(n, args[0].shape[0] // n)
        tables = (jnp.asarray(table), jnp.asarray(np.swapaxes(table, 1, 2)))
        return jax.shard_map(
            functools.partial(on_device, tables),
            mesh=mesh,
            in_specs=in_specs,
            out_specs=out_specs,
            check_vma=False,
        )(*args)

    return run
```

```python
import functools
import math

import jax
import jax.numpy as jnp
import numpy as np
from jax import lax
from jax.experimental import pallas as pl
from jax.experimental.pallas import tpu as pltpu
from jax.sharding import PartitionSpec as P

BASES = 4
LANES = 128
MATRIX_ROWS = 512
VMEM_GRANT = 24 * 2**20
F32 = jnp.float32
BF16 = jnp.bfloat16


def complex_dft(values, sign):
    length = len(values)
    if length == 1:
        return values
    half = length // 2
    even = [
        (values[b][0] + values[b + half][0], values[b][1] + values[b + half][1])
        for b in range(half)
    ]
    odd = [
        twist(
            (values[b][0] - values[b + half][0], values[b][1] - values[b + half][1]),
            sign * b,
            length,
        )
        for b in range(half)
    ]
    even = complex_dft(even, sign)
    odd = complex_dft(odd, sign)
    return [part for pair in zip(even, odd) for part in pair]


def twist(value, step, length):
    real, imag = value
    step = step % length
    if step == 0:
        return real, imag
    if 4 * step == length:
        return -imag, real
    if 2 * step == length:
        return -real, -imag
    if 4 * step == 3 * length:
        return imag, -real
    cos = math.cos(2.0 * math.pi * step / length)
    sin = math.sin(2.0 * math.pi * step / length)
    if 8 * step % length == 0:
        root = math.sqrt(0.5)
        signed_cos = 1.0 if cos > 0 else -1.0
        signed_sin = 1.0 if sin > 0 else -1.0
        a = real * root
        b = imag * root
        if signed_cos == signed_sin:
            return (a - b, a + b) if signed_cos > 0 else (b - a, -a - b)
        return (a + b, b - a) if signed_cos > 0 else (-a - b, a - b)
    return real * cos - imag * sin, real * sin + imag * cos


def real_dft(values, length):
    if length == 2:
        if len(values) == 1:
            return [(values[0], None), (values[0], None)]
        return [(values[0] + values[1], None), (values[0] - values[1], None)]
    half, quarter = length // 2, length // 4
    if len(values) == length:
        total = [values[b] + values[b + half] for b in range(half)]
        rest = [values[b] - values[b + half] for b in range(half)]
    else:
        total = values
        rest = values
    out = [None] * (half + 1)
    for index, value in enumerate(real_dft(total, half)):
        out[2 * index] = value
    turned = [
        twist((rest[b], -rest[b + quarter]), -b, length) for b in range(quarter)
    ]
    for index, (real, imag) in enumerate(complex_dft(turned, -1)):
        place = 4 * index + 1
        if place <= half:
            out[place] = (real, imag)
        else:
            out[length - place] = (real, -imag)
    return out


def real_dft_transposed(spectrum, length, padded):
    if length == 2:
        first, second = spectrum[0][0], spectrum[1][0]
        return [first + second] if padded else [first + second, first - second]
    half, quarter = length // 2, length // 4
    total = real_dft_transposed(
        [spectrum[2 * index] for index in range(quarter + 1)], half, False
    )
    odd = []
    for index in range(quarter):
        place = 4 * index + 1
        if place <= half:
            odd.append(spectrum[place])
        else:
            real, imag = spectrum[length - place]
            odd.append((real, -imag))
    rest = [None] * half
    for b, value in enumerate(complex_dft(odd, 1)):
        real, imag = twist(value, b, length)
        rest[b] = real
        rest[b + quarter] = -imag
    low = [total[b] + rest[b] for b in range(half)]
    if padded:
        return low
    return low + [total[b] - rest[b] for b in range(half)]


def pack_inputs(
    parts,
    token_hbm,
    pre_hbm,
    feat_hbm,
    filt_hbm,
    out_hbm,
    token_ref,
    pre_ref,
    feat_ref,
    filt_ref,
    out_ref,
    in_sems,
    out_sems,
):
    n, rows, _ = out_ref.shape
    width, dests = rows // 2, n // parts
    cut = dests * width
    (token_copy,) = started((token_hbm, token_ref, in_sems.at[3, 0]))
    copies = [
        started(
            *(
                (source.at[:, pl.ds(k * cut, cut)], target.at[:, pl.ds(k * cut, cut)], in_sems.at[i, k])
                for i, (source, target) in enumerate(
                    ((pre_hbm, pre_ref), (feat_hbm, feat_ref), (filt_hbm, filt_ref))
                )
            )
        )
        for k in range(parts)
    ]
    token_copy.wait()
    keep = (token_ref[...] < BASES).astype(F32)
    row = lax.broadcasted_iota(jnp.int32, (cut, cut), 0)
    column = lax.broadcasted_iota(jnp.int32, (cut, cut), 1)
    identity = jnp.where(row == column, 1.0, 0.0).astype(BF16)
    sent = []
    for k in range(parts):
        for copy in copies[k]:
            copy.wait()
        at = slice(k * cut, (k + 1) * cut)
        mixer = (pre_ref[:, at].astype(F32) * feat_ref[:, at].astype(F32)).astype(BF16)
        mixer = (times_transposed(identity, mixer) * keep).astype(BF16)
        filt = times_transposed(identity, filt_ref[:, at].astype(BF16)).astype(BF16)
        for j in range(dests):
            mine = slice(j * width, (j + 1) * width)
            out_ref[k * dests + j] = jnp.concatenate([mixer[mine], filt[mine]], axis=0)
        here = pl.ds(k * dests, dests)
        sent += started((out_ref.at[here], out_hbm.at[here], out_sems.at[k]))
    for copy in sent:
        copy.wait()


def own_grad(rank_ref, own_ref, weight_ref, out_ref):
    out_ref[...] = times_transposed(weight_ref[...], own_ref[...])


def times_transposed(left, right):
    return lax.dot_general(left, right, (((1,), (1,)), ((), ())), preferred_element_type=F32)


def pack_grad(
    dests, rank_ref, other_ref, weight_ref, part_ref, post_ref, gated_ref, out_ref, away_ref
):
    width = out_ref.shape[1]
    weight = weight_ref[...]
    away_ref[...] = weight
    grad_gated = part_ref[...] + times_transposed(weight, other_ref[...])
    gated_ref[...] = grad_gated
    mixed = grad_gated * post_ref[...].T.astype(F32)
    for k in range(dests):
        out_ref[k] = mixed[k * width : (k + 1) * width].astype(BF16)


def started(*copies):
    made = [pltpu.make_async_copy(*copy) for copy in copies]
    for copy in made:
        copy.start()
    return made


def forward_blocks(n, load, twist_ref, mid_ref):
    rows, length = mid_ref.shape[1], mid_ref.shape[2] // 2
    chunk = rows // row_chunks(rows)

    def body(index, carry):
        at = pl.ds(pl.multiple_of(index * chunk, chunk), chunk)
        spectrum = real_dft([load(b, at).astype(F32) for b in range(n)], 2 * n)
        for m, (real, imag) in enumerate(spectrum):
            cos, sin = twist_ref[m : m + 1], twist_ref[n + 1 + m : n + 2 + m]
            if m == 0:
                imag = jnp.zeros_like(real)
            elif imag is None:
                real, imag = real * cos, -(real * sin)
            else:
                real, imag = real * cos + imag * sin, imag * cos - real * sin
            mid_ref[m, at, :length] = real.astype(mid_ref.dtype)
            mid_ref[m, at, length:] = imag.astype(mid_ref.dtype)
        return carry

    lax.fori_loop(0, rows // chunk, body, 0, unroll=min(2, rows // chunk))


def inverse_blocks(n, twist_ref, spec_ref, store, after=None):
    rows, length = spec_ref.shape[1], spec_ref.shape[2] // 2
    chunk = rows // row_chunks(rows)

    def body(index, carry):
        at = pl.ds(pl.multiple_of(index * chunk, chunk), chunk)
        spectrum = [(0.5 * spec_ref[0, at, :length], None)]
        for m in range(1, n + 1):
            cos, sin = twist_ref[m : m + 1], twist_ref[n + 1 + m : n + 2 + m]
            real, imag = spec_ref[m, at, :length], spec_ref[m, at, length:]
            if m == n:
                spectrum.append((0.5 * (real * cos - imag * sin), None))
            else:
                spectrum.append((real * cos - imag * sin, real * sin + imag * cos))
        for b, value in enumerate(real_dft_transposed(spectrum, 2 * n, True)):
            store(b, at, value.astype(BF16))
        if after is not None:
            after(index, at)
        return carry

    lax.fori_loop(0, rows // chunk, body, 0, unroll=min(2, rows // chunk))


def inner_product(values_ref, matrix, first, last):
    _, rows, wide = values_ref.shape
    values = values_ref[first:last].reshape((last - first) * rows, wide).astype(BF16)
    return jnp.dot(values, matrix, preferred_element_type=F32)


def frequency_groups(n, rows):
    step = max(1, MATRIX_ROWS // rows)
    return [(first, min(first + step, n + 1)) for first in range(0, n + 1, step)]


def inner_back(n, matrix, prod_ref, spec_ref):
    rows = prod_ref.shape[1]
    for first, last in frequency_groups(n, rows):
        back = inner_product(prod_ref, matrix, first, last)
        spec_ref[first:last] = back.reshape(last - first, rows, back.shape[1])


def mix_forward(
    n,
    pair_ref,
    grad_ref,
    twist_ref,
    dft_hbm,
    both_ref,
    filt_ref,
    dft_ref,
    mid_ref,
    prod_ref,
    spec_ref,
    sems,
):
    length = twist_ref.shape[1]
    width = grad_ref.shape[1]
    (dft_copy,) = started((dft_hbm, dft_ref, sems.at[0]))
    forward_blocks(n, lambda b, at: pair_ref[b, at], twist_ref, mid_ref)
    both_ref[:, :, length:] = grad_ref[...]
    dft_copy.wait()
    for first, last in frequency_groups(n, 2 * width):
        spec = inner_product(mid_ref, dft_ref[0], first, last)
        for m in range(first, last):
            at = (m - first) * 2 * width
            signal, filt = spec[at : at + width], spec[at + width : at + 2 * width]
            filt_ref[m] = filt.astype(filt_ref.dtype)
            real, imag = signal[:, :length], signal[:, length:]
            filt_real, filt_imag = filt[:, :length], filt[:, length:]
            prod_ref[m, :, :length] = (real * filt_real - imag * filt_imag).astype(prod_ref.dtype)
            prod_ref[m, :, length:] = (real * filt_imag + imag * filt_real).astype(prod_ref.dtype)
    inner_back(n, dft_ref[1], prod_ref, spec_ref)

    def store(b, at, value):
        both_ref[b, at, :length] = value

    inverse_blocks(n, twist_ref, spec_ref, store)


def mix_backward(
    n,
    both_ref,
    post_ref,
    twist_ref,
    dft_ref,
    filt_ref,
    weight_ref,
    out_hbm,
    gated_hbm,
    away_hbm,
    mid_ref,
    prod_ref,
    spec_ref,
    out_ref,
    gated_ref,
    away_ref,
    sems,
):
    length = twist_ref.shape[1]
    width = out_ref.shape[1]
    mixed = channel_rows(both_ref, length).T.astype(F32)
    gated = (post_ref[...].astype(F32) * mixed).astype(BF16)
    gated_ref[...] = gated
    away_ref[...] = jnp.dot(gated, weight_ref[...], preferred_element_type=F32).astype(BF16)
    copies = started((away_ref, away_hbm, sems.at[0]), (gated_ref, gated_hbm, sems.at[1]))
    forward_blocks(n, lambda b, at: both_ref[b, at, length:], twist_ref, mid_ref)
    for first, last in frequency_groups(n, width):
        spec = inner_product(mid_ref, dft_ref[0], first, last)
        for m in range(first, last):
            at = (m - first) * width
            signal, filt = spec[at : at + width], filt_ref[m].astype(F32)
            real, imag = signal[:, :length], signal[:, length:]
            filt_real, filt_imag = filt[:, :length], filt[:, length:]
            prod_ref[m, :, :length] = (filt_real * real + filt_imag * imag).astype(prod_ref.dtype)
            prod_ref[m, :, length:] = (filt_real * imag - filt_imag * real).astype(prod_ref.dtype)
    inner_back(n, dft_ref[1], prod_ref, spec_ref)

    def store(b, at, value):
        out_ref[b, at] = value

    def out_copy(index, at):
        return pltpu.make_async_copy(out_ref.at[:, at], out_hbm.at[:, at], sems.at[2 + index])

    chunks = row_chunks(width)
    if chunks == 1:
        inverse_blocks(n, twist_ref, spec_ref, store)
        copies += started((out_ref, out_hbm, sems.at[2]))
    else:
        inverse_blocks(
            n, twist_ref, spec_ref, store, lambda index, at: out_copy(index, at).start()
        )
        step = width // chunks
        copies += [out_copy(index, pl.ds(index * step, step)) for index in range(chunks)]
    for copy in copies:
        copy.wait()


def row_chunks(rows):
    return max(1, rows // 16)


def channel_rows(blocks_ref, length):
    return jnp.concatenate(
        [blocks_ref[k, :, :length] for k in range(blocks_ref.shape[0])], axis=0
    )


def weight_copies(parts, side, weight_hbm, weight_ref, sems):
    channels, columns = weight_ref.shape
    rows = channels // parts
    start = pl.multiple_of(side * columns, LANES)
    return started(
        *(
            (
                weight_hbm.at[pl.ds(k * rows, rows), pl.ds(start, columns)],
                weight_ref.at[pl.ds(k * rows, rows)],
                sems[k],
            )
            for k in range(parts)
        )
    )


def part_products(copies, gated, weight_ref):
    rows = weight_ref.shape[0] // len(copies)
    total = None
    for k, copy in enumerate(copies):
        copy.wait()
        at = slice(k * rows, (k + 1) * rows)
        product = jnp.dot(gated[:, at], weight_ref[at], preferred_element_type=F32)
        total = product if total is None else total + product
    return total


def project_home(
    parts,
    rank_ref,
    gated_ref,
    both_ref,
    grad_ref,
    weight_hbm,
    home_ref,
    post_grad_ref,
    weight_ref,
    sems,
):
    copies = weight_copies(
        parts, rank_ref[0], weight_hbm, weight_ref, [sems.at[k] for k in range(parts)]
    )
    mixed = channel_rows(both_ref, grad_ref.shape[1]).astype(F32)
    post_grad_ref[...] = (grad_ref[...] * mixed).astype(BF16).T
    home_ref[...] = part_products(copies, gated_ref[...], weight_ref)


def finish(
    token_ref,
    packed_ref,
    pre_ref,
    feat_ref,
    home_ref,
    other_ref,
    pre_grad_ref,
    feat_grad_ref,
    out_ref,
):
    keep = (token_ref[...] < BASES).astype(BF16)
    grad = (channel_rows(packed_ref, packed_ref.shape[2]) * keep).T.astype(F32)
    pre_grad_ref[...] = (grad * feat_ref[...].astype(F32)).astype(BF16)
    feat_grad_ref[...] = (grad * pre_ref[...].astype(F32)).astype(BF16)
    out_ref[...] = (home_ref[...] + other_ref[...].astype(F32)).astype(BF16)


def dft_tables(n, length):
    index = np.arange(length)
    angle = index[:, None] * index[None, :] % length * (2.0 * math.pi / length)
    cos, sin = np.cos(angle), np.sin(angle)
    matrix = np.block([[cos, -sin], [sin, cos]])
    dft = np.stack([matrix, matrix.T / (n * length)]).astype(jnp.bfloat16)
    angle = np.arange(n + 1)[:, None] * index[None, :] * (math.pi / (n * length))
    twist = np.concatenate([np.cos(angle), np.sin(angle)], axis=0).astype(np.float32)
    return twist, dft


def call(kernel, outs, args, grid=None, blocks=None, out_blocks=None, flops=0, scratch=(), prefetch=0, from_hbm=()):
    leaves = jax.tree.leaves(outs)
    args = [
        pltpu.with_memory_space_constraint(x, pltpu.HBM) if k in from_hbm else x
        for k, x in enumerate(args)
    ]
    tensors = args[prefetch:]

    def spec(array, block):
        if block == "hbm":
            return pl.BlockSpec(memory_space=pltpu.HBM)
        if block is None:
            rank = len(array.shape)
            if grid is None:
                return pl.BlockSpec(memory_space=pltpu.VMEM)
            return pl.BlockSpec(array.shape, lambda *_: (0,) * rank)
        return pl.BlockSpec(*block)

    blocks = blocks or [None] * len(tensors)
    out_blocks = out_blocks or [None] * len(leaves)
    in_specs = [spec(x, b) for x, b in zip(tensors, blocks)]
    out_specs = [spec(x, b) for x, b in zip(leaves, out_blocks)]
    moved = sum(math.prod(x.shape) * np.dtype(x.dtype).itemsize for x in [*tensors, *leaves])
    return pl.pallas_call(
        kernel,
        out_shape=outs,
        grid_spec=pltpu.PrefetchScalarGridSpec(
            num_scalar_prefetch=prefetch,
            grid=grid or (),
            in_specs=in_specs,
            out_specs=out_specs if isinstance(outs, tuple) else out_specs[0],
            scratch_shapes=list(scratch),
        ),
        compiler_params=pltpu.CompilerParams(vmem_limit_bytes=VMEM_GRANT),
        cost_estimate=pl.CostEstimate(flops=flops, bytes_accessed=moved, transcendentals=0),
    )(*args)


def exchange(block):
    return lax.all_to_all(block, "ctx", split_axis=0, concat_axis=0, tiled=True)


def swap_tp(block):
    count = lax.axis_size("tp")
    assert count == 2
    return lax.ppermute(block, "tp", [(0, 1), (1, 0)])


def on_device(
    tables, post_gate, pre_gate, features, filters, token_ids, out_weight, out_grad
):
    n = lax.axis_size("ctx")
    length, channels = post_gate.shape
    columns = out_grad.shape[1]
    width = channels // n
    shape = jax.ShapeDtypeStruct
    one = (n, width, length)
    pair = (n, 2 * width, length)
    both = (n, width, 2 * length)
    twist, dft = tables
    tokens = token_ids.reshape(1, length)
    rank = lax.axis_index("tp").astype(jnp.int32).reshape(1)
    inner_flops = 2 * (n + 1) * (2 * length) ** 2 * width
    spec_shape = (n + 1, width, 2 * length)
    narrow = BF16 if width >= 16 else F32
    spec_scratch = pltpu.VMEM(spec_shape, F32)
    narrow_scratch = pltpu.VMEM(spec_shape, narrow)

    def by_channels(steps):
        cut, dests = channels // steps, n // steps
        return (
            ((length, cut), lambda i, *_: (0, i)),
            ((cut, length), lambda i, *_: (i, 0)),
            ((dests, *one[1:]), lambda i, *_: (i, 0, 0)),
        )

    other_grad = swap_tp(out_grad)
    parts = 4
    pair_out = call(
        functools.partial(pack_inputs, parts),
        pltpu.HBM(pair, BF16),
        (tokens, pre_gate, features, filters),
        blocks=["hbm"] * 4,
        out_blocks=["hbm"],
        from_hbm=range(4),
        scratch=[
            pltpu.VMEM(tokens.shape, jnp.int32),
            pltpu.VMEM((length, channels), BF16),
            pltpu.VMEM((length, channels), BF16),
            pltpu.VMEM((length, channels), F32),
            pltpu.VMEM(pair, BF16),
            pltpu.SemaphoreType.DMA((4, parts)),
            pltpu.SemaphoreType.DMA((parts,)),
        ],
    )
    pair_in = exchange(pair_out)
    steps = 4
    flat, turned, packed = by_channels(steps)
    weight_block = (channels // steps, columns)
    grad_part = call(
        own_grad,
        pltpu.VMEM((channels, length), F32),
        (rank, out_grad, out_weight),
        grid=(steps,),
        blocks=[None, (weight_block, lambda i, rank: (i, rank[0]))],
        out_blocks=[turned],
        flops=2 * length * channels * columns,
        prefetch=1,
        from_hbm=(1, 2),
    )
    grad_gated, grad_out, away_weight = call(
        functools.partial(pack_grad, n // steps),
        (
            pltpu.HBM((channels, length), F32),
            pltpu.VMEM(one, BF16),
            pltpu.VMEM((channels, columns), BF16),
        ),
        (rank, other_grad, out_weight, grad_part, post_gate),
        grid=(steps,),
        blocks=[None, (weight_block, lambda i, rank: (i, 1 - rank[0])), turned, flat],
        out_blocks=[turned, packed, (weight_block, lambda i, *_: (i, 0))],
        flops=2 * length * channels * columns,
        prefetch=1,
        from_hbm=(2, 4),
    )
    both_out, filt_spec, kept_dft = call(
        functools.partial(mix_forward, n),
        (
            shape(both, BF16),
            pltpu.VMEM(spec_shape, narrow),
            pltpu.VMEM(dft.shape, BF16),
        ),
        (pair_in, grad_out, twist, dft),
        blocks=[None, None, None, "hbm"],
        from_hbm=(3,),
        flops=3 * inner_flops,
        scratch=[
            pltpu.VMEM((n + 1, 2 * width, 2 * length), BF16),
            narrow_scratch,
            spec_scratch,
            pltpu.SemaphoreType.DMA((1,)),
        ],
    )
    both_in = exchange(both_out)
    grad_back_out, gated, away = call(
        functools.partial(mix_backward, n),
        (
            pltpu.HBM(one, BF16),
            pltpu.HBM((length, channels), BF16),
            pltpu.HBM((length, columns), BF16),
        ),
        (both_in, post_gate, twist, kept_dft, filt_spec, away_weight),
        out_blocks=["hbm", "hbm", "hbm"],
        flops=2 * inner_flops + 2 * length * channels * columns,
        scratch=[
            narrow_scratch,
            narrow_scratch,
            spec_scratch,
            pltpu.VMEM(one, BF16),
            pltpu.VMEM((length, channels), BF16),
            pltpu.VMEM((length, columns), BF16),
            pltpu.SemaphoreType.DMA((2 + row_chunks(width),)),
        ],
    )
    grad_back_in = exchange(grad_back_out)
    other_part = swap_tp(away)
    parts = 2
    home, grad_post = call(
        functools.partial(project_home, parts),
        (shape((length, columns), F32), shape((length, channels), BF16)),
        (rank, gated, both_in, grad_gated, out_weight),
        grid=(1,),
        blocks=[None, (one, lambda *_: (0, 0, 0)), None, "hbm"],
        flops=2 * length * channels * columns,
        scratch=[pltpu.VMEM((channels, columns), BF16), pltpu.SemaphoreType.DMA((parts,))],
        prefetch=1,
    )
    steps = 2
    flat, _, packed = by_channels(steps)
    half = ((length, columns // steps), lambda i, *_: (0, i))
    grad_pre, grad_features, output = call(
        finish,
        (
            shape((length, channels), BF16),
            shape((length, channels), BF16),
            shape((length, columns), BF16),
        ),
        (tokens, grad_back_in, pre_gate, features, home, other_part),
        grid=(steps,),
        blocks=[None, packed, flat, flat, half, half],
        out_blocks=[flat, flat, half],
    )
    return (output, grad_post, grad_pre, grad_features)


def solution(mesh):
    in_specs = (
        P("ctx", "tp"),
        P("ctx", "tp"),
        P("ctx", "tp"),
        P("ctx", "tp"),
        P("ctx"),
        P("tp", None),
        P("ctx", "tp"),
    )
    out_specs = (P("ctx", "tp"), P("ctx", "tp"), P("ctx", "tp"), P("ctx", "tp"))

    def run(*args):
        n = mesh.shape["ctx"]
        tables = tuple(jnp.asarray(x) for x in dft_tables(n, args[0].shape[0] // n))
        return jax.shard_map(
            functools.partial(on_device, tables),
            mesh=mesh,
            in_specs=in_specs,
            out_specs=out_specs,
            check_vma=False,
        )(*args)

    return run
```

```python
import functools
import math

import jax
import jax.numpy as jnp
import numpy as np
from jax import lax
from jax.experimental import pallas as pl
from jax.experimental.pallas import tpu as pltpu
from jax.sharding import PartitionSpec as P

BASES = 4
LANES = 128
VMEM_GRANT = 24 * 2**20
F32 = jnp.float32
BF16 = jnp.bfloat16


def complex_dft(values, sign):
    length = len(values)
    if length == 1:
        return values
    half = length // 2
    even = [
        (values[b][0] + values[b + half][0], values[b][1] + values[b + half][1])
        for b in range(half)
    ]
    odd = [
        twist(
            (values[b][0] - values[b + half][0], values[b][1] - values[b + half][1]),
            sign * b,
            length,
        )
        for b in range(half)
    ]
    even = complex_dft(even, sign)
    odd = complex_dft(odd, sign)
    return [part for pair in zip(even, odd) for part in pair]


def twist(value, step, length):
    real, imag = value
    step = step % length
    if step == 0:
        return real, imag
    if 4 * step == length:
        return -imag, real
    if 2 * step == length:
        return -real, -imag
    if 4 * step == 3 * length:
        return imag, -real
    cos = math.cos(2.0 * math.pi * step / length)
    sin = math.sin(2.0 * math.pi * step / length)
    if 8 * step % length == 0:
        root = math.sqrt(0.5)
        signed_cos = 1.0 if cos > 0 else -1.0
        signed_sin = 1.0 if sin > 0 else -1.0
        a = real * root
        b = imag * root
        if signed_cos == signed_sin:
            return (a - b, a + b) if signed_cos > 0 else (b - a, -a - b)
        return (a + b, b - a) if signed_cos > 0 else (-a - b, a - b)
    return real * cos - imag * sin, real * sin + imag * cos


def real_dft(values, length):
    if length == 2:
        if len(values) == 1:
            return [(values[0], None), (values[0], None)]
        return [(values[0] + values[1], None), (values[0] - values[1], None)]
    half, quarter = length // 2, length // 4
    if len(values) == length:
        total = [values[b] + values[b + half] for b in range(half)]
        rest = [values[b] - values[b + half] for b in range(half)]
    else:
        total = values
        rest = values
    out = [None] * (half + 1)
    for index, value in enumerate(real_dft(total, half)):
        out[2 * index] = value
    turned = [
        twist((rest[b], -rest[b + quarter]), -b, length) for b in range(quarter)
    ]
    for index, (real, imag) in enumerate(complex_dft(turned, -1)):
        place = 4 * index + 1
        if place <= half:
            out[place] = (real, imag)
        else:
            out[length - place] = (real, -imag)
    return out


def real_dft_transposed(spectrum, length, padded):
    if length == 2:
        first, second = spectrum[0][0], spectrum[1][0]
        return [first + second] if padded else [first + second, first - second]
    half, quarter = length // 2, length // 4
    total = real_dft_transposed(
        [spectrum[2 * index] for index in range(quarter + 1)], half, False
    )
    odd = []
    for index in range(quarter):
        place = 4 * index + 1
        if place <= half:
            odd.append(spectrum[place])
        else:
            real, imag = spectrum[length - place]
            odd.append((real, -imag))
    rest = [None] * half
    for b, value in enumerate(complex_dft(odd, 1)):
        real, imag = twist(value, b, length)
        rest[b] = real
        rest[b + quarter] = -imag
    low = [total[b] + rest[b] for b in range(half)]
    if padded:
        return low
    return low + [total[b] - rest[b] for b in range(half)]


def pack_inputs(dests, token_ref, pre_ref, feat_ref, filt_ref, out_ref):
    width = out_ref.shape[1] // 2
    keep = (token_ref[...] < BASES).astype(BF16)
    mixer = (pre_ref[...].astype(F32) * feat_ref[...].astype(F32)).astype(BF16).T * keep
    filt = filt_ref[...].astype(BF16).T
    for k in range(dests):
        at = slice(k * width, (k + 1) * width)
        out_ref[k] = jnp.concatenate([mixer[at], filt[at]], axis=0)


def own_grad(rank_ref, own_ref, weight_ref, out_ref):
    out_ref[...] = times_transposed(weight_ref[...], own_ref[...])


def times_transposed(left, right):
    return lax.dot_general(left, right, (((1,), (1,)), ((), ())), preferred_element_type=F32)


def pack_grad(
    dests, rank_ref, other_ref, weight_ref, part_ref, post_ref, gated_ref, out_ref, away_ref
):
    width = out_ref.shape[1]
    weight = weight_ref[...]
    away_ref[...] = weight
    grad_gated = part_ref[...] + times_transposed(weight, other_ref[...])
    gated_ref[...] = grad_gated
    mixed = grad_gated * post_ref[...].T.astype(F32)
    for k in range(dests):
        out_ref[k] = mixed[k * width : (k + 1) * width].astype(BF16)


def started(*copies):
    made = [pltpu.make_async_copy(*copy) for copy in copies]
    for copy in made:
        copy.start()
    return made


def forward_blocks(n, blocks, twist_ref, mid_ref, rows):
    length = mid_ref.shape[2] // 2
    for m, (real, imag) in enumerate(real_dft([x.astype(F32) for x in blocks], 2 * n)):
        cos, sin = twist_ref[m : m + 1], twist_ref[n + 1 + m : n + 2 + m]
        if m == 0:
            imag = jnp.zeros_like(real)
        elif imag is None:
            real, imag = real * cos, -(real * sin)
        else:
            real, imag = real * cos + imag * sin, imag * cos - real * sin
        mid_ref[m, rows, :length] = real.astype(mid_ref.dtype)
        mid_ref[m, rows, length:] = imag.astype(mid_ref.dtype)


def inverse_blocks(n, back, twist_ref):
    length = back.shape[1] // 2
    rows = back.shape[0] // (n + 1)
    spectrum = []
    for m in range(n + 1):
        cos, sin = twist_ref[m : m + 1], twist_ref[n + 1 + m : n + 2 + m]
        at = slice(m * rows, (m + 1) * rows)
        real, imag = back[at, :length], back[at, length:]
        if m == 0:
            spectrum.append((0.5 * real, None))
        elif m == n:
            spectrum.append((0.5 * (real * cos - imag * sin), None))
        else:
            spectrum.append((real * cos - imag * sin, real * sin + imag * cos))
    return [x.astype(BF16) for x in real_dft_transposed(spectrum, 2 * n, True)]


def inner_product(values_ref, matrix):
    count, rows, wide = values_ref.shape
    values = values_ref[...].reshape(count * rows, wide).astype(BF16)
    return jnp.dot(values, matrix, preferred_element_type=F32)


def row_chunks(rows):
    return max(1, rows // 16)


def mix_forward(
    n,
    pair_ref,
    grad_ref,
    twist_ref,
    dft_hbm,
    both_ref,
    filt_ref,
    dft_ref,
    mid_ref,
    prod_ref,
    sems,
):
    length = twist_ref.shape[1]
    width = grad_ref.shape[1]
    chunks = row_chunks(width)
    step = width // chunks
    (dft_copy,) = started((dft_hbm, dft_ref, sems.at[0]))
    both_ref[:, :, length:] = grad_ref[...]
    for c in range(chunks):
        at = slice(c * step, (c + 1) * step)
        for kind in range(2):
            start = kind * width + c * step
            blocks = [pair_ref[b, start : start + step] for b in range(n)]
            forward_blocks(
                n, blocks, twist_ref, mid_ref.at[c], slice(kind * step, (kind + 1) * step)
            )
        if c == 0:
            dft_copy.wait()
        spec = inner_product(mid_ref.at[c], dft_ref[0])
        for m in range(n + 1):
            first = 2 * m * step
            signal, filt = spec[first : first + step], spec[first + step : first + 2 * step]
            filt_ref[m, at] = filt.astype(filt_ref.dtype)
            real, imag = signal[:, :length], signal[:, length:]
            filt_real, filt_imag = filt[:, :length], filt[:, length:]
            prod_ref[c, m, :, :length] = (real * filt_real - imag * filt_imag).astype(
                prod_ref.dtype
            )
            prod_ref[c, m, :, length:] = (real * filt_imag + imag * filt_real).astype(
                prod_ref.dtype
            )
        back = inner_product(prod_ref.at[c], dft_ref[1])
        for b, value in enumerate(inverse_blocks(n, back, twist_ref)):
            both_ref[b, at, :length] = value


def mix_backward(
    n,
    both_ref,
    post_ref,
    twist_ref,
    dft_ref,
    filt_ref,
    weight_ref,
    out_hbm,
    gated_hbm,
    away_hbm,
    mid_ref,
    prod_ref,
    out_ref,
    gated_ref,
    away_ref,
    sems,
):
    length = twist_ref.shape[1]
    width = out_ref.shape[1]
    mixed = channel_rows(both_ref, length).T.astype(F32)
    gated = (post_ref[...].astype(F32) * mixed).astype(BF16)
    gated_ref[...] = gated
    away_ref[...] = jnp.dot(gated, weight_ref[...], preferred_element_type=F32).astype(BF16)
    copies = started((away_ref, away_hbm, sems.at[0]), (gated_ref, gated_hbm, sems.at[1]))
    chunks = row_chunks(width)
    step = width // chunks
    for c in range(chunks):
        at = slice(c * step, (c + 1) * step)
        blocks = [both_ref[b, at, length:] for b in range(n)]
        forward_blocks(n, blocks, twist_ref, mid_ref.at[c], slice(0, step))
        spec = inner_product(mid_ref.at[c], dft_ref[0])
        for m in range(n + 1):
            signal, filt = spec[m * step : (m + 1) * step], filt_ref[m, at].astype(F32)
            real, imag = signal[:, :length], signal[:, length:]
            filt_real, filt_imag = filt[:, :length], filt[:, length:]
            prod_ref[c, m, :, :length] = (filt_real * real + filt_imag * imag).astype(
                prod_ref.dtype
            )
            prod_ref[c, m, :, length:] = (filt_real * imag - filt_imag * real).astype(
                prod_ref.dtype
            )
        back = inner_product(prod_ref.at[c], dft_ref[1])
        for b, value in enumerate(inverse_blocks(n, back, twist_ref)):
            out_ref[b, at] = value
        if chunks == 1:
            copies += started((out_ref, out_hbm, sems.at[2]))
        else:
            rows = pl.ds(c * step, step)
            copies += started((out_ref.at[:, rows], out_hbm.at[:, rows], sems.at[2 + c]))
    for copy in copies:
        copy.wait()


def channel_rows(blocks_ref, length):
    return jnp.concatenate(
        [blocks_ref[k, :, :length] for k in range(blocks_ref.shape[0])], axis=0
    )


def weight_copies(parts, side, weight_hbm, weight_ref, sems):
    channels, columns = weight_ref.shape
    rows = channels // parts
    start = pl.multiple_of(side * columns, LANES)
    return started(
        *(
            (
                weight_hbm.at[pl.ds(k * rows, rows), pl.ds(start, columns)],
                weight_ref.at[pl.ds(k * rows, rows)],
                sems[k],
            )
            for k in range(parts)
        )
    )


def part_products(copies, gated, weight_ref):
    rows = weight_ref.shape[0] // len(copies)
    total = None
    for k, copy in enumerate(copies):
        copy.wait()
        at = slice(k * rows, (k + 1) * rows)
        product = jnp.dot(gated[:, at], weight_ref[at], preferred_element_type=F32)
        total = product if total is None else total + product
    return total


def project_home(
    parts,
    rank_ref,
    gated_ref,
    both_ref,
    grad_ref,
    weight_hbm,
    home_ref,
    post_grad_ref,
    weight_ref,
    sems,
):
    copies = weight_copies(
        parts, rank_ref[0], weight_hbm, weight_ref, [sems.at[k] for k in range(parts)]
    )
    mixed = channel_rows(both_ref, grad_ref.shape[1]).astype(F32)
    post_grad_ref[...] = (grad_ref[...] * mixed).astype(BF16).T
    home_ref[...] = part_products(copies, gated_ref[...], weight_ref)


def finish(
    token_ref,
    packed_ref,
    pre_ref,
    feat_ref,
    home_ref,
    other_ref,
    pre_grad_ref,
    feat_grad_ref,
    out_ref,
):
    keep = (token_ref[...] < BASES).astype(BF16)
    grad = (channel_rows(packed_ref, packed_ref.shape[2]) * keep).T.astype(F32)
    pre_grad_ref[...] = (grad * feat_ref[...].astype(F32)).astype(BF16)
    feat_grad_ref[...] = (grad * pre_ref[...].astype(F32)).astype(BF16)
    out_ref[...] = (home_ref[...] + other_ref[...].astype(F32)).astype(BF16)


def dft_tables(n, length):
    index = np.arange(length)
    angle = index[:, None] * index[None, :] % length * (2.0 * math.pi / length)
    cos, sin = np.cos(angle), np.sin(angle)
    matrix = np.block([[cos, -sin], [sin, cos]])
    dft = np.stack([matrix, matrix.T / (n * length)]).astype(jnp.bfloat16)
    angle = np.arange(n + 1)[:, None] * index[None, :] * (math.pi / (n * length))
    twist = np.concatenate([np.cos(angle), np.sin(angle)], axis=0).astype(np.float32)
    return twist, dft


def call(kernel, outs, args, grid=None, blocks=None, out_blocks=None, flops=0, scratch=(), prefetch=0, from_hbm=()):
    leaves = jax.tree.leaves(outs)
    args = [
        pltpu.with_memory_space_constraint(x, pltpu.HBM) if k in from_hbm else x
        for k, x in enumerate(args)
    ]
    tensors = args[prefetch:]

    def spec(array, block):
        if block == "hbm":
            return pl.BlockSpec(memory_space=pltpu.HBM)
        if block is None:
            rank = len(array.shape)
            if grid is None:
                return pl.BlockSpec(memory_space=pltpu.VMEM)
            return pl.BlockSpec(array.shape, lambda *_: (0,) * rank)
        return pl.BlockSpec(*block)

    blocks = blocks or [None] * len(tensors)
    out_blocks = out_blocks or [None] * len(leaves)
    in_specs = [spec(x, b) for x, b in zip(tensors, blocks)]
    out_specs = [spec(x, b) for x, b in zip(leaves, out_blocks)]
    moved = sum(math.prod(x.shape) * np.dtype(x.dtype).itemsize for x in [*tensors, *leaves])
    return pl.pallas_call(
        kernel,
        out_shape=outs,
        grid_spec=pltpu.PrefetchScalarGridSpec(
            num_scalar_prefetch=prefetch,
            grid=grid or (),
            in_specs=in_specs,
            out_specs=out_specs if isinstance(outs, tuple) else out_specs[0],
            scratch_shapes=list(scratch),
        ),
        compiler_params=pltpu.CompilerParams(vmem_limit_bytes=VMEM_GRANT),
        cost_estimate=pl.CostEstimate(flops=flops, bytes_accessed=moved, transcendentals=0),
    )(*args)


def exchange(block):
    return lax.all_to_all(block, "ctx", split_axis=0, concat_axis=0, tiled=True)


def swap_tp(block):
    count = lax.axis_size("tp")
    assert count == 2
    return lax.ppermute(block, "tp", [(0, 1), (1, 0)])


def on_device(
    tables, post_gate, pre_gate, features, filters, token_ids, out_weight, out_grad
):
    n = lax.axis_size("ctx")
    length, channels = post_gate.shape
    columns = out_grad.shape[1]
    width = channels // n
    shape = jax.ShapeDtypeStruct
    one = (n, width, length)
    pair = (n, 2 * width, length)
    both = (n, width, 2 * length)
    twist, dft = tables
    tokens = token_ids.reshape(1, length)
    rank = lax.axis_index("tp").astype(jnp.int32).reshape(1)
    inner_flops = 2 * (n + 1) * (2 * length) ** 2 * width
    spec_shape = (n + 1, width, 2 * length)
    narrow = BF16 if width >= 16 else F32
    chunks = row_chunks(width)
    narrow_scratch = pltpu.VMEM((chunks, n + 1, width // chunks, 2 * length), narrow)

    def by_channels(steps):
        cut, dests = channels // steps, n // steps
        return (
            ((length, cut), lambda i, *_: (0, i)),
            ((cut, length), lambda i, *_: (i, 0)),
            ((dests, *one[1:]), lambda i, *_: (i, 0, 0)),
        )

    other_grad = swap_tp(out_grad)
    steps = 2
    flat, _, _ = by_channels(steps)
    pair_out = call(
        functools.partial(pack_inputs, n // steps),
        pltpu.HBM(pair, BF16),
        (tokens, pre_gate, features, filters),
        grid=(steps,),
        blocks=[None, flat, flat, flat],
        out_blocks=[((n // steps, *pair[1:]), lambda i, *_: (i, 0, 0))],
        from_hbm=range(4),
    )
    pair_in = exchange(pair_out)
    steps = 4
    flat, turned, packed = by_channels(steps)
    weight_block = (channels // steps, columns)
    grad_part = call(
        own_grad,
        pltpu.VMEM((channels, length), F32),
        (rank, out_grad, out_weight),
        grid=(steps,),
        blocks=[None, (weight_block, lambda i, rank: (i, rank[0]))],
        out_blocks=[turned],
        flops=2 * length * channels * columns,
        prefetch=1,
        from_hbm=(1, 2),
    )
    grad_gated, grad_out, away_weight = call(
        functools.partial(pack_grad, n // steps),
        (
            pltpu.HBM((channels, length), F32),
            pltpu.VMEM(one, BF16),
            pltpu.VMEM((channels, columns), BF16),
        ),
        (rank, other_grad, out_weight, grad_part, post_gate),
        grid=(steps,),
        blocks=[None, (weight_block, lambda i, rank: (i, 1 - rank[0])), turned, flat],
        out_blocks=[turned, packed, (weight_block, lambda i, *_: (i, 0))],
        flops=2 * length * channels * columns,
        prefetch=1,
        from_hbm=(2, 4),
    )
    both_out, filt_spec, kept_dft = call(
        functools.partial(mix_forward, n),
        (
            shape(both, BF16),
            pltpu.VMEM(spec_shape, narrow),
            pltpu.VMEM(dft.shape, BF16),
        ),
        (pair_in, grad_out, twist, dft),
        blocks=[None, None, None, "hbm"],
        from_hbm=(3,),
        flops=3 * inner_flops,
        scratch=[
            pltpu.VMEM((chunks, n + 1, 2 * width // chunks, 2 * length), BF16),
            narrow_scratch,
            pltpu.SemaphoreType.DMA((1,)),
        ],
    )
    both_in = exchange(both_out)
    grad_back_out, gated, away = call(
        functools.partial(mix_backward, n),
        (
            pltpu.HBM(one, BF16),
            pltpu.HBM((length, channels), BF16),
            pltpu.HBM((length, columns), BF16),
        ),
        (both_in, post_gate, twist, kept_dft, filt_spec, away_weight),
        out_blocks=["hbm", "hbm", "hbm"],
        flops=2 * inner_flops + 2 * length * channels * columns,
        scratch=[
            narrow_scratch,
            narrow_scratch,
            pltpu.VMEM(one, BF16),
            pltpu.VMEM((length, channels), BF16),
            pltpu.VMEM((length, columns), BF16),
            pltpu.SemaphoreType.DMA((2 + chunks,)),
        ],
    )
    grad_back_in = exchange(grad_back_out)
    other_part = swap_tp(away)
    parts = 2
    home, grad_post = call(
        functools.partial(project_home, parts),
        (shape((length, columns), F32), shape((length, channels), BF16)),
        (rank, gated, both_in, grad_gated, out_weight),
        grid=(1,),
        blocks=[None, (one, lambda *_: (0, 0, 0)), None, "hbm"],
        flops=2 * length * channels * columns,
        scratch=[pltpu.VMEM((channels, columns), BF16), pltpu.SemaphoreType.DMA((parts,))],
        prefetch=1,
    )
    steps = 2
    flat, _, packed = by_channels(steps)
    half = ((length, columns // steps), lambda i, *_: (0, i))
    grad_pre, grad_features, output = call(
        finish,
        (
            shape((length, channels), BF16),
            shape((length, channels), BF16),
            shape((length, columns), BF16),
        ),
        (tokens, grad_back_in, pre_gate, features, home, other_part),
        grid=(steps,),
        blocks=[None, packed, flat, flat, half, half],
        out_blocks=[flat, flat, half],
    )
    return (output, grad_post, grad_pre, grad_features)


def solution(mesh):
    in_specs = (
        P("ctx", "tp"),
        P("ctx", "tp"),
        P("ctx", "tp"),
        P("ctx", "tp"),
        P("ctx"),
        P("tp", None),
        P("ctx", "tp"),
    )
    out_specs = (P("ctx", "tp"), P("ctx", "tp"), P("ctx", "tp"), P("ctx", "tp"))

    def run(*args):
        n = mesh.shape["ctx"]
        tables = tuple(jnp.asarray(x) for x in dft_tables(n, args[0].shape[0] // n))
        return jax.shard_map(
            functools.partial(on_device, tables),
            mesh=mesh,
            in_specs=in_specs,
            out_specs=out_specs,
            check_vma=False,
        )(*args)

    return run
```

```python
import functools
import math

import jax
import jax.numpy as jnp
import numpy as np
from jax import lax
from jax.experimental import pallas as pl
from jax.experimental.pallas import tpu as pltpu
from jax.sharding import PartitionSpec as P

BASES = 4
LANES = 128
VMEM_GRANT = 24 * 2**20
F32 = jnp.float32
BF16 = jnp.bfloat16


def complex_dft(values, sign):
    length = len(values)
    if length == 1:
        return values
    half = length // 2
    even = [
        (values[b][0] + values[b + half][0], values[b][1] + values[b + half][1])
        for b in range(half)
    ]
    odd = [
        twist(
            (values[b][0] - values[b + half][0], values[b][1] - values[b + half][1]),
            sign * b,
            length,
        )
        for b in range(half)
    ]
    even = complex_dft(even, sign)
    odd = complex_dft(odd, sign)
    return [part for pair in zip(even, odd) for part in pair]


def twist(value, step, length):
    real, imag = value
    step = step % length
    if step == 0:
        return real, imag
    if 4 * step == length:
        return -imag, real
    if 2 * step == length:
        return -real, -imag
    if 4 * step == 3 * length:
        return imag, -real
    cos = math.cos(2.0 * math.pi * step / length)
    sin = math.sin(2.0 * math.pi * step / length)
    if 8 * step % length == 0:
        root = math.sqrt(0.5)
        signed_cos = 1.0 if cos > 0 else -1.0
        signed_sin = 1.0 if sin > 0 else -1.0
        a = real * root
        b = imag * root
        if signed_cos == signed_sin:
            return (a - b, a + b) if signed_cos > 0 else (b - a, -a - b)
        return (a + b, b - a) if signed_cos > 0 else (-a - b, a - b)
    return real * cos - imag * sin, real * sin + imag * cos


def real_dft(values, length):
    if length == 2:
        if len(values) == 1:
            return [(values[0], None), (values[0], None)]
        return [(values[0] + values[1], None), (values[0] - values[1], None)]
    half, quarter = length // 2, length // 4
    if len(values) == length:
        total = [values[b] + values[b + half] for b in range(half)]
        rest = [values[b] - values[b + half] for b in range(half)]
    else:
        total = values
        rest = values
    out = [None] * (half + 1)
    for index, value in enumerate(real_dft(total, half)):
        out[2 * index] = value
    turned = [
        twist((rest[b], -rest[b + quarter]), -b, length) for b in range(quarter)
    ]
    for index, (real, imag) in enumerate(complex_dft(turned, -1)):
        place = 4 * index + 1
        if place <= half:
            out[place] = (real, imag)
        else:
            out[length - place] = (real, -imag)
    return out


def real_dft_transposed(spectrum, length, padded):
    if length == 2:
        first, second = spectrum[0][0], spectrum[1][0]
        return [first + second] if padded else [first + second, first - second]
    half, quarter = length // 2, length // 4
    total = real_dft_transposed(
        [spectrum[2 * index] for index in range(quarter + 1)], half, False
    )
    odd = []
    for index in range(quarter):
        place = 4 * index + 1
        if place <= half:
            odd.append(spectrum[place])
        else:
            real, imag = spectrum[length - place]
            odd.append((real, -imag))
    rest = [None] * half
    for b, value in enumerate(complex_dft(odd, 1)):
        real, imag = twist(value, b, length)
        rest[b] = real
        rest[b + quarter] = -imag
    low = [total[b] + rest[b] for b in range(half)]
    if padded:
        return low
    return low + [total[b] - rest[b] for b in range(half)]


def pack_inputs(dests, token_ref, pre_ref, feat_ref, filt_ref, out_ref):
    width = out_ref.shape[1] // 2
    keep = (token_ref[...] < BASES).astype(BF16)
    mixer = (pre_ref[...].astype(F32) * feat_ref[...].astype(F32)).astype(BF16).T * keep
    filt = filt_ref[...].astype(BF16).T
    for k in range(dests):
        at = slice(k * width, (k + 1) * width)
        out_ref[k] = jnp.concatenate([mixer[at], filt[at]], axis=0)


def own_grad(rank_ref, own_ref, weight_ref, out_ref):
    out_ref[...] = times_transposed(weight_ref[...], own_ref[...])


def times_transposed(left, right):
    return lax.dot_general(left, right, (((1,), (1,)), ((), ())), preferred_element_type=F32)


def pack_grad(
    dests,
    rank_ref,
    other_ref,
    weight_ref,
    part_ref,
    post_ref,
    dft_ref,
    gated_ref,
    out_ref,
    away_ref,
    kept_dft_ref,
):
    width = out_ref.shape[1]
    weight = weight_ref[...]
    away_ref[...] = weight
    kept_dft_ref[...] = dft_ref[...]
    grad_gated = part_ref[...] + times_transposed(weight, other_ref[...])
    gated_ref[...] = grad_gated
    mixed = grad_gated * post_ref[...].T.astype(F32)
    for k in range(dests):
        out_ref[k] = mixed[k * width : (k + 1) * width].astype(BF16)


def started(*copies):
    made = [pltpu.make_async_copy(*copy) for copy in copies]
    for copy in made:
        copy.start()
    return made


def forward_blocks(n, blocks, twist_ref, mid_ref, rows):
    length = mid_ref.shape[2] // 2
    for m, (real, imag) in enumerate(real_dft([x.astype(F32) for x in blocks], 2 * n)):
        cos, sin = twist_ref[m : m + 1], twist_ref[n + 1 + m : n + 2 + m]
        if m == 0:
            imag = jnp.zeros_like(real)
        elif imag is None:
            real, imag = real * cos, -(real * sin)
        else:
            real, imag = real * cos + imag * sin, imag * cos - real * sin
        mid_ref[m, rows, :length] = real.astype(mid_ref.dtype)
        mid_ref[m, rows, length:] = imag.astype(mid_ref.dtype)


def inverse_blocks(n, back, twist_ref):
    length = back.shape[1] // 2
    rows = back.shape[0] // (n + 1)
    spectrum = []
    for m in range(n + 1):
        cos, sin = twist_ref[m : m + 1], twist_ref[n + 1 + m : n + 2 + m]
        at = slice(m * rows, (m + 1) * rows)
        real, imag = back[at, :length], back[at, length:]
        if m == 0:
            spectrum.append((0.5 * real, None))
        elif m == n:
            spectrum.append((0.5 * (real * cos - imag * sin), None))
        else:
            spectrum.append((real * cos - imag * sin, real * sin + imag * cos))
    return [x.astype(BF16) for x in real_dft_transposed(spectrum, 2 * n, True)]


def inner_product(values_ref, matrix):
    count, rows, wide = values_ref.shape
    values = values_ref[...].reshape(count * rows, wide).astype(BF16)
    return jnp.dot(values, matrix, preferred_element_type=F32)


def row_chunks(rows):
    return max(1, rows // 16)


def mix_forward(
    n,
    pair_ref,
    grad_ref,
    twist_ref,
    dft_ref,
    both_ref,
    filt_ref,
    mid_ref,
    prod_ref,
):
    length = twist_ref.shape[1]
    width = grad_ref.shape[1]
    chunks = row_chunks(width)
    step = width // chunks
    both_ref[:, :, length:] = grad_ref[...]
    for c in range(chunks):
        at = slice(c * step, (c + 1) * step)
        for kind in range(2):
            start = kind * width + c * step
            blocks = [pair_ref[b, start : start + step] for b in range(n)]
            forward_blocks(
                n, blocks, twist_ref, mid_ref.at[c], slice(kind * step, (kind + 1) * step)
            )
        spec = inner_product(mid_ref.at[c], dft_ref[0])
        for m in range(n + 1):
            first = 2 * m * step
            signal, filt = spec[first : first + step], spec[first + step : first + 2 * step]
            filt_ref[m, at] = filt.astype(filt_ref.dtype)
            real, imag = signal[:, :length], signal[:, length:]
            filt_real, filt_imag = filt[:, :length], filt[:, length:]
            prod_ref[c, m, :, :length] = (real * filt_real - imag * filt_imag).astype(
                prod_ref.dtype
            )
            prod_ref[c, m, :, length:] = (real * filt_imag + imag * filt_real).astype(
                prod_ref.dtype
            )
        back = inner_product(prod_ref.at[c], dft_ref[1])
        for b, value in enumerate(inverse_blocks(n, back, twist_ref)):
            both_ref[b, at, :length] = value


def mix_backward(
    n,
    both_ref,
    post_ref,
    twist_ref,
    dft_ref,
    filt_ref,
    weight_ref,
    out_hbm,
    gated_hbm,
    away_hbm,
    mid_ref,
    prod_ref,
    out_ref,
    gated_ref,
    away_ref,
    sems,
):
    length = twist_ref.shape[1]
    width = out_ref.shape[1]
    mixed = channel_rows(both_ref, length).T.astype(F32)
    gated = (post_ref[...].astype(F32) * mixed).astype(BF16)
    gated_ref[...] = gated
    away_ref[...] = jnp.dot(gated, weight_ref[...], preferred_element_type=F32).astype(BF16)
    copies = started((away_ref, away_hbm, sems.at[0]), (gated_ref, gated_hbm, sems.at[1]))
    chunks = row_chunks(width)
    step = width // chunks
    for c in range(chunks):
        at = slice(c * step, (c + 1) * step)
        blocks = [both_ref[b, at, length:] for b in range(n)]
        forward_blocks(n, blocks, twist_ref, mid_ref.at[c], slice(0, step))
        spec = inner_product(mid_ref.at[c], dft_ref[0])
        for m in range(n + 1):
            signal, filt = spec[m * step : (m + 1) * step], filt_ref[m, at].astype(F32)
            real, imag = signal[:, :length], signal[:, length:]
            filt_real, filt_imag = filt[:, :length], filt[:, length:]
            prod_ref[c, m, :, :length] = (filt_real * real + filt_imag * imag).astype(
                prod_ref.dtype
            )
            prod_ref[c, m, :, length:] = (filt_real * imag - filt_imag * real).astype(
                prod_ref.dtype
            )
        back = inner_product(prod_ref.at[c], dft_ref[1])
        for b, value in enumerate(inverse_blocks(n, back, twist_ref)):
            out_ref[b, at] = value
        if chunks == 1:
            copies += started((out_ref, out_hbm, sems.at[2]))
        else:
            rows = pl.ds(c * step, step)
            copies += started((out_ref.at[:, rows], out_hbm.at[:, rows], sems.at[2 + c]))
    for copy in copies:
        copy.wait()


def channel_rows(blocks_ref, length):
    return jnp.concatenate(
        [blocks_ref[k, :, :length] for k in range(blocks_ref.shape[0])], axis=0
    )


def weight_copies(parts, side, weight_hbm, weight_ref, sems):
    channels, columns = weight_ref.shape
    rows = channels // parts
    start = pl.multiple_of(side * columns, LANES)
    return started(
        *(
            (
                weight_hbm.at[pl.ds(k * rows, rows), pl.ds(start, columns)],
                weight_ref.at[pl.ds(k * rows, rows)],
                sems[k],
            )
            for k in range(parts)
        )
    )


def part_products(copies, gated, weight_ref):
    rows = weight_ref.shape[0] // len(copies)
    total = None
    for k, copy in enumerate(copies):
        copy.wait()
        at = slice(k * rows, (k + 1) * rows)
        product = jnp.dot(gated[:, at], weight_ref[at], preferred_element_type=F32)
        total = product if total is None else total + product
    return total


def project_home(
    parts,
    rank_ref,
    gated_ref,
    both_ref,
    grad_ref,
    weight_hbm,
    home_ref,
    post_grad_ref,
    weight_ref,
    sems,
):
    copies = weight_copies(
        parts, rank_ref[0], weight_hbm, weight_ref, [sems.at[k] for k in range(parts)]
    )
    mixed = channel_rows(both_ref, grad_ref.shape[1]).astype(F32)
    post_grad_ref[...] = (grad_ref[...] * mixed).astype(BF16).T
    home_ref[...] = part_products(copies, gated_ref[...], weight_ref)


def finish(
    token_ref,
    packed_ref,
    pre_ref,
    feat_ref,
    home_ref,
    other_ref,
    pre_grad_ref,
    feat_grad_ref,
    out_ref,
):
    keep = (token_ref[...] < BASES).astype(BF16)
    grad = (channel_rows(packed_ref, packed_ref.shape[2]) * keep).T.astype(F32)
    pre_grad_ref[...] = (grad * feat_ref[...].astype(F32)).astype(BF16)
    feat_grad_ref[...] = (grad * pre_ref[...].astype(F32)).astype(BF16)
    out_ref[...] = (home_ref[...] + other_ref[...].astype(F32)).astype(BF16)


def dft_tables(n, length):
    index = np.arange(length)
    angle = index[:, None] * index[None, :] % length * (2.0 * math.pi / length)
    cos, sin = np.cos(angle), np.sin(angle)
    matrix = np.block([[cos, -sin], [sin, cos]])
    dft = np.stack([matrix, matrix.T / (n * length)]).astype(jnp.bfloat16)
    angle = np.arange(n + 1)[:, None] * index[None, :] * (math.pi / (n * length))
    twist = np.concatenate([np.cos(angle), np.sin(angle)], axis=0).astype(np.float32)
    return twist, dft


def call(kernel, outs, args, grid=None, blocks=None, out_blocks=None, flops=0, scratch=(), prefetch=0, from_hbm=()):
    leaves = jax.tree.leaves(outs)
    args = [
        pltpu.with_memory_space_constraint(x, pltpu.HBM) if k in from_hbm else x
        for k, x in enumerate(args)
    ]
    tensors = args[prefetch:]

    def spec(array, block):
        if block == "hbm":
            return pl.BlockSpec(memory_space=pltpu.HBM)
        if block is None:
            rank = len(array.shape)
            if grid is None:
                return pl.BlockSpec(memory_space=pltpu.VMEM)
            return pl.BlockSpec(array.shape, lambda *_: (0,) * rank)
        return pl.BlockSpec(*block)

    blocks = blocks or [None] * len(tensors)
    out_blocks = out_blocks or [None] * len(leaves)
    in_specs = [spec(x, b) for x, b in zip(tensors, blocks)]
    out_specs = [spec(x, b) for x, b in zip(leaves, out_blocks)]
    moved = sum(math.prod(x.shape) * np.dtype(x.dtype).itemsize for x in [*tensors, *leaves])
    return pl.pallas_call(
        kernel,
        out_shape=outs,
        grid_spec=pltpu.PrefetchScalarGridSpec(
            num_scalar_prefetch=prefetch,
            grid=grid or (),
            in_specs=in_specs,
            out_specs=out_specs if isinstance(outs, tuple) else out_specs[0],
            scratch_shapes=list(scratch),
        ),
        compiler_params=pltpu.CompilerParams(vmem_limit_bytes=VMEM_GRANT),
        cost_estimate=pl.CostEstimate(flops=flops, bytes_accessed=moved, transcendentals=0),
    )(*args)


def exchange(block):
    return lax.all_to_all(block, "ctx", split_axis=0, concat_axis=0, tiled=True)


def swap_tp(block):
    count = lax.axis_size("tp")
    assert count == 2
    return lax.ppermute(block, "tp", [(0, 1), (1, 0)])


def on_device(
    tables, post_gate, pre_gate, features, filters, token_ids, out_weight, out_grad
):
    n = lax.axis_size("ctx")
    length, channels = post_gate.shape
    columns = out_grad.shape[1]
    width = channels // n
    shape = jax.ShapeDtypeStruct
    one = (n, width, length)
    pair = (n, 2 * width, length)
    both = (n, width, 2 * length)
    twist, dft = tables
    tokens = token_ids.reshape(1, length)
    rank = lax.axis_index("tp").astype(jnp.int32).reshape(1)
    inner_flops = 2 * (n + 1) * (2 * length) ** 2 * width
    spec_shape = (n + 1, width, 2 * length)
    narrow = BF16 if width >= 16 else F32
    chunks = row_chunks(width)
    narrow_scratch = pltpu.VMEM((chunks, n + 1, width // chunks, 2 * length), narrow)

    def by_channels(steps):
        cut, dests = channels // steps, n // steps
        return (
            ((length, cut), lambda i, *_: (0, i)),
            ((cut, length), lambda i, *_: (i, 0)),
            ((dests, *one[1:]), lambda i, *_: (i, 0, 0)),
        )

    other_grad = swap_tp(out_grad)
    steps = 2
    flat, _, _ = by_channels(steps)
    pair_out = call(
        functools.partial(pack_inputs, n // steps),
        pltpu.HBM(pair, BF16),
        (tokens, pre_gate, features, filters),
        grid=(steps,),
        blocks=[None, flat, flat, flat],
        out_blocks=[((n // steps, *pair[1:]), lambda i, *_: (i, 0, 0))],
        from_hbm=range(4),
    )
    pair_in = exchange(pair_out)
    steps = 4
    flat, turned, packed = by_channels(steps)
    weight_block = (channels // steps, columns)
    grad_part = call(
        own_grad,
        pltpu.VMEM((channels, length), F32),
        (rank, out_grad, out_weight),
        grid=(steps,),
        blocks=[None, (weight_block, lambda i, rank: (i, rank[0]))],
        out_blocks=[turned],
        flops=2 * length * channels * columns,
        prefetch=1,
        from_hbm=(1, 2),
    )
    grad_gated, grad_out, away_weight, kept_dft = call(
        functools.partial(pack_grad, n // steps),
        (
            pltpu.HBM((channels, length), F32),
            pltpu.VMEM(one, BF16),
            pltpu.VMEM((channels, columns), BF16),
            pltpu.VMEM(dft.shape, BF16),
        ),
        (rank, other_grad, out_weight, grad_part, post_gate, dft),
        grid=(steps,),
        blocks=[None, (weight_block, lambda i, rank: (i, 1 - rank[0])), turned, flat, None],
        out_blocks=[turned, packed, (weight_block, lambda i, *_: (i, 0)), None],
        flops=2 * length * channels * columns,
        prefetch=1,
        from_hbm=(2, 4, 5),
    )
    both_out, filt_spec = call(
        functools.partial(mix_forward, n),
        (
            shape(both, BF16),
            pltpu.VMEM(spec_shape, narrow),
        ),
        (pair_in, grad_out, twist, kept_dft),
        flops=3 * inner_flops,
        scratch=[
            pltpu.VMEM((chunks, n + 1, 2 * width // chunks, 2 * length), BF16),
            narrow_scratch,
        ],
    )
    both_in = exchange(both_out)
    grad_back_out, gated, away = call(
        functools.partial(mix_backward, n),
        (
            pltpu.HBM(one, BF16),
            pltpu.HBM((length, channels), BF16),
            pltpu.HBM((length, columns), BF16),
        ),
        (both_in, post_gate, twist, kept_dft, filt_spec, away_weight),
        out_blocks=["hbm", "hbm", "hbm"],
        flops=2 * inner_flops + 2 * length * channels * columns,
        scratch=[
            narrow_scratch,
            narrow_scratch,
            pltpu.VMEM(one, BF16),
            pltpu.VMEM((length, channels), BF16),
            pltpu.VMEM((length, columns), BF16),
            pltpu.SemaphoreType.DMA((2 + chunks,)),
        ],
    )
    grad_back_in = exchange(grad_back_out)
    other_part = swap_tp(away)
    parts = 2
    home, grad_post = call(
        functools.partial(project_home, parts),
        (shape((length, columns), F32), shape((length, channels), BF16)),
        (rank, gated, both_in, grad_gated, out_weight),
        grid=(1,),
        blocks=[None, (one, lambda *_: (0, 0, 0)), None, "hbm"],
        flops=2 * length * channels * columns,
        scratch=[pltpu.VMEM((channels, columns), BF16), pltpu.SemaphoreType.DMA((parts,))],
        prefetch=1,
    )
    steps = 2
    flat, _, packed = by_channels(steps)
    half = ((length, columns // steps), lambda i, *_: (0, i))
    grad_pre, grad_features, output = call(
        finish,
        (
            shape((length, channels), BF16),
            shape((length, channels), BF16),
            shape((length, columns), BF16),
        ),
        (tokens, grad_back_in, pre_gate, features, home, other_part),
        grid=(steps,),
        blocks=[None, packed, flat, flat, half, half],
        out_blocks=[flat, flat, half],
    )
    return (output, grad_post, grad_pre, grad_features)


def solution(mesh):
    in_specs = (
        P("ctx", "tp"),
        P("ctx", "tp"),
        P("ctx", "tp"),
        P("ctx", "tp"),
        P("ctx"),
        P("tp", None),
        P("ctx", "tp"),
    )
    out_specs = (P("ctx", "tp"), P("ctx", "tp"), P("ctx", "tp"), P("ctx", "tp"))

    def run(*args):
        n = mesh.shape["ctx"]
        tables = tuple(jnp.asarray(x) for x in dft_tables(n, args[0].shape[0] // n))
        return jax.shard_map(
            functools.partial(on_device, tables),
            mesh=mesh,
            in_specs=in_specs,
            out_specs=out_specs,
            check_vma=False,
        )(*args)

    return run
```

```python
import functools
import math

import jax
import jax.numpy as jnp
import numpy as np
from jax import lax
from jax.experimental import pallas as pl
from jax.experimental.pallas import tpu as pltpu
from jax.sharding import PartitionSpec as P

BASES = 4
LANES = 128
VMEM_GRANT = 24 * 2**20
F32 = jnp.float32
BF16 = jnp.bfloat16


def complex_dft(values, sign):
    length = len(values)
    if length == 1:
        return values
    half = length // 2
    even = [
        (values[b][0] + values[b + half][0], values[b][1] + values[b + half][1])
        for b in range(half)
    ]
    odd = [
        twist(
            (values[b][0] - values[b + half][0], values[b][1] - values[b + half][1]),
            sign * b,
            length,
        )
        for b in range(half)
    ]
    even = complex_dft(even, sign)
    odd = complex_dft(odd, sign)
    return [part for pair in zip(even, odd) for part in pair]


def twist(value, step, length):
    real, imag = value
    step = step % length
    if step == 0:
        return real, imag
    if 4 * step == length:
        return -imag, real
    if 2 * step == length:
        return -real, -imag
    if 4 * step == 3 * length:
        return imag, -real
    cos = math.cos(2.0 * math.pi * step / length)
    sin = math.sin(2.0 * math.pi * step / length)
    if 8 * step % length == 0:
        root = math.sqrt(0.5)
        signed_cos = 1.0 if cos > 0 else -1.0
        signed_sin = 1.0 if sin > 0 else -1.0
        a = real * root
        b = imag * root
        if signed_cos == signed_sin:
            return (a - b, a + b) if signed_cos > 0 else (b - a, -a - b)
        return (a + b, b - a) if signed_cos > 0 else (-a - b, a - b)
    return real * cos - imag * sin, real * sin + imag * cos


def real_dft(values, length):
    if length == 2:
        if len(values) == 1:
            return [(values[0], None), (values[0], None)]
        return [(values[0] + values[1], None), (values[0] - values[1], None)]
    half, quarter = length // 2, length // 4
    if len(values) == length:
        total = [values[b] + values[b + half] for b in range(half)]
        rest = [values[b] - values[b + half] for b in range(half)]
    else:
        total = values
        rest = values
    out = [None] * (half + 1)
    for index, value in enumerate(real_dft(total, half)):
        out[2 * index] = value
    turned = [
        twist((rest[b], -rest[b + quarter]), -b, length) for b in range(quarter)
    ]
    for index, (real, imag) in enumerate(complex_dft(turned, -1)):
        place = 4 * index + 1
        if place <= half:
            out[place] = (real, imag)
        else:
            out[length - place] = (real, -imag)
    return out


def real_dft_transposed(spectrum, length, padded):
    if length == 2:
        first, second = spectrum[0][0], spectrum[1][0]
        return [first + second] if padded else [first + second, first - second]
    half, quarter = length // 2, length // 4
    total = real_dft_transposed(
        [spectrum[2 * index] for index in range(quarter + 1)], half, False
    )
    odd = []
    for index in range(quarter):
        place = 4 * index + 1
        if place <= half:
            odd.append(spectrum[place])
        else:
            real, imag = spectrum[length - place]
            odd.append((real, -imag))
    rest = [None] * half
    for b, value in enumerate(complex_dft(odd, 1)):
        real, imag = twist(value, b, length)
        rest[b] = real
        rest[b + quarter] = -imag
    low = [total[b] + rest[b] for b in range(half)]
    if padded:
        return low
    return low + [total[b] - rest[b] for b in range(half)]


def pack_inputs(dests, token_ref, pre_ref, feat_ref, filt_ref, out_ref):
    width = out_ref.shape[1] // 2
    keep = (token_ref[...] < BASES).astype(BF16)
    mixer = (pre_ref[...].astype(F32) * feat_ref[...].astype(F32)).astype(BF16).T * keep
    filt = filt_ref[...].astype(BF16).T
    for k in range(dests):
        at = slice(k * width, (k + 1) * width)
        out_ref[k] = jnp.concatenate([mixer[at], filt[at]], axis=0)


def own_grad(rank_ref, own_ref, weight_ref, out_ref):
    out_ref[...] = times_transposed(weight_ref[...], own_ref[...])


def times_transposed(left, right):
    return lax.dot_general(left, right, (((1,), (1,)), ((), ())), preferred_element_type=F32)


def pack_grad(
    dests, rank_ref, other_ref, weight_ref, part_ref, post_ref, gated_ref, out_ref, away_ref
):
    width = out_ref.shape[1]
    weight = weight_ref[...]
    away_ref[...] = weight
    grad_gated = part_ref[...] + times_transposed(weight, other_ref[...])
    gated_ref[...] = grad_gated
    mixed = grad_gated * post_ref[...].T.astype(F32)
    for k in range(dests):
        out_ref[k] = mixed[k * width : (k + 1) * width].astype(BF16)


def started(*copies):
    made = [pltpu.make_async_copy(*copy) for copy in copies]
    for copy in made:
        copy.start()
    return made


def forward_blocks(n, blocks, twist_ref, mid_ref, rows):
    length = mid_ref.shape[2] // 2
    for m, (real, imag) in enumerate(real_dft([x.astype(F32) for x in blocks], 2 * n)):
        cos, sin = twist_ref[m : m + 1], twist_ref[n + 1 + m : n + 2 + m]
        if m == 0:
            imag = jnp.zeros_like(real)
        elif imag is None:
            real, imag = real * cos, -(real * sin)
        else:
            real, imag = real * cos + imag * sin, imag * cos - real * sin
        mid_ref[m, rows, :length] = real.astype(mid_ref.dtype)
        mid_ref[m, rows, length:] = imag.astype(mid_ref.dtype)


def inverse_blocks(n, back, twist_ref):
    length = back.shape[1] // 2
    rows = back.shape[0] // (n + 1)
    spectrum = []
    for m in range(n + 1):
        cos, sin = twist_ref[m : m + 1], twist_ref[n + 1 + m : n + 2 + m]
        at = slice(m * rows, (m + 1) * rows)
        real, imag = back[at, :length], back[at, length:]
        if m == 0:
            spectrum.append((0.5 * real, None))
        elif m == n:
            spectrum.append((0.5 * (real * cos - imag * sin), None))
        else:
            spectrum.append((real * cos - imag * sin, real * sin + imag * cos))
    return [x.astype(BF16) for x in real_dft_transposed(spectrum, 2 * n, True)]


def inner_product(values_ref, matrix):
    count, rows, wide = values_ref.shape
    values = values_ref[...].reshape(count * rows, wide).astype(BF16)
    return jnp.dot(values, matrix, preferred_element_type=F32)


def dft_matrices(dft_ref, points):
    length = dft_ref.shape[0]
    cos, sin = dft_ref[:, :length], dft_ref[:, length:]
    forward = jnp.concatenate(
        [jnp.concatenate([cos, -sin], axis=1), jnp.concatenate([sin, cos], axis=1)], axis=0
    )
    cos, sin = cos * (1.0 / points), sin * (1.0 / points)
    back = jnp.concatenate(
        [jnp.concatenate([cos, sin], axis=1), jnp.concatenate([-sin, cos], axis=1)], axis=0
    )
    return forward, back


def row_chunks(rows):
    return max(1, rows // 16)


def mix_forward(
    n,
    pair_ref,
    grad_ref,
    twist_ref,
    dft_ref,
    both_ref,
    filt_ref,
    mid_ref,
    prod_ref,
):
    length = twist_ref.shape[1]
    width = grad_ref.shape[1]
    chunks = row_chunks(width)
    step = width // chunks
    forward, back = dft_matrices(dft_ref, n * length)
    both_ref[:, :, length:] = grad_ref[...]
    for c in range(chunks):
        at = slice(c * step, (c + 1) * step)
        for kind in range(2):
            start = kind * width + c * step
            blocks = [pair_ref[b, start : start + step] for b in range(n)]
            forward_blocks(
                n, blocks, twist_ref, mid_ref.at[c], slice(kind * step, (kind + 1) * step)
            )
        spec = inner_product(mid_ref.at[c], forward)
        for m in range(n + 1):
            first = 2 * m * step
            signal, filt = spec[first : first + step], spec[first + step : first + 2 * step]
            filt_ref[m, at] = filt.astype(filt_ref.dtype)
            real, imag = signal[:, :length], signal[:, length:]
            filt_real, filt_imag = filt[:, :length], filt[:, length:]
            prod_ref[c, m, :, :length] = (real * filt_real - imag * filt_imag).astype(
                prod_ref.dtype
            )
            prod_ref[c, m, :, length:] = (real * filt_imag + imag * filt_real).astype(
                prod_ref.dtype
            )
        mid = inner_product(prod_ref.at[c], back)
        for b, value in enumerate(inverse_blocks(n, mid, twist_ref)):
            both_ref[b, at, :length] = value


def mix_backward(
    n,
    both_ref,
    post_ref,
    twist_ref,
    dft_ref,
    filt_ref,
    weight_ref,
    out_hbm,
    gated_hbm,
    away_hbm,
    mid_ref,
    prod_ref,
    out_ref,
    gated_ref,
    away_ref,
    sems,
):
    length = twist_ref.shape[1]
    width = out_ref.shape[1]
    forward, back = dft_matrices(dft_ref, n * length)
    mixed = channel_rows(both_ref, length).T.astype(F32)
    gated = (post_ref[...].astype(F32) * mixed).astype(BF16)
    gated_ref[...] = gated
    away_ref[...] = jnp.dot(gated, weight_ref[...], preferred_element_type=F32).astype(BF16)
    copies = started((away_ref, away_hbm, sems.at[0]), (gated_ref, gated_hbm, sems.at[1]))
    chunks = row_chunks(width)
    step = width // chunks
    for c in range(chunks):
        at = slice(c * step, (c + 1) * step)
        blocks = [both_ref[b, at, length:] for b in range(n)]
        forward_blocks(n, blocks, twist_ref, mid_ref.at[c], slice(0, step))
        spec = inner_product(mid_ref.at[c], forward)
        for m in range(n + 1):
            signal, filt = spec[m * step : (m + 1) * step], filt_ref[m, at].astype(F32)
            real, imag = signal[:, :length], signal[:, length:]
            filt_real, filt_imag = filt[:, :length], filt[:, length:]
            prod_ref[c, m, :, :length] = (filt_real * real + filt_imag * imag).astype(
                prod_ref.dtype
            )
            prod_ref[c, m, :, length:] = (filt_real * imag - filt_imag * real).astype(
                prod_ref.dtype
            )
        mid = inner_product(prod_ref.at[c], back)
        for b, value in enumerate(inverse_blocks(n, mid, twist_ref)):
            out_ref[b, at] = value
        if chunks == 1:
            copies += started((out_ref, out_hbm, sems.at[2]))
        else:
            rows = pl.ds(c * step, step)
            copies += started((out_ref.at[:, rows], out_hbm.at[:, rows], sems.at[2 + c]))
    for copy in copies:
        copy.wait()


def channel_rows(blocks_ref, length):
    return jnp.concatenate(
        [blocks_ref[k, :, :length] for k in range(blocks_ref.shape[0])], axis=0
    )


def weight_copies(parts, side, weight_hbm, weight_ref, sems):
    channels, columns = weight_ref.shape
    rows = channels // parts
    start = pl.multiple_of(side * columns, LANES)
    return started(
        *(
            (
                weight_hbm.at[pl.ds(k * rows, rows), pl.ds(start, columns)],
                weight_ref.at[pl.ds(k * rows, rows)],
                sems[k],
            )
            for k in range(parts)
        )
    )


def part_products(copies, gated, weight_ref):
    rows = weight_ref.shape[0] // len(copies)
    total = None
    for k, copy in enumerate(copies):
        copy.wait()
        at = slice(k * rows, (k + 1) * rows)
        product = jnp.dot(gated[:, at], weight_ref[at], preferred_element_type=F32)
        total = product if total is None else total + product
    return total


def project_home(
    parts,
    rank_ref,
    gated_ref,
    both_ref,
    grad_ref,
    weight_hbm,
    home_ref,
    post_grad_ref,
    weight_ref,
    sems,
):
    copies = weight_copies(
        parts, rank_ref[0], weight_hbm, weight_ref, [sems.at[k] for k in range(parts)]
    )
    mixed = channel_rows(both_ref, grad_ref.shape[1]).astype(F32)
    post_grad_ref[...] = (grad_ref[...] * mixed).astype(BF16).T
    home_ref[...] = part_products(copies, gated_ref[...], weight_ref)


def finish(
    token_ref,
    packed_ref,
    pre_ref,
    feat_ref,
    home_ref,
    other_ref,
    pre_grad_ref,
    feat_grad_ref,
    out_ref,
):
    keep = (token_ref[...] < BASES).astype(BF16)
    grad = (channel_rows(packed_ref, packed_ref.shape[2]) * keep).T.astype(F32)
    pre_grad_ref[...] = (grad * feat_ref[...].astype(F32)).astype(BF16)
    feat_grad_ref[...] = (grad * pre_ref[...].astype(F32)).astype(BF16)
    out_ref[...] = (home_ref[...] + other_ref[...].astype(F32)).astype(BF16)


def dft_tables(n, length):
    index = np.arange(length)
    angle = index[:, None] * index[None, :] % length * (2.0 * math.pi / length)
    dft = np.concatenate([np.cos(angle), np.sin(angle)], axis=1).astype(jnp.bfloat16)
    angle = np.arange(n + 1)[:, None] * index[None, :] * (math.pi / (n * length))
    twist = np.concatenate([np.cos(angle), np.sin(angle)], axis=0).astype(np.float32)
    return twist, dft


def call(kernel, outs, args, grid=None, blocks=None, out_blocks=None, flops=0, scratch=(), prefetch=0, from_hbm=()):
    leaves = jax.tree.leaves(outs)
    args = [
        pltpu.with_memory_space_constraint(x, pltpu.HBM) if k in from_hbm else x
        for k, x in enumerate(args)
    ]
    tensors = args[prefetch:]

    def spec(array, block):
        if block == "hbm":
            return pl.BlockSpec(memory_space=pltpu.HBM)
        if block is None:
            rank = len(array.shape)
            if grid is None:
                return pl.BlockSpec(memory_space=pltpu.VMEM)
            return pl.BlockSpec(array.shape, lambda *_: (0,) * rank)
        return pl.BlockSpec(*block)

    blocks = blocks or [None] * len(tensors)
    out_blocks = out_blocks or [None] * len(leaves)
    in_specs = [spec(x, b) for x, b in zip(tensors, blocks)]
    out_specs = [spec(x, b) for x, b in zip(leaves, out_blocks)]
    moved = sum(math.prod(x.shape) * np.dtype(x.dtype).itemsize for x in [*tensors, *leaves])
    return pl.pallas_call(
        kernel,
        out_shape=outs,
        grid_spec=pltpu.PrefetchScalarGridSpec(
            num_scalar_prefetch=prefetch,
            grid=grid or (),
            in_specs=in_specs,
            out_specs=out_specs if isinstance(outs, tuple) else out_specs[0],
            scratch_shapes=list(scratch),
        ),
        compiler_params=pltpu.CompilerParams(vmem_limit_bytes=VMEM_GRANT),
        cost_estimate=pl.CostEstimate(flops=flops, bytes_accessed=moved, transcendentals=0),
    )(*args)


def exchange(block):
    return lax.all_to_all(block, "ctx", split_axis=0, concat_axis=0, tiled=True)


def swap_tp(block):
    count = lax.axis_size("tp")
    assert count == 2
    return lax.ppermute(block, "tp", [(0, 1), (1, 0)])


def on_device(
    tables, post_gate, pre_gate, features, filters, token_ids, out_weight, out_grad
):
    n = lax.axis_size("ctx")
    length, channels = post_gate.shape
    columns = out_grad.shape[1]
    width = channels // n
    shape = jax.ShapeDtypeStruct
    one = (n, width, length)
    pair = (n, 2 * width, length)
    both = (n, width, 2 * length)
    twist, dft = tables
    tokens = token_ids.reshape(1, length)
    rank = lax.axis_index("tp").astype(jnp.int32).reshape(1)
    inner_flops = 2 * (n + 1) * (2 * length) ** 2 * width
    spec_shape = (n + 1, width, 2 * length)
    narrow = BF16 if width >= 16 else F32
    chunks = row_chunks(width)
    narrow_scratch = pltpu.VMEM((chunks, n + 1, width // chunks, 2 * length), narrow)

    def by_channels(steps):
        cut, dests = channels // steps, n // steps
        return (
            ((length, cut), lambda i, *_: (0, i)),
            ((cut, length), lambda i, *_: (i, 0)),
            ((dests, *one[1:]), lambda i, *_: (i, 0, 0)),
        )

    other_grad = swap_tp(out_grad)
    steps = 2
    flat, _, _ = by_channels(steps)
    pair_out = call(
        functools.partial(pack_inputs, n // steps),
        pltpu.HBM(pair, BF16),
        (tokens, pre_gate, features, filters),
        grid=(steps,),
        blocks=[None, flat, flat, flat],
        out_blocks=[((n // steps, *pair[1:]), lambda i, *_: (i, 0, 0))],
        from_hbm=range(4),
    )
    pair_in = exchange(pair_out)
    steps = 4
    flat, turned, packed = by_channels(steps)
    weight_block = (channels // steps, columns)
    grad_part = call(
        own_grad,
        pltpu.VMEM((channels, length), F32),
        (rank, out_grad, out_weight),
        grid=(steps,),
        blocks=[None, (weight_block, lambda i, rank: (i, rank[0]))],
        out_blocks=[turned],
        flops=2 * length * channels * columns,
        prefetch=1,
        from_hbm=(1, 2),
    )
    grad_gated, grad_out, away_weight = call(
        functools.partial(pack_grad, n // steps),
        (
            pltpu.HBM((channels, length), F32),
            pltpu.VMEM(one, BF16),
            pltpu.VMEM((channels, columns), BF16),
        ),
        (rank, other_grad, out_weight, grad_part, post_gate),
        grid=(steps,),
        blocks=[None, (weight_block, lambda i, rank: (i, 1 - rank[0])), turned, flat],
        out_blocks=[turned, packed, (weight_block, lambda i, *_: (i, 0))],
        flops=2 * length * channels * columns,
        prefetch=1,
        from_hbm=(2, 4),
    )
    both_out, filt_spec = call(
        functools.partial(mix_forward, n),
        (
            shape(both, BF16),
            pltpu.VMEM(spec_shape, narrow),
        ),
        (pair_in, grad_out, twist, dft),
        flops=3 * inner_flops,
        scratch=[
            pltpu.VMEM((chunks, n + 1, 2 * width // chunks, 2 * length), BF16),
            narrow_scratch,
        ],
    )
    both_in = exchange(both_out)
    grad_back_out, gated, away = call(
        functools.partial(mix_backward, n),
        (
            pltpu.HBM(one, BF16),
            pltpu.HBM((length, channels), BF16),
            pltpu.HBM((length, columns), BF16),
        ),
        (both_in, post_gate, twist, dft, filt_spec, away_weight),
        out_blocks=["hbm", "hbm", "hbm"],
        flops=2 * inner_flops + 2 * length * channels * columns,
        scratch=[
            narrow_scratch,
            narrow_scratch,
            pltpu.VMEM(one, BF16),
            pltpu.VMEM((length, channels), BF16),
            pltpu.VMEM((length, columns), BF16),
            pltpu.SemaphoreType.DMA((2 + chunks,)),
        ],
    )
    grad_back_in = exchange(grad_back_out)
    other_part = swap_tp(away)
    parts = 2
    home, grad_post = call(
        functools.partial(project_home, parts),
        (shape((length, columns), F32), shape((length, channels), BF16)),
        (rank, gated, both_in, grad_gated, out_weight),
        grid=(1,),
        blocks=[None, (one, lambda *_: (0, 0, 0)), None, "hbm"],
        flops=2 * length * channels * columns,
        scratch=[pltpu.VMEM((channels, columns), BF16), pltpu.SemaphoreType.DMA((parts,))],
        prefetch=1,
    )
    steps = 2
    flat, _, packed = by_channels(steps)
    half = ((length, columns // steps), lambda i, *_: (0, i))
    grad_pre, grad_features, output = call(
        finish,
        (
            shape((length, channels), BF16),
            shape((length, channels), BF16),
            shape((length, columns), BF16),
        ),
        (tokens, grad_back_in, pre_gate, features, home, other_part),
        grid=(steps,),
        blocks=[None, packed, flat, flat, half, half],
        out_blocks=[flat, flat, half],
    )
    return (output, grad_post, grad_pre, grad_features)


def solution(mesh):
    in_specs = (
        P("ctx", "tp"),
        P("ctx", "tp"),
        P("ctx", "tp"),
        P("ctx", "tp"),
        P("ctx"),
        P("tp", None),
        P("ctx", "tp"),
    )
    out_specs = (P("ctx", "tp"), P("ctx", "tp"), P("ctx", "tp"), P("ctx", "tp"))

    def run(*args):
        n = mesh.shape["ctx"]
        tables = tuple(jnp.asarray(x) for x in dft_tables(n, args[0].shape[0] // n))
        return jax.shard_map(
            functools.partial(on_device, tables),
            mesh=mesh,
            in_specs=in_specs,
            out_specs=out_specs,
            check_vma=False,
        )(*args)

    return run
```

```python
import functools
import math

import jax
import jax.numpy as jnp
import numpy as np
from jax import lax
from jax.experimental import pallas as pl
from jax.experimental.pallas import tpu as pltpu
from jax.sharding import PartitionSpec as P

BASES = 4
LANES = 128
VMEM_GRANT = 24 * 2**20
F32 = jnp.float32
BF16 = jnp.bfloat16


def complex_dft(values, sign):
    length = len(values)
    if length == 1:
        return values
    half = length // 2
    even = [
        (values[b][0] + values[b + half][0], values[b][1] + values[b + half][1])
        for b in range(half)
    ]
    odd = [
        twist(
            (values[b][0] - values[b + half][0], values[b][1] - values[b + half][1]),
            sign * b,
            length,
        )
        for b in range(half)
    ]
    even = complex_dft(even, sign)
    odd = complex_dft(odd, sign)
    return [part for pair in zip(even, odd) for part in pair]


def twist(value, step, length):
    real, imag = value
    step = step % length
    if step == 0:
        return real, imag
    if 4 * step == length:
        return -imag, real
    if 2 * step == length:
        return -real, -imag
    if 4 * step == 3 * length:
        return imag, -real
    cos = math.cos(2.0 * math.pi * step / length)
    sin = math.sin(2.0 * math.pi * step / length)
    if 8 * step % length == 0:
        root = math.sqrt(0.5)
        signed_cos = 1.0 if cos > 0 else -1.0
        signed_sin = 1.0 if sin > 0 else -1.0
        a = real * root
        b = imag * root
        if signed_cos == signed_sin:
            return (a - b, a + b) if signed_cos > 0 else (b - a, -a - b)
        return (a + b, b - a) if signed_cos > 0 else (-a - b, a - b)
    return real * cos - imag * sin, real * sin + imag * cos


def real_dft(values, length):
    if length == 2:
        if len(values) == 1:
            return [(values[0], None), (values[0], None)]
        return [(values[0] + values[1], None), (values[0] - values[1], None)]
    half, quarter = length // 2, length // 4
    if len(values) == length:
        total = [values[b] + values[b + half] for b in range(half)]
        rest = [values[b] - values[b + half] for b in range(half)]
    else:
        total = values
        rest = values
    out = [None] * (half + 1)
    for index, value in enumerate(real_dft(total, half)):
        out[2 * index] = value
    turned = [
        twist((rest[b], -rest[b + quarter]), -b, length) for b in range(quarter)
    ]
    for index, (real, imag) in enumerate(complex_dft(turned, -1)):
        place = 4 * index + 1
        if place <= half:
            out[place] = (real, imag)
        else:
            out[length - place] = (real, -imag)
    return out


def real_dft_transposed(spectrum, length, padded):
    if length == 2:
        first, second = spectrum[0][0], spectrum[1][0]
        return [first + second] if padded else [first + second, first - second]
    half, quarter = length // 2, length // 4
    total = real_dft_transposed(
        [spectrum[2 * index] for index in range(quarter + 1)], half, False
    )
    odd = []
    for index in range(quarter):
        place = 4 * index + 1
        if place <= half:
            odd.append(spectrum[place])
        else:
            real, imag = spectrum[length - place]
            odd.append((real, -imag))
    rest = [None] * half
    for b, value in enumerate(complex_dft(odd, 1)):
        real, imag = twist(value, b, length)
        rest[b] = real
        rest[b + quarter] = -imag
    low = [total[b] + rest[b] for b in range(half)]
    if padded:
        return low
    return low + [total[b] - rest[b] for b in range(half)]


def pack_inputs(
    parts,
    token_hbm,
    pre_hbm,
    feat_hbm,
    filt_hbm,
    out_hbm,
    token_ref,
    pre_ref,
    feat_ref,
    filt_ref,
    out_ref,
    in_sems,
    out_sems,
):
    n, rows, _ = out_ref.shape
    width, dests = rows // 2, n // parts
    cut = dests * width
    pairs = ((pre_hbm, pre_ref), (feat_hbm, feat_ref), (filt_hbm, filt_ref))
    copies = []
    for k in range(parts):
        at = pl.ds(k * cut, cut)
        copies.append(
            started(
                *((a.at[:, at], b.at[:, at], in_sems.at[k, i]) for i, (a, b) in enumerate(pairs))
            )
        )
        if k == 0:
            copies[0] += started((token_hbm, token_ref, in_sems.at[k, 3]))
    sent = []
    for k in range(parts):
        for copy in copies[k]:
            copy.wait()
        at = slice(k * cut, (k + 1) * cut)
        keep = (token_ref[...] < BASES).astype(BF16)
        mixer = (pre_ref[:, at].astype(F32) * feat_ref[:, at].astype(F32)).astype(BF16).T * keep
        filt = filt_ref[:, at].astype(BF16).T
        for j in range(dests):
            mine = slice(j * width, (j + 1) * width)
            out_ref[k * dests + j] = jnp.concatenate([mixer[mine], filt[mine]], axis=0)
        here = pl.ds(k * dests, dests)
        sent += started((out_ref.at[here], out_hbm.at[here], out_sems.at[k]))
    for copy in sent:
        copy.wait()


def own_grad(rank_ref, own_ref, weight_ref, out_ref):
    out_ref[...] = times_transposed(weight_ref[...], own_ref[...])


def times_transposed(left, right):
    return lax.dot_general(left, right, (((1,), (1,)), ((), ())), preferred_element_type=F32)


def pack_grad(
    dests, rank_ref, other_ref, weight_ref, part_ref, post_ref, gated_ref, out_ref, away_ref
):
    width = out_ref.shape[1]
    weight = weight_ref[...]
    away_ref[...] = weight
    grad_gated = part_ref[...] + times_transposed(weight, other_ref[...])
    gated_ref[...] = grad_gated
    mixed = grad_gated * post_ref[...].T.astype(F32)
    for k in range(dests):
        out_ref[k] = mixed[k * width : (k + 1) * width].astype(BF16)


def started(*copies):
    made = [pltpu.make_async_copy(*copy) for copy in copies]
    for copy in made:
        copy.start()
    return made


def forward_blocks(n, blocks, twist_ref, mid_ref, rows):
    length = mid_ref.shape[2] // 2
    for m, (real, imag) in enumerate(real_dft([x.astype(F32) for x in blocks], 2 * n)):
        cos, sin = twist_ref[m : m + 1], twist_ref[n + 1 + m : n + 2 + m]
        if m == 0:
            imag = jnp.zeros_like(real)
        elif imag is None:
            real, imag = real * cos, -(real * sin)
        else:
            real, imag = real * cos + imag * sin, imag * cos - real * sin
        mid_ref[m, rows, :length] = real.astype(mid_ref.dtype)
        mid_ref[m, rows, length:] = imag.astype(mid_ref.dtype)


def inverse_blocks(n, back, twist_ref):
    length = back.shape[1] // 2
    rows = back.shape[0] // (n + 1)
    spectrum = []
    for m in range(n + 1):
        cos, sin = twist_ref[m : m + 1], twist_ref[n + 1 + m : n + 2 + m]
        at = slice(m * rows, (m + 1) * rows)
        real, imag = back[at, :length], back[at, length:]
        if m == 0:
            spectrum.append((0.5 * real, None))
        elif m == n:
            spectrum.append((0.5 * (real * cos - imag * sin), None))
        else:
            spectrum.append((real * cos - imag * sin, real * sin + imag * cos))
    return [x.astype(BF16) for x in real_dft_transposed(spectrum, 2 * n, True)]


def inner_product(values_ref, matrix):
    count, rows, wide = values_ref.shape
    values = values_ref[...].reshape(count * rows, wide).astype(BF16)
    return jnp.dot(values, matrix, preferred_element_type=F32)


def dft_matrices(dft_ref, points):
    length = dft_ref.shape[0]
    cos, sin = dft_ref[:, :length], dft_ref[:, length:]
    forward = jnp.concatenate(
        [jnp.concatenate([cos, -sin], axis=1), jnp.concatenate([sin, cos], axis=1)], axis=0
    )
    cos, sin = cos * (1.0 / points), sin * (1.0 / points)
    back = jnp.concatenate(
        [jnp.concatenate([cos, sin], axis=1), jnp.concatenate([-sin, cos], axis=1)], axis=0
    )
    return forward, back


def row_chunks(rows):
    return max(1, rows // 16)


def mix_forward(
    n,
    pair_ref,
    grad_ref,
    twist_ref,
    dft_ref,
    both_ref,
    filt_ref,
    mid_ref,
    prod_ref,
):
    length = twist_ref.shape[1]
    width = grad_ref.shape[1]
    chunks = row_chunks(width)
    step = width // chunks
    forward, back = dft_matrices(dft_ref, n * length)
    both_ref[:, :, length:] = grad_ref[...]
    for c in range(chunks):
        at = slice(c * step, (c + 1) * step)
        for kind in range(2):
            start = kind * width + c * step
            blocks = [pair_ref[b, start : start + step] for b in range(n)]
            forward_blocks(
                n, blocks, twist_ref, mid_ref.at[c], slice(kind * step, (kind + 1) * step)
            )
        spec = inner_product(mid_ref.at[c], forward)
        for m in range(n + 1):
            first = 2 * m * step
            signal, filt = spec[first : first + step], spec[first + step : first + 2 * step]
            filt_ref[m, at] = filt.astype(filt_ref.dtype)
            real, imag = signal[:, :length], signal[:, length:]
            filt_real, filt_imag = filt[:, :length], filt[:, length:]
            prod_ref[c, m, :, :length] = (real * filt_real - imag * filt_imag).astype(
                prod_ref.dtype
            )
            prod_ref[c, m, :, length:] = (real * filt_imag + imag * filt_real).astype(
                prod_ref.dtype
            )
        mid = inner_product(prod_ref.at[c], back)
        for b, value in enumerate(inverse_blocks(n, mid, twist_ref)):
            both_ref[b, at, :length] = value


def mix_backward(
    n,
    both_ref,
    post_ref,
    twist_ref,
    dft_ref,
    filt_ref,
    weight_ref,
    out_hbm,
    gated_hbm,
    away_hbm,
    mid_ref,
    prod_ref,
    out_ref,
    gated_ref,
    away_ref,
    sems,
):
    length = twist_ref.shape[1]
    width = out_ref.shape[1]
    forward, back = dft_matrices(dft_ref, n * length)
    mixed = channel_rows(both_ref, length).T.astype(F32)
    gated = (post_ref[...].astype(F32) * mixed).astype(BF16)
    gated_ref[...] = gated
    copies = started((gated_ref, gated_hbm, sems.at[0]))
    chunks = row_chunks(width)
    step = width // chunks
    cut = weight_ref.shape[1] // chunks
    for c in range(chunks):
        share = slice(c * cut, (c + 1) * cut)
        away_ref[:, share] = jnp.dot(
            gated, weight_ref[:, share], preferred_element_type=F32
        ).astype(BF16)
        share = pl.ds(c * cut, cut)
        copies += started((away_ref.at[:, share], away_hbm.at[:, share], sems.at[1 + c]))
        at = slice(c * step, (c + 1) * step)
        blocks = [both_ref[b, at, length:] for b in range(n)]
        forward_blocks(n, blocks, twist_ref, mid_ref.at[c], slice(0, step))
        spec = inner_product(mid_ref.at[c], forward)
        for m in range(n + 1):
            signal, filt = spec[m * step : (m + 1) * step], filt_ref[m, at].astype(F32)
            real, imag = signal[:, :length], signal[:, length:]
            filt_real, filt_imag = filt[:, :length], filt[:, length:]
            prod_ref[c, m, :, :length] = (filt_real * real + filt_imag * imag).astype(
                prod_ref.dtype
            )
            prod_ref[c, m, :, length:] = (filt_real * imag - filt_imag * real).astype(
                prod_ref.dtype
            )
        mid = inner_product(prod_ref.at[c], back)
        for b, value in enumerate(inverse_blocks(n, mid, twist_ref)):
            out_ref[b, at] = value
        if chunks == 1:
            copies += started((out_ref, out_hbm, sems.at[1 + chunks]))
        else:
            rows = pl.ds(c * step, step)
            copies += started(
                (out_ref.at[:, rows], out_hbm.at[:, rows], sems.at[1 + chunks + c])
            )
    for copy in copies:
        copy.wait()


def channel_rows(blocks_ref, length):
    return jnp.concatenate(
        [blocks_ref[k, :, :length] for k in range(blocks_ref.shape[0])], axis=0
    )


def weight_copies(parts, side, weight_hbm, weight_ref, sems):
    channels, columns = weight_ref.shape
    rows = channels // parts
    start = pl.multiple_of(side * columns, LANES)
    return started(
        *(
            (
                weight_hbm.at[pl.ds(k * rows, rows), pl.ds(start, columns)],
                weight_ref.at[pl.ds(k * rows, rows)],
                sems[k],
            )
            for k in range(parts)
        )
    )


def part_products(copies, gated, weight_ref):
    rows = weight_ref.shape[0] // len(copies)
    total = None
    for k, copy in enumerate(copies):
        copy.wait()
        at = slice(k * rows, (k + 1) * rows)
        product = jnp.dot(gated[:, at], weight_ref[at], preferred_element_type=F32)
        total = product if total is None else total + product
    return total


def project_home(
    parts,
    rank_ref,
    gated_ref,
    both_ref,
    grad_ref,
    weight_hbm,
    home_ref,
    post_grad_ref,
    weight_ref,
    sems,
):
    copies = weight_copies(
        parts, rank_ref[0], weight_hbm, weight_ref, [sems.at[k] for k in range(parts)]
    )
    mixed = channel_rows(both_ref, grad_ref.shape[1]).astype(F32)
    post_grad_ref[...] = (grad_ref[...] * mixed).astype(BF16).T
    home_ref[...] = part_products(copies, gated_ref[...], weight_ref)


def finish(
    token_ref,
    packed_ref,
    pre_ref,
    feat_ref,
    home_ref,
    other_ref,
    pre_grad_ref,
    feat_grad_ref,
    out_ref,
):
    keep = (token_ref[...] < BASES).astype(BF16)
    grad = (channel_rows(packed_ref, packed_ref.shape[2]) * keep).T.astype(F32)
    pre_grad_ref[...] = (grad * feat_ref[...].astype(F32)).astype(BF16)
    feat_grad_ref[...] = (grad * pre_ref[...].astype(F32)).astype(BF16)
    out_ref[...] = (home_ref[...] + other_ref[...].astype(F32)).astype(BF16)


def dft_tables(n, length):
    index = np.arange(length)
    angle = index[:, None] * index[None, :] % length * (2.0 * math.pi / length)
    dft = np.concatenate([np.cos(angle), np.sin(angle)], axis=1).astype(jnp.bfloat16)
    angle = np.arange(n + 1)[:, None] * index[None, :] * (math.pi / (n * length))
    twist = np.concatenate([np.cos(angle), np.sin(angle)], axis=0).astype(np.float32)
    return twist, dft


def call(kernel, outs, args, grid=None, blocks=None, out_blocks=None, flops=0, scratch=(), prefetch=0, from_hbm=()):
    leaves = jax.tree.leaves(outs)
    args = [
        pltpu.with_memory_space_constraint(x, pltpu.HBM) if k in from_hbm else x
        for k, x in enumerate(args)
    ]
    tensors = args[prefetch:]

    def spec(array, block):
        if block == "hbm":
            return pl.BlockSpec(memory_space=pltpu.HBM)
        if block is None:
            rank = len(array.shape)
            if grid is None:
                return pl.BlockSpec(memory_space=pltpu.VMEM)
            return pl.BlockSpec(array.shape, lambda *_: (0,) * rank)
        return pl.BlockSpec(*block)

    blocks = blocks or [None] * len(tensors)
    out_blocks = out_blocks or [None] * len(leaves)
    in_specs = [spec(x, b) for x, b in zip(tensors, blocks)]
    out_specs = [spec(x, b) for x, b in zip(leaves, out_blocks)]
    moved = sum(math.prod(x.shape) * np.dtype(x.dtype).itemsize for x in [*tensors, *leaves])
    return pl.pallas_call(
        kernel,
        out_shape=outs,
        grid_spec=pltpu.PrefetchScalarGridSpec(
            num_scalar_prefetch=prefetch,
            grid=grid or (),
            in_specs=in_specs,
            out_specs=out_specs if isinstance(outs, tuple) else out_specs[0],
            scratch_shapes=list(scratch),
        ),
        compiler_params=pltpu.CompilerParams(vmem_limit_bytes=VMEM_GRANT),
        cost_estimate=pl.CostEstimate(flops=flops, bytes_accessed=moved, transcendentals=0),
    )(*args)


def exchange(block):
    return lax.all_to_all(block, "ctx", split_axis=0, concat_axis=0, tiled=True)


def swap_tp(block):
    count = lax.axis_size("tp")
    assert count == 2
    return lax.ppermute(block, "tp", [(0, 1), (1, 0)])


def on_device(
    tables, post_gate, pre_gate, features, filters, token_ids, out_weight, out_grad
):
    n = lax.axis_size("ctx")
    length, channels = post_gate.shape
    columns = out_grad.shape[1]
    width = channels // n
    shape = jax.ShapeDtypeStruct
    one = (n, width, length)
    pair = (n, 2 * width, length)
    both = (n, width, 2 * length)
    twist, dft = tables
    tokens = token_ids.reshape(1, length)
    rank = lax.axis_index("tp").astype(jnp.int32).reshape(1)
    inner_flops = 2 * (n + 1) * (2 * length) ** 2 * width
    spec_shape = (n + 1, width, 2 * length)
    narrow = BF16 if width >= 16 else F32
    chunks = row_chunks(width)
    narrow_scratch = pltpu.VMEM((chunks, n + 1, width // chunks, 2 * length), narrow)

    def by_channels(steps):
        cut, dests = channels // steps, n // steps
        return (
            ((length, cut), lambda i, *_: (0, i)),
            ((cut, length), lambda i, *_: (i, 0)),
            ((dests, *one[1:]), lambda i, *_: (i, 0, 0)),
        )

    other_grad = swap_tp(out_grad)
    parts = 2
    pair_out = call(
        functools.partial(pack_inputs, parts),
        pltpu.HBM(pair, BF16),
        (tokens, pre_gate, features, filters),
        blocks=["hbm"] * 4,
        out_blocks=["hbm"],
        from_hbm=range(4),
        scratch=[
            pltpu.VMEM(tokens.shape, jnp.int32),
            pltpu.VMEM((length, channels), BF16),
            pltpu.VMEM((length, channels), BF16),
            pltpu.VMEM((length, channels), F32),
            pltpu.VMEM(pair, BF16),
            pltpu.SemaphoreType.DMA((parts, 4)),
            pltpu.SemaphoreType.DMA((parts,)),
        ],
    )
    pair_in = exchange(pair_out)
    steps = 4
    flat, turned, packed = by_channels(steps)
    weight_block = (channels // steps, columns)
    grad_part = call(
        own_grad,
        pltpu.VMEM((channels, length), F32),
        (rank, out_grad, out_weight),
        grid=(steps,),
        blocks=[None, (weight_block, lambda i, rank: (i, rank[0]))],
        out_blocks=[turned],
        flops=2 * length * channels * columns,
        prefetch=1,
        from_hbm=(1, 2),
    )
    grad_gated, grad_out, away_weight = call(
        functools.partial(pack_grad, n // steps),
        (
            pltpu.HBM((channels, length), F32),
            pltpu.VMEM(one, BF16),
            pltpu.VMEM((channels, columns), BF16),
        ),
        (rank, other_grad, out_weight, grad_part, post_gate),
        grid=(steps,),
        blocks=[None, (weight_block, lambda i, rank: (i, 1 - rank[0])), turned, flat],
        out_blocks=[turned, packed, (weight_block, lambda i, *_: (i, 0))],
        flops=2 * length * channels * columns,
        prefetch=1,
        from_hbm=(2, 4),
    )
    both_out, filt_spec = call(
        functools.partial(mix_forward, n),
        (
            shape(both, BF16),
            pltpu.VMEM(spec_shape, narrow),
        ),
        (pair_in, grad_out, twist, dft),
        flops=3 * inner_flops,
        scratch=[
            pltpu.VMEM((chunks, n + 1, 2 * width // chunks, 2 * length), BF16),
            narrow_scratch,
        ],
    )
    both_in = exchange(both_out)
    grad_back_out, gated, away = call(
        functools.partial(mix_backward, n),
        (
            pltpu.HBM(one, BF16),
            pltpu.HBM((length, channels), BF16),
            pltpu.HBM((length, columns), BF16),
        ),
        (both_in, post_gate, twist, dft, filt_spec, away_weight),
        out_blocks=["hbm", "hbm", "hbm"],
        flops=2 * inner_flops + 2 * length * channels * columns,
        scratch=[
            narrow_scratch,
            narrow_scratch,
            pltpu.VMEM(one, BF16),
            pltpu.VMEM((length, channels), BF16),
            pltpu.VMEM((length, columns), BF16),
            pltpu.SemaphoreType.DMA((1 + 2 * chunks,)),
        ],
    )
    grad_back_in = exchange(grad_back_out)
    other_part = swap_tp(away)
    parts = 2
    home, grad_post = call(
        functools.partial(project_home, parts),
        (shape((length, columns), F32), shape((length, channels), BF16)),
        (rank, gated, both_in, grad_gated, out_weight),
        grid=(1,),
        blocks=[None, (one, lambda *_: (0, 0, 0)), None, "hbm"],
        flops=2 * length * channels * columns,
        scratch=[pltpu.VMEM((channels, columns), BF16), pltpu.SemaphoreType.DMA((parts,))],
        prefetch=1,
    )
    steps = 2
    flat, _, packed = by_channels(steps)
    half = ((length, columns // steps), lambda i, *_: (0, i))
    grad_pre, grad_features, output = call(
        finish,
        (
            shape((length, channels), BF16),
            shape((length, channels), BF16),
            shape((length, columns), BF16),
        ),
        (tokens, grad_back_in, pre_gate, features, home, other_part),
        grid=(steps,),
        blocks=[None, packed, flat, flat, half, half],
        out_blocks=[flat, flat, half],
    )
    return (output, grad_post, grad_pre, grad_features)


def solution(mesh):
    in_specs = (
        P("ctx", "tp"),
        P("ctx", "tp"),
        P("ctx", "tp"),
        P("ctx", "tp"),
        P("ctx"),
        P("tp", None),
        P("ctx", "tp"),
    )
    out_specs = (P("ctx", "tp"), P("ctx", "tp"), P("ctx", "tp"), P("ctx", "tp"))

    def run(*args):
        n = mesh.shape["ctx"]
        tables = tuple(jnp.asarray(x) for x in dft_tables(n, args[0].shape[0] // n))
        return jax.shard_map(
            functools.partial(on_device, tables),
            mesh=mesh,
            in_specs=in_specs,
            out_specs=out_specs,
            check_vma=False,
        )(*args)

    return run
```

```python
import functools
import math

import jax
import jax.numpy as jnp
import numpy as np
from jax import lax
from jax.experimental import pallas as pl
from jax.experimental.pallas import tpu as pltpu
from jax.sharding import PartitionSpec as P

BASES = 4
LANES = 128
VMEM_GRANT = 24 * 2**20
F32 = jnp.float32
BF16 = jnp.bfloat16


def complex_dft(values, sign):
    length = len(values)
    if length == 1:
        return values
    half = length // 2
    even = [
        (values[b][0] + values[b + half][0], values[b][1] + values[b + half][1])
        for b in range(half)
    ]
    odd = [
        twist(
            (values[b][0] - values[b + half][0], values[b][1] - values[b + half][1]),
            sign * b,
            length,
        )
        for b in range(half)
    ]
    even = complex_dft(even, sign)
    odd = complex_dft(odd, sign)
    return [part for pair in zip(even, odd) for part in pair]


def twist(value, step, length):
    real, imag = value
    step = step % length
    if step == 0:
        return real, imag
    if 4 * step == length:
        return -imag, real
    if 2 * step == length:
        return -real, -imag
    if 4 * step == 3 * length:
        return imag, -real
    cos = math.cos(2.0 * math.pi * step / length)
    sin = math.sin(2.0 * math.pi * step / length)
    if 8 * step % length == 0:
        root = math.sqrt(0.5)
        signed_cos = 1.0 if cos > 0 else -1.0
        signed_sin = 1.0 if sin > 0 else -1.0
        a = real * root
        b = imag * root
        if signed_cos == signed_sin:
            return (a - b, a + b) if signed_cos > 0 else (b - a, -a - b)
        return (a + b, b - a) if signed_cos > 0 else (-a - b, a - b)
    return real * cos - imag * sin, real * sin + imag * cos


def real_dft(values, length):
    if length == 2:
        if len(values) == 1:
            return [(values[0], None), (values[0], None)]
        return [(values[0] + values[1], None), (values[0] - values[1], None)]
    half, quarter = length // 2, length // 4
    if len(values) == length:
        total = [values[b] + values[b + half] for b in range(half)]
        rest = [values[b] - values[b + half] for b in range(half)]
    else:
        total = values
        rest = values
    out = [None] * (half + 1)
    for index, value in enumerate(real_dft(total, half)):
        out[2 * index] = value
    turned = [
        twist((rest[b], -rest[b + quarter]), -b, length) for b in range(quarter)
    ]
    for index, (real, imag) in enumerate(complex_dft(turned, -1)):
        place = 4 * index + 1
        if place <= half:
            out[place] = (real, imag)
        else:
            out[length - place] = (real, -imag)
    return out


def real_dft_transposed(spectrum, length, padded):
    if length == 2:
        first, second = spectrum[0][0], spectrum[1][0]
        return [first + second] if padded else [first + second, first - second]
    half, quarter = length // 2, length // 4
    total = real_dft_transposed(
        [spectrum[2 * index] for index in range(quarter + 1)], half, False
    )
    odd = []
    for index in range(quarter):
        place = 4 * index + 1
        if place <= half:
            odd.append(spectrum[place])
        else:
            real, imag = spectrum[length - place]
            odd.append((real, -imag))
    rest = [None] * half
    for b, value in enumerate(complex_dft(odd, 1)):
        real, imag = twist(value, b, length)
        rest[b] = real
        rest[b + quarter] = -imag
    low = [total[b] + rest[b] for b in range(half)]
    if padded:
        return low
    return low + [total[b] - rest[b] for b in range(half)]


def pack_inputs(dests, token_ref, pre_ref, feat_ref, filt_ref, out_ref):
    width = out_ref.shape[1] // 2
    keep = (token_ref[...] < BASES).astype(BF16)
    mixer = (pre_ref[...].astype(F32) * feat_ref[...].astype(F32)).astype(BF16).T * keep
    filt = filt_ref[...].astype(BF16).T
    for k in range(dests):
        at = slice(k * width, (k + 1) * width)
        out_ref[k] = jnp.concatenate([mixer[at], filt[at]], axis=0)


def own_grad(rank_ref, own_ref, weight_ref, out_ref):
    out_ref[...] = times_transposed(weight_ref[...], own_ref[...])


def times_transposed(left, right):
    return lax.dot_general(left, right, (((1,), (1,)), ((), ())), preferred_element_type=F32)


def pack_grad(
    dests, rank_ref, other_ref, weight_ref, part_ref, post_ref, gated_ref, out_ref, away_ref
):
    width = out_ref.shape[1]
    weight = weight_ref[...]
    away_ref[...] = weight
    grad_gated = part_ref[...] + times_transposed(weight, other_ref[...])
    gated_ref[...] = grad_gated
    mixed = grad_gated * post_ref[...].T.astype(F32)
    for k in range(dests):
        out_ref[k] = mixed[k * width : (k + 1) * width].astype(BF16)


def started(*copies):
    made = [pltpu.make_async_copy(*copy) for copy in copies]
    for copy in made:
        copy.start()
    return made


def forward_blocks(n, blocks, twist_ref, mid_ref, rows):
    length = mid_ref.shape[2] // 2
    for m, (real, imag) in enumerate(real_dft([x.astype(F32) for x in blocks], 2 * n)):
        cos, sin = twist_ref[m : m + 1], twist_ref[n + 1 + m : n + 2 + m]
        if m == 0:
            imag = jnp.zeros_like(real)
        elif imag is None:
            real, imag = real * cos, -(real * sin)
        else:
            real, imag = real * cos + imag * sin, imag * cos - real * sin
        mid_ref[m, rows, :length] = real.astype(mid_ref.dtype)
        mid_ref[m, rows, length:] = imag.astype(mid_ref.dtype)


def inverse_blocks(n, back, twist_ref):
    length = back.shape[1] // 2
    rows = back.shape[0] // (n + 1)
    spectrum = []
    for m in range(n + 1):
        cos, sin = twist_ref[m : m + 1], twist_ref[n + 1 + m : n + 2 + m]
        at = slice(m * rows, (m + 1) * rows)
        real, imag = back[at, :length], back[at, length:]
        if m == 0:
            spectrum.append((0.5 * real, None))
        elif m == n:
            spectrum.append((0.5 * (real * cos - imag * sin), None))
        else:
            spectrum.append((real * cos - imag * sin, real * sin + imag * cos))
    return [x.astype(BF16) for x in real_dft_transposed(spectrum, 2 * n, True)]


def inner_product(values_ref, matrix):
    count, rows, wide = values_ref.shape
    values = values_ref[...].reshape(count * rows, wide).astype(BF16)
    return jnp.dot(values, matrix, preferred_element_type=F32)


def dft_matrices(dft_ref, points):
    length = dft_ref.shape[0]
    cos, sin = dft_ref[:, :length], dft_ref[:, length:]
    forward = jnp.concatenate(
        [jnp.concatenate([cos, -sin], axis=1), jnp.concatenate([sin, cos], axis=1)], axis=0
    )
    cos, sin = cos * (1.0 / points), sin * (1.0 / points)
    back = jnp.concatenate(
        [jnp.concatenate([cos, sin], axis=1), jnp.concatenate([-sin, cos], axis=1)], axis=0
    )
    return forward, back


def row_chunks(rows):
    return max(1, rows // 16)


def mix_forward(
    n,
    pair_ref,
    grad_ref,
    twist_ref,
    dft_ref,
    both_ref,
    filt_ref,
    mid_ref,
    prod_ref,
):
    length = twist_ref.shape[1]
    width = grad_ref.shape[1]
    chunks = row_chunks(width)
    step = width // chunks
    forward, back = dft_matrices(dft_ref, n * length)
    both_ref[:, :, length:] = grad_ref[...]

    def transform(c):
        for kind in range(2):
            start = kind * width + c * step
            blocks = [pair_ref[b, start : start + step] for b in range(n)]
            forward_blocks(
                n, blocks, twist_ref, mid_ref.at[c], slice(kind * step, (kind + 1) * step)
            )

    transform(0)
    for c in range(chunks):
        at = slice(c * step, (c + 1) * step)
        if c + 1 < chunks:
            transform(c + 1)
        spec = inner_product(mid_ref.at[c], forward)
        for m in range(n + 1):
            first = 2 * m * step
            signal, filt = spec[first : first + step], spec[first + step : first + 2 * step]
            filt_ref[m, at] = filt.astype(filt_ref.dtype)
            real, imag = signal[:, :length], signal[:, length:]
            filt_real, filt_imag = filt[:, :length], filt[:, length:]
            prod_ref[c, m, :, :length] = (real * filt_real - imag * filt_imag).astype(
                prod_ref.dtype
            )
            prod_ref[c, m, :, length:] = (real * filt_imag + imag * filt_real).astype(
                prod_ref.dtype
            )
        mid = inner_product(prod_ref.at[c], back)
        for b, value in enumerate(inverse_blocks(n, mid, twist_ref)):
            both_ref[b, at, :length] = value


def mix_backward(
    n,
    both_ref,
    post_ref,
    twist_ref,
    dft_ref,
    filt_ref,
    weight_ref,
    out_hbm,
    gated_hbm,
    away_hbm,
    mid_ref,
    prod_ref,
    out_ref,
    gated_ref,
    away_ref,
    sems,
):
    length = twist_ref.shape[1]
    width = out_ref.shape[1]
    forward, back = dft_matrices(dft_ref, n * length)
    mixed = channel_rows(both_ref, length).T.astype(F32)
    gated = (post_ref[...].astype(F32) * mixed).astype(BF16)
    gated_ref[...] = gated
    away_ref[...] = jnp.dot(gated, weight_ref[...], preferred_element_type=F32).astype(BF16)
    copies = started((away_ref, away_hbm, sems.at[0]), (gated_ref, gated_hbm, sems.at[1]))
    chunks = row_chunks(width)
    step = width // chunks

    def transform(c):
        blocks = [both_ref[b, c * step : (c + 1) * step, length:] for b in range(n)]
        forward_blocks(n, blocks, twist_ref, mid_ref.at[c], slice(0, step))

    transform(0)
    for c in range(chunks):
        at = slice(c * step, (c + 1) * step)
        if c + 1 < chunks:
            transform(c + 1)
        spec = inner_product(mid_ref.at[c], forward)
        for m in range(n + 1):
            signal, filt = spec[m * step : (m + 1) * step], filt_ref[m, at].astype(F32)
            real, imag = signal[:, :length], signal[:, length:]
            filt_real, filt_imag = filt[:, :length], filt[:, length:]
            prod_ref[c, m, :, :length] = (filt_real * real + filt_imag * imag).astype(
                prod_ref.dtype
            )
            prod_ref[c, m, :, length:] = (filt_real * imag - filt_imag * real).astype(
                prod_ref.dtype
            )
        mid = inner_product(prod_ref.at[c], back)
        for b, value in enumerate(inverse_blocks(n, mid, twist_ref)):
            out_ref[b, at] = value
        if chunks == 1:
            copies += started((out_ref, out_hbm, sems.at[2]))
        else:
            rows = pl.ds(c * step, step)
            copies += started((out_ref.at[:, rows], out_hbm.at[:, rows], sems.at[2 + c]))
    for copy in copies:
        copy.wait()


def channel_rows(blocks_ref, length):
    return jnp.concatenate(
        [blocks_ref[k, :, :length] for k in range(blocks_ref.shape[0])], axis=0
    )


def weight_copies(parts, side, weight_hbm, weight_ref, sems):
    channels, columns = weight_ref.shape
    rows = channels // parts
    start = pl.multiple_of(side * columns, LANES)
    return started(
        *(
            (
                weight_hbm.at[pl.ds(k * rows, rows), pl.ds(start, columns)],
                weight_ref.at[pl.ds(k * rows, rows)],
                sems[k],
            )
            for k in range(parts)
        )
    )


def part_products(copies, gated, weight_ref):
    rows = weight_ref.shape[0] // len(copies)
    total = None
    for k, copy in enumerate(copies):
        copy.wait()
        at = slice(k * rows, (k + 1) * rows)
        product = jnp.dot(gated[:, at], weight_ref[at], preferred_element_type=F32)
        total = product if total is None else total + product
    return total


def project_home(
    parts,
    rank_ref,
    gated_ref,
    both_ref,
    grad_ref,
    weight_hbm,
    home_ref,
    post_grad_ref,
    weight_ref,
    sems,
):
    copies = weight_copies(
        parts, rank_ref[0], weight_hbm, weight_ref, [sems.at[k] for k in range(parts)]
    )
    mixed = channel_rows(both_ref, grad_ref.shape[1]).astype(F32)
    post_grad_ref[...] = (grad_ref[...] * mixed).astype(BF16).T
    home_ref[...] = part_products(copies, gated_ref[...], weight_ref)


def finish(
    parts,
    token_ref,
    packed_ref,
    pre_ref,
    feat_ref,
    home_ref,
    other_ref,
    pre_grad_hbm,
    feat_grad_hbm,
    out_hbm,
    pre_grad_ref,
    feat_grad_ref,
    out_ref,
    sems,
):
    out_ref[...] = (home_ref[...] + other_ref[...].astype(F32)).astype(BF16)
    copies = started((out_ref, out_hbm, sems.at[2, 0]))
    keep = (token_ref[...] < BASES).astype(BF16)
    dests = packed_ref.shape[0] // parts
    cut = pre_ref.shape[1] // parts
    for k in range(parts):
        at = pl.ds(k * cut, cut)
        blocks = packed_ref.at[pl.ds(k * dests, dests)]
        grad = (channel_rows(blocks, blocks.shape[2]) * keep).T.astype(F32)
        pre_grad_ref[:, at] = (grad * feat_ref[:, at].astype(F32)).astype(BF16)
        feat_grad_ref[:, at] = (grad * pre_ref[:, at].astype(F32)).astype(BF16)
        copies += started(
            (pre_grad_ref.at[:, at], pre_grad_hbm.at[:, at], sems.at[0, k]),
            (feat_grad_ref.at[:, at], feat_grad_hbm.at[:, at], sems.at[1, k]),
        )
    for copy in copies:
        copy.wait()


def dft_tables(n, length):
    index = np.arange(length)
    angle = index[:, None] * index[None, :] % length * (2.0 * math.pi / length)
    dft = np.concatenate([np.cos(angle), np.sin(angle)], axis=1).astype(jnp.bfloat16)
    angle = np.arange(n + 1)[:, None] * index[None, :] * (math.pi / (n * length))
    twist = np.concatenate([np.cos(angle), np.sin(angle)], axis=0).astype(np.float32)
    return twist, dft


def call(kernel, outs, args, grid=None, blocks=None, out_blocks=None, flops=0, scratch=(), prefetch=0, from_hbm=()):
    leaves = jax.tree.leaves(outs)
    args = [
        pltpu.with_memory_space_constraint(x, pltpu.HBM) if k in from_hbm else x
        for k, x in enumerate(args)
    ]
    tensors = args[prefetch:]

    def spec(array, block):
        if block == "hbm":
            return pl.BlockSpec(memory_space=pltpu.HBM)
        if block is None:
            rank = len(array.shape)
            if grid is None:
                return pl.BlockSpec(memory_space=pltpu.VMEM)
            return pl.BlockSpec(array.shape, lambda *_: (0,) * rank)
        return pl.BlockSpec(*block)

    blocks = blocks or [None] * len(tensors)
    out_blocks = out_blocks or [None] * len(leaves)
    in_specs = [spec(x, b) for x, b in zip(tensors, blocks)]
    out_specs = [spec(x, b) for x, b in zip(leaves, out_blocks)]
    moved = sum(math.prod(x.shape) * np.dtype(x.dtype).itemsize for x in [*tensors, *leaves])
    return pl.pallas_call(
        kernel,
        out_shape=outs,
        grid_spec=pltpu.PrefetchScalarGridSpec(
            num_scalar_prefetch=prefetch,
            grid=grid or (),
            in_specs=in_specs,
            out_specs=out_specs if isinstance(outs, tuple) else out_specs[0],
            scratch_shapes=list(scratch),
        ),
        compiler_params=pltpu.CompilerParams(vmem_limit_bytes=VMEM_GRANT),
        cost_estimate=pl.CostEstimate(flops=flops, bytes_accessed=moved, transcendentals=0),
    )(*args)


def exchange(block):
    return lax.all_to_all(block, "ctx", split_axis=0, concat_axis=0, tiled=True)


def swap_tp(block):
    count = lax.axis_size("tp")
    assert count == 2
    return lax.ppermute(block, "tp", [(0, 1), (1, 0)])


def on_device(
    tables, post_gate, pre_gate, features, filters, token_ids, out_weight, out_grad
):
    n = lax.axis_size("ctx")
    length, channels = post_gate.shape
    columns = out_grad.shape[1]
    width = channels // n
    shape = jax.ShapeDtypeStruct
    one = (n, width, length)
    pair = (n, 2 * width, length)
    both = (n, width, 2 * length)
    twist, dft = tables
    tokens = token_ids.reshape(1, length)
    rank = lax.axis_index("tp").astype(jnp.int32).reshape(1)
    inner_flops = 2 * (n + 1) * (2 * length) ** 2 * width
    spec_shape = (n + 1, width, 2 * length)
    narrow = BF16 if width >= 16 else F32
    chunks = row_chunks(width)
    narrow_scratch = pltpu.VMEM((chunks, n + 1, width // chunks, 2 * length), narrow)

    def by_channels(steps):
        cut, dests = channels // steps, n // steps
        return (
            ((length, cut), lambda i, *_: (0, i)),
            ((cut, length), lambda i, *_: (i, 0)),
            ((dests, *one[1:]), lambda i, *_: (i, 0, 0)),
        )

    other_grad = swap_tp(out_grad)
    steps = 2
    flat, _, _ = by_channels(steps)
    pair_out = call(
        functools.partial(pack_inputs, n // steps),
        pltpu.HBM(pair, BF16),
        (tokens, pre_gate, features, filters),
        grid=(steps,),
        blocks=[None, flat, flat, flat],
        out_blocks=[((n // steps, *pair[1:]), lambda i, *_: (i, 0, 0))],
        from_hbm=range(4),
    )
    pair_in = exchange(pair_out)
    steps = 4
    flat, turned, packed = by_channels(steps)
    weight_block = (channels // steps, columns)
    grad_part = call(
        own_grad,
        pltpu.VMEM((channels, length), F32),
        (rank, out_grad, out_weight),
        grid=(steps,),
        blocks=[None, (weight_block, lambda i, rank: (i, rank[0]))],
        out_blocks=[turned],
        flops=2 * length * channels * columns,
        prefetch=1,
        from_hbm=(1, 2),
    )
    grad_gated, grad_out, away_weight = call(
        functools.partial(pack_grad, n // steps),
        (
            pltpu.HBM((channels, length), F32),
            pltpu.VMEM(one, BF16),
            pltpu.VMEM((channels, columns), BF16),
        ),
        (rank, other_grad, out_weight, grad_part, post_gate),
        grid=(steps,),
        blocks=[None, (weight_block, lambda i, rank: (i, 1 - rank[0])), turned, flat],
        out_blocks=[turned, packed, (weight_block, lambda i, *_: (i, 0))],
        flops=2 * length * channels * columns,
        prefetch=1,
        from_hbm=(2, 4),
    )
    both_out, filt_spec = call(
        functools.partial(mix_forward, n),
        (
            shape(both, BF16),
            pltpu.VMEM(spec_shape, narrow),
        ),
        (pair_in, grad_out, twist, dft),
        flops=3 * inner_flops,
        scratch=[
            pltpu.VMEM((chunks, n + 1, 2 * width // chunks, 2 * length), BF16),
            narrow_scratch,
        ],
    )
    both_in = exchange(both_out)
    grad_back_out, gated, away = call(
        functools.partial(mix_backward, n),
        (
            pltpu.HBM(one, BF16),
            pltpu.HBM((length, channels), BF16),
            pltpu.HBM((length, columns), BF16),
        ),
        (both_in, post_gate, twist, dft, filt_spec, away_weight),
        out_blocks=["hbm", "hbm", "hbm"],
        flops=2 * inner_flops + 2 * length * channels * columns,
        scratch=[
            narrow_scratch,
            narrow_scratch,
            pltpu.VMEM(one, BF16),
            pltpu.VMEM((length, channels), BF16),
            pltpu.VMEM((length, columns), BF16),
            pltpu.SemaphoreType.DMA((2 + chunks,)),
        ],
    )
    grad_back_in = exchange(grad_back_out)
    other_part = swap_tp(away)
    parts = 2
    home, grad_post = call(
        functools.partial(project_home, parts),
        (shape((length, columns), F32), shape((length, channels), BF16)),
        (rank, gated, both_in, grad_gated, out_weight),
        grid=(1,),
        blocks=[None, (one, lambda *_: (0, 0, 0)), None, "hbm"],
        flops=2 * length * channels * columns,
        scratch=[pltpu.VMEM((channels, columns), BF16), pltpu.SemaphoreType.DMA((parts,))],
        prefetch=1,
    )
    flat = (length, channels)
    grad_pre, grad_features, output = call(
        functools.partial(finish, parts),
        (pltpu.HBM(flat, BF16), pltpu.HBM(flat, BF16), pltpu.HBM((length, columns), BF16)),
        (tokens, grad_back_in, pre_gate, features, home, other_part),
        out_blocks=["hbm"] * 3,
        scratch=[
            pltpu.VMEM(flat, BF16),
            pltpu.VMEM(flat, BF16),
            pltpu.VMEM((length, columns), BF16),
            pltpu.SemaphoreType.DMA((3, parts)),
        ],
    )
    return (output, grad_post, grad_pre, grad_features)


def solution(mesh):
    in_specs = (
        P("ctx", "tp"),
        P("ctx", "tp"),
        P("ctx", "tp"),
        P("ctx", "tp"),
        P("ctx"),
        P("tp", None),
        P("ctx", "tp"),
    )
    out_specs = (P("ctx", "tp"), P("ctx", "tp"), P("ctx", "tp"), P("ctx", "tp"))

    def run(*args):
        n = mesh.shape["ctx"]
        tables = tuple(jnp.asarray(x) for x in dft_tables(n, args[0].shape[0] // n))
        return jax.shard_map(
            functools.partial(on_device, tables),
            mesh=mesh,
            in_specs=in_specs,
            out_specs=out_specs,
            check_vma=False,
        )(*args)

    return run
```

```python
import functools
import math

import jax
import jax.numpy as jnp
import numpy as np
from jax import lax
from jax.experimental import pallas as pl
from jax.experimental.pallas import tpu as pltpu
from jax.sharding import PartitionSpec as P

BASES = 4
LANES = 128
VMEM_GRANT = 24 * 2**20
F32 = jnp.float32
BF16 = jnp.bfloat16


def complex_dft(values, sign):
    length = len(values)
    if length == 1:
        return values
    half = length // 2
    even = [
        (values[b][0] + values[b + half][0], values[b][1] + values[b + half][1])
        for b in range(half)
    ]
    odd = [
        twist(
            (values[b][0] - values[b + half][0], values[b][1] - values[b + half][1]),
            sign * b,
            length,
        )
        for b in range(half)
    ]
    even = complex_dft(even, sign)
    odd = complex_dft(odd, sign)
    return [part for pair in zip(even, odd) for part in pair]


def twist(value, step, length):
    real, imag = value
    step = step % length
    if step == 0:
        return real, imag
    if 4 * step == length:
        return -imag, real
    if 2 * step == length:
        return -real, -imag
    if 4 * step == 3 * length:
        return imag, -real
    cos = math.cos(2.0 * math.pi * step / length)
    sin = math.sin(2.0 * math.pi * step / length)
    if 8 * step % length == 0:
        root = math.sqrt(0.5)
        signed_cos = 1.0 if cos > 0 else -1.0
        signed_sin = 1.0 if sin > 0 else -1.0
        a = real * root
        b = imag * root
        if signed_cos == signed_sin:
            return (a - b, a + b) if signed_cos > 0 else (b - a, -a - b)
        return (a + b, b - a) if signed_cos > 0 else (-a - b, a - b)
    return real * cos - imag * sin, real * sin + imag * cos


def real_dft(values, length):
    if length == 2:
        if len(values) == 1:
            return [(values[0], None), (values[0], None)]
        return [(values[0] + values[1], None), (values[0] - values[1], None)]
    half, quarter = length // 2, length // 4
    if len(values) == length:
        total = [values[b] + values[b + half] for b in range(half)]
        rest = [values[b] - values[b + half] for b in range(half)]
    else:
        total = values
        rest = values
    out = [None] * (half + 1)
    for index, value in enumerate(real_dft(total, half)):
        out[2 * index] = value
    turned = [
        twist((rest[b], -rest[b + quarter]), -b, length) for b in range(quarter)
    ]
    for index, (real, imag) in enumerate(complex_dft(turned, -1)):
        place = 4 * index + 1
        if place <= half:
            out[place] = (real, imag)
        else:
            out[length - place] = (real, -imag)
    return out


def real_dft_transposed(spectrum, length, padded):
    if length == 2:
        first, second = spectrum[0][0], spectrum[1][0]
        return [first + second] if padded else [first + second, first - second]
    half, quarter = length // 2, length // 4
    total = real_dft_transposed(
        [spectrum[2 * index] for index in range(quarter + 1)], half, False
    )
    odd = []
    for index in range(quarter):
        place = 4 * index + 1
        if place <= half:
            odd.append(spectrum[place])
        else:
            real, imag = spectrum[length - place]
            odd.append((real, -imag))
    rest = [None] * half
    for b, value in enumerate(complex_dft(odd, 1)):
        real, imag = twist(value, b, length)
        rest[b] = real
        rest[b + quarter] = -imag
    low = [total[b] + rest[b] for b in range(half)]
    if padded:
        return low
    return low + [total[b] - rest[b] for b in range(half)]


def pack_inputs(dests, token_ref, pre_ref, feat_ref, filt_ref, out_ref):
    width = out_ref.shape[1] // 2
    keep = (token_ref[...] < BASES).astype(BF16)
    mixer = (pre_ref[...].astype(F32) * feat_ref[...].astype(F32)).astype(BF16).T * keep
    filt = filt_ref[...].astype(BF16).T
    for k in range(dests):
        at = slice(k * width, (k + 1) * width)
        out_ref[k] = jnp.concatenate([mixer[at], filt[at]], axis=0)


def own_grad(rank_ref, own_ref, weight_ref, out_ref):
    out_ref[...] = times_transposed(weight_ref[...], own_ref[...])


def times_transposed(left, right):
    return lax.dot_general(left, right, (((1,), (1,)), ((), ())), preferred_element_type=F32)


def pack_grad(
    dests, rank_ref, other_ref, weight_ref, part_ref, post_ref, gated_ref, out_ref, away_ref
):
    width = out_ref.shape[1]
    weight = weight_ref[...]
    away_ref[...] = weight
    grad_gated = part_ref[...] + times_transposed(weight, other_ref[...])
    gated_ref[...] = grad_gated
    mixed = grad_gated * post_ref[...].T.astype(F32)
    for k in range(dests):
        out_ref[k] = mixed[k * width : (k + 1) * width].astype(BF16)


def group_order(n):
    return list(range(n - 1, -1, -1))


def started(*copies):
    made = [pltpu.make_async_copy(*copy) for copy in copies]
    for copy in made:
        copy.start()
    return made


def forward_blocks(n, blocks, twist_ref, mid_ref, rows):
    length = mid_ref.shape[2] // 2
    for m, (real, imag) in enumerate(real_dft([x.astype(F32) for x in blocks], 2 * n)):
        cos, sin = twist_ref[m : m + 1], twist_ref[n + 1 + m : n + 2 + m]
        if m == 0:
            imag = jnp.zeros_like(real)
        elif imag is None:
            real, imag = real * cos, -(real * sin)
        else:
            real, imag = real * cos + imag * sin, imag * cos - real * sin
        mid_ref[m, rows, :length] = real.astype(mid_ref.dtype)
        mid_ref[m, rows, length:] = imag.astype(mid_ref.dtype)


def inverse_blocks(n, back, twist_ref):
    length = back.shape[1] // 2
    rows = back.shape[0] // (n + 1)
    spectrum = []
    for m in range(n + 1):
        cos, sin = twist_ref[m : m + 1], twist_ref[n + 1 + m : n + 2 + m]
        at = slice(m * rows, (m + 1) * rows)
        real, imag = back[at, :length], back[at, length:]
        if m == 0:
            spectrum.append((0.5 * real, None))
        elif m == n:
            spectrum.append((0.5 * (real * cos - imag * sin), None))
        else:
            spectrum.append((real * cos - imag * sin, real * sin + imag * cos))
    return [x.astype(BF16) for x in real_dft_transposed(spectrum, 2 * n, True)]


def inner_product(values_ref, matrix):
    count, rows, wide = values_ref.shape
    values = values_ref[...].reshape(count * rows, wide).astype(BF16)
    return jnp.dot(values, matrix, preferred_element_type=F32)


def dft_matrices(dft_ref, points):
    length = dft_ref.shape[0]
    cos, sin = dft_ref[:, :length], dft_ref[:, length:]
    forward = jnp.concatenate(
        [jnp.concatenate([cos, -sin], axis=1), jnp.concatenate([sin, cos], axis=1)], axis=0
    )
    cos, sin = cos * (1.0 / points), sin * (1.0 / points)
    back = jnp.concatenate(
        [jnp.concatenate([cos, sin], axis=1), jnp.concatenate([-sin, cos], axis=1)], axis=0
    )
    return forward, back


def row_chunks(rows):
    return max(1, rows // 16)


def mix_forward(
    n,
    pair_ref,
    grad_ref,
    twist_ref,
    dft_ref,
    both_ref,
    filt_ref,
    mid_ref,
    prod_ref,
):
    length = twist_ref.shape[1]
    width = grad_ref.shape[1]
    chunks = row_chunks(width)
    step = width // chunks
    forward, back = dft_matrices(dft_ref, n * length)
    both_ref[:, :, length:] = grad_ref[...]

    def transform(c):
        for kind in range(2):
            start = kind * width + c * step
            blocks = [pair_ref[b, start : start + step] for b in group_order(n)]
            forward_blocks(
                n, blocks, twist_ref, mid_ref.at[c], slice(kind * step, (kind + 1) * step)
            )

    transform(0)
    for c in range(chunks):
        at = slice(c * step, (c + 1) * step)
        if c + 1 < chunks:
            transform(c + 1)
        spec = inner_product(mid_ref.at[c], forward)
        for m in range(n + 1):
            first = 2 * m * step
            signal, filt = spec[first : first + step], spec[first + step : first + 2 * step]
            filt_ref[m, at] = filt.astype(filt_ref.dtype)
            real, imag = signal[:, :length], signal[:, length:]
            filt_real, filt_imag = filt[:, :length], filt[:, length:]
            prod_ref[c, m, :, :length] = (real * filt_real - imag * filt_imag).astype(
                prod_ref.dtype
            )
            prod_ref[c, m, :, length:] = (real * filt_imag + imag * filt_real).astype(
                prod_ref.dtype
            )
        mid = inner_product(prod_ref.at[c], back)
        for b, value in zip(group_order(n), inverse_blocks(n, mid, twist_ref)):
            both_ref[b, at, :length] = value


def mix_backward(
    n,
    both_ref,
    post_ref,
    twist_ref,
    dft_ref,
    filt_ref,
    weight_ref,
    out_hbm,
    gated_hbm,
    away_hbm,
    mid_ref,
    prod_ref,
    out_ref,
    gated_ref,
    away_ref,
    sems,
):
    length = twist_ref.shape[1]
    width = out_ref.shape[1]
    forward, back = dft_matrices(dft_ref, n * length)
    mixed = channel_rows(both_ref, length).T.astype(F32)
    gated = (post_ref[...].astype(F32) * mixed).astype(BF16)
    gated_ref[...] = gated
    away_ref[...] = jnp.dot(gated, weight_ref[...], preferred_element_type=F32).astype(BF16)
    copies = started((away_ref, away_hbm, sems.at[0]), (gated_ref, gated_hbm, sems.at[1]))
    chunks = row_chunks(width)
    step = width // chunks

    def transform(c):
        blocks = [both_ref[b, c * step : (c + 1) * step, length:] for b in group_order(n)]
        forward_blocks(n, blocks, twist_ref, mid_ref.at[c], slice(0, step))

    transform(0)
    for c in range(chunks):
        at = slice(c * step, (c + 1) * step)
        if c + 1 < chunks:
            transform(c + 1)
        spec = inner_product(mid_ref.at[c], forward)
        for m in range(n + 1):
            signal, filt = spec[m * step : (m + 1) * step], filt_ref[m, at].astype(F32)
            real, imag = signal[:, :length], signal[:, length:]
            filt_real, filt_imag = filt[:, :length], filt[:, length:]
            prod_ref[c, m, :, :length] = (filt_real * real + filt_imag * imag).astype(
                prod_ref.dtype
            )
            prod_ref[c, m, :, length:] = (filt_real * imag - filt_imag * real).astype(
                prod_ref.dtype
            )
        mid = inner_product(prod_ref.at[c], back)
        for b, value in zip(group_order(n), inverse_blocks(n, mid, twist_ref)):
            out_ref[b, at] = value
        if chunks == 1:
            copies += started((out_ref, out_hbm, sems.at[2]))
        else:
            rows = pl.ds(c * step, step)
            copies += started((out_ref.at[:, rows], out_hbm.at[:, rows], sems.at[2 + c]))
    for copy in copies:
        copy.wait()


def channel_rows(blocks_ref, length):
    return jnp.concatenate(
        [blocks_ref[k, :, :length] for k in range(blocks_ref.shape[0])], axis=0
    )


def weight_copies(parts, side, weight_hbm, weight_ref, sems):
    channels, columns = weight_ref.shape
    rows = channels // parts
    start = pl.multiple_of(side * columns, LANES)
    return started(
        *(
            (
                weight_hbm.at[pl.ds(k * rows, rows), pl.ds(start, columns)],
                weight_ref.at[pl.ds(k * rows, rows)],
                sems[k],
            )
            for k in range(parts)
        )
    )


def part_products(copies, gated, weight_ref):
    rows = weight_ref.shape[0] // len(copies)
    total = None
    for k, copy in enumerate(copies):
        copy.wait()
        at = slice(k * rows, (k + 1) * rows)
        product = jnp.dot(gated[:, at], weight_ref[at], preferred_element_type=F32)
        total = product if total is None else total + product
    return total


def project_home(
    parts,
    rank_ref,
    gated_ref,
    both_ref,
    grad_ref,
    weight_hbm,
    home_ref,
    post_grad_ref,
    weight_ref,
    sems,
):
    copies = weight_copies(
        parts, rank_ref[0], weight_hbm, weight_ref, [sems.at[k] for k in range(parts)]
    )
    mixed = channel_rows(both_ref, grad_ref.shape[1]).astype(F32)
    post_grad_ref[...] = (grad_ref[...] * mixed).astype(BF16).T
    home_ref[...] = part_products(copies, gated_ref[...], weight_ref)


def finish(
    parts,
    token_ref,
    packed_ref,
    pre_ref,
    feat_ref,
    home_ref,
    other_ref,
    pre_grad_hbm,
    feat_grad_hbm,
    out_hbm,
    pre_grad_ref,
    feat_grad_ref,
    out_ref,
    sems,
):
    out_ref[...] = (home_ref[...] + other_ref[...].astype(F32)).astype(BF16)
    copies = started((out_ref, out_hbm, sems.at[2, 0]))
    keep = (token_ref[...] < BASES).astype(BF16)
    dests = packed_ref.shape[0] // parts
    cut = pre_ref.shape[1] // parts
    for k in range(parts):
        at = pl.ds(k * cut, cut)
        blocks = packed_ref.at[pl.ds(k * dests, dests)]
        grad = (channel_rows(blocks, blocks.shape[2]) * keep).T.astype(F32)
        pre_grad_ref[:, at] = (grad * feat_ref[:, at].astype(F32)).astype(BF16)
        feat_grad_ref[:, at] = (grad * pre_ref[:, at].astype(F32)).astype(BF16)
        copies += started(
            (pre_grad_ref.at[:, at], pre_grad_hbm.at[:, at], sems.at[0, k]),
            (feat_grad_ref.at[:, at], feat_grad_hbm.at[:, at], sems.at[1, k]),
        )
    for copy in copies:
        copy.wait()


def dft_tables(n, length):
    index = np.arange(length)
    angle = index[:, None] * index[None, :] % length * (2.0 * math.pi / length)
    dft = np.concatenate([np.cos(angle), np.sin(angle)], axis=1).astype(jnp.bfloat16)
    angle = np.arange(n + 1)[:, None] * index[None, :] * (math.pi / (n * length))
    twist = np.concatenate([np.cos(angle), np.sin(angle)], axis=0).astype(np.float32)
    return twist, dft


def call(kernel, outs, args, grid=None, blocks=None, out_blocks=None, flops=0, scratch=(), prefetch=0, from_hbm=()):
    leaves = jax.tree.leaves(outs)
    args = [
        pltpu.with_memory_space_constraint(x, pltpu.HBM) if k in from_hbm else x
        for k, x in enumerate(args)
    ]
    tensors = args[prefetch:]

    def spec(array, block):
        if block == "hbm":
            return pl.BlockSpec(memory_space=pltpu.HBM)
        if block is None:
            rank = len(array.shape)
            if grid is None:
                return pl.BlockSpec(memory_space=pltpu.VMEM)
            return pl.BlockSpec(array.shape, lambda *_: (0,) * rank)
        return pl.BlockSpec(*block)

    blocks = blocks or [None] * len(tensors)
    out_blocks = out_blocks or [None] * len(leaves)
    in_specs = [spec(x, b) for x, b in zip(tensors, blocks)]
    out_specs = [spec(x, b) for x, b in zip(leaves, out_blocks)]
    moved = sum(math.prod(x.shape) * np.dtype(x.dtype).itemsize for x in [*tensors, *leaves])
    return pl.pallas_call(
        kernel,
        out_shape=outs,
        grid_spec=pltpu.PrefetchScalarGridSpec(
            num_scalar_prefetch=prefetch,
            grid=grid or (),
            in_specs=in_specs,
            out_specs=out_specs if isinstance(outs, tuple) else out_specs[0],
            scratch_shapes=list(scratch),
        ),
        compiler_params=pltpu.CompilerParams(vmem_limit_bytes=VMEM_GRANT),
        cost_estimate=pl.CostEstimate(flops=flops, bytes_accessed=moved, transcendentals=0),
    )(*args)


def exchange(block):
    return lax.all_to_all(
        block,
        "ctx",
        split_axis=0,
        concat_axis=0,
        tiled=True,
        axis_index_groups=[group_order(block.shape[0])],
    )


def swap_tp(block):
    count = lax.axis_size("tp")
    assert count == 2
    return lax.ppermute(block, "tp", [(0, 1), (1, 0)])


def on_device(
    tables, post_gate, pre_gate, features, filters, token_ids, out_weight, out_grad
):
    n = lax.axis_size("ctx")
    length, channels = post_gate.shape
    columns = out_grad.shape[1]
    width = channels // n
    shape = jax.ShapeDtypeStruct
    one = (n, width, length)
    pair = (n, 2 * width, length)
    both = (n, width, 2 * length)
    twist, dft = tables
    tokens = token_ids.reshape(1, length)
    rank = lax.axis_index("tp").astype(jnp.int32).reshape(1)
    inner_flops = 2 * (n + 1) * (2 * length) ** 2 * width
    spec_shape = (n + 1, width, 2 * length)
    narrow = BF16 if width >= 16 else F32
    chunks = row_chunks(width)
    narrow_scratch = pltpu.VMEM((chunks, n + 1, width // chunks, 2 * length), narrow)

    def by_channels(steps):
        cut, dests = channels // steps, n // steps
        return (
            ((length, cut), lambda i, *_: (0, i)),
            ((cut, length), lambda i, *_: (i, 0)),
            ((dests, *one[1:]), lambda i, *_: (i, 0, 0)),
        )

    other_grad = swap_tp(out_grad)
    steps = 2
    flat, _, _ = by_channels(steps)
    pair_out = call(
        functools.partial(pack_inputs, n // steps),
        pltpu.HBM(pair, BF16),
        (tokens, pre_gate, features, filters),
        grid=(steps,),
        blocks=[None, flat, flat, flat],
        out_blocks=[((n // steps, *pair[1:]), lambda i, *_: (i, 0, 0))],
        from_hbm=range(4),
    )
    pair_in = exchange(pair_out)
    steps = 4
    flat, turned, packed = by_channels(steps)
    weight_block = (channels // steps, columns)
    grad_part = call(
        own_grad,
        pltpu.VMEM((channels, length), F32),
        (rank, out_grad, out_weight),
        grid=(steps,),
        blocks=[None, (weight_block, lambda i, rank: (i, rank[0]))],
        out_blocks=[turned],
        flops=2 * length * channels * columns,
        prefetch=1,
        from_hbm=(1, 2),
    )
    grad_gated, grad_out, away_weight = call(
        functools.partial(pack_grad, n // steps),
        (
            pltpu.HBM((channels, length), F32),
            pltpu.VMEM(one, BF16),
            pltpu.VMEM((channels, columns), BF16),
        ),
        (rank, other_grad, out_weight, grad_part, post_gate),
        grid=(steps,),
        blocks=[None, (weight_block, lambda i, rank: (i, 1 - rank[0])), turned, flat],
        out_blocks=[turned, packed, (weight_block, lambda i, *_: (i, 0))],
        flops=2 * length * channels * columns,
        prefetch=1,
        from_hbm=(2, 4),
    )
    both_out, filt_spec = call(
        functools.partial(mix_forward, n),
        (
            shape(both, BF16),
            pltpu.VMEM(spec_shape, narrow),
        ),
        (pair_in, grad_out, twist, dft),
        flops=3 * inner_flops,
        scratch=[
            pltpu.VMEM((chunks, n + 1, 2 * width // chunks, 2 * length), BF16),
            narrow_scratch,
        ],
    )
    both_in = exchange(both_out)
    grad_back_out, gated, away = call(
        functools.partial(mix_backward, n),
        (
            pltpu.HBM(one, BF16),
            pltpu.HBM((length, channels), BF16),
            pltpu.HBM((length, columns), BF16),
        ),
        (both_in, post_gate, twist, dft, filt_spec, away_weight),
        out_blocks=["hbm", "hbm", "hbm"],
        flops=2 * inner_flops + 2 * length * channels * columns,
        scratch=[
            narrow_scratch,
            narrow_scratch,
            pltpu.VMEM(one, BF16),
            pltpu.VMEM((length, channels), BF16),
            pltpu.VMEM((length, columns), BF16),
            pltpu.SemaphoreType.DMA((2 + chunks,)),
        ],
    )
    grad_back_in = exchange(grad_back_out)
    other_part = swap_tp(away)
    parts = 2
    home, grad_post = call(
        functools.partial(project_home, parts),
        (shape((length, columns), F32), shape((length, channels), BF16)),
        (rank, gated, both_in, grad_gated, out_weight),
        grid=(1,),
        blocks=[None, (one, lambda *_: (0, 0, 0)), None, "hbm"],
        flops=2 * length * channels * columns,
        scratch=[pltpu.VMEM((channels, columns), BF16), pltpu.SemaphoreType.DMA((parts,))],
        prefetch=1,
    )
    flat = (length, channels)
    grad_pre, grad_features, output = call(
        functools.partial(finish, parts),
        (pltpu.HBM(flat, BF16), pltpu.HBM(flat, BF16), pltpu.HBM((length, columns), BF16)),
        (tokens, grad_back_in, pre_gate, features, home, other_part),
        out_blocks=["hbm"] * 3,
        scratch=[
            pltpu.VMEM(flat, BF16),
            pltpu.VMEM(flat, BF16),
            pltpu.VMEM((length, columns), BF16),
            pltpu.SemaphoreType.DMA((3, parts)),
        ],
    )
    return (output, grad_post, grad_pre, grad_features)


def solution(mesh):
    in_specs = (
        P("ctx", "tp"),
        P("ctx", "tp"),
        P("ctx", "tp"),
        P("ctx", "tp"),
        P("ctx"),
        P("tp", None),
        P("ctx", "tp"),
    )
    out_specs = (P("ctx", "tp"), P("ctx", "tp"), P("ctx", "tp"), P("ctx", "tp"))

    def run(*args):
        n = mesh.shape["ctx"]
        tables = tuple(jnp.asarray(x) for x in dft_tables(n, args[0].shape[0] // n))
        return jax.shard_map(
            functools.partial(on_device, tables),
            mesh=mesh,
            in_specs=in_specs,
            out_specs=out_specs,
            check_vma=False,
        )(*args)

    return run
```

```python
import functools
import math

import jax
import jax.numpy as jnp
import numpy as np
from jax import lax
from jax.experimental import pallas as pl
from jax.experimental.pallas import tpu as pltpu
from jax.sharding import PartitionSpec as P

BASES = 4
LANES = 128
VMEM_GRANT = 24 * 2**20
F32 = jnp.float32
BF16 = jnp.bfloat16


def complex_dft(values, sign):
    length = len(values)
    if length == 1:
        return values
    half = length // 2
    even = [
        (values[b][0] + values[b + half][0], values[b][1] + values[b + half][1])
        for b in range(half)
    ]
    odd = [
        twist(
            (values[b][0] - values[b + half][0], values[b][1] - values[b + half][1]),
            sign * b,
            length,
        )
        for b in range(half)
    ]
    even = complex_dft(even, sign)
    odd = complex_dft(odd, sign)
    return [part for pair in zip(even, odd) for part in pair]


def twist(value, step, length):
    real, imag = value
    step = step % length
    if step == 0:
        return real, imag
    if 4 * step == length:
        return -imag, real
    if 2 * step == length:
        return -real, -imag
    if 4 * step == 3 * length:
        return imag, -real
    cos = math.cos(2.0 * math.pi * step / length)
    sin = math.sin(2.0 * math.pi * step / length)
    if 8 * step % length == 0:
        root = math.sqrt(0.5)
        signed_cos = 1.0 if cos > 0 else -1.0
        signed_sin = 1.0 if sin > 0 else -1.0
        a = real * root
        b = imag * root
        if signed_cos == signed_sin:
            return (a - b, a + b) if signed_cos > 0 else (b - a, -a - b)
        return (a + b, b - a) if signed_cos > 0 else (-a - b, a - b)
    return real * cos - imag * sin, real * sin + imag * cos


def real_dft(values, length):
    if length == 2:
        if len(values) == 1:
            return [(values[0], None), (values[0], None)]
        return [(values[0] + values[1], None), (values[0] - values[1], None)]
    half, quarter = length // 2, length // 4
    if len(values) == length:
        total = [values[b] + values[b + half] for b in range(half)]
        rest = [values[b] - values[b + half] for b in range(half)]
    else:
        total = values
        rest = values
    out = [None] * (half + 1)
    for index, value in enumerate(real_dft(total, half)):
        out[2 * index] = value
    turned = [
        twist((rest[b], -rest[b + quarter]), -b, length) for b in range(quarter)
    ]
    for index, (real, imag) in enumerate(complex_dft(turned, -1)):
        place = 4 * index + 1
        if place <= half:
            out[place] = (real, imag)
        else:
            out[length - place] = (real, -imag)
    return out


def real_dft_transposed(spectrum, length, padded):
    if length == 2:
        first, second = spectrum[0][0], spectrum[1][0]
        return [first + second] if padded else [first + second, first - second]
    half, quarter = length // 2, length // 4
    total = real_dft_transposed(
        [spectrum[2 * index] for index in range(quarter + 1)], half, False
    )
    odd = []
    for index in range(quarter):
        place = 4 * index + 1
        if place <= half:
            odd.append(spectrum[place])
        else:
            real, imag = spectrum[length - place]
            odd.append((real, -imag))
    rest = [None] * half
    for b, value in enumerate(complex_dft(odd, 1)):
        real, imag = twist(value, b, length)
        rest[b] = real
        rest[b + quarter] = -imag
    low = [total[b] + rest[b] for b in range(half)]
    if padded:
        return low
    return low + [total[b] - rest[b] for b in range(half)]


def pack_inputs(dests, token_ref, pre_ref, feat_ref, filt_ref, out_ref):
    width = out_ref.shape[1] // 2
    keep = (token_ref[...] < BASES).astype(BF16)
    mixer = (pre_ref[...].astype(F32) * feat_ref[...].astype(F32)).astype(BF16).T * keep
    filt = filt_ref[...].astype(BF16).T
    for k in range(dests):
        at = slice(k * width, (k + 1) * width)
        out_ref[k] = jnp.concatenate([mixer[at], filt[at]], axis=0)


def own_grad(rank_ref, own_ref, weight_ref, out_ref):
    out_ref[...] = times_transposed(weight_ref[...], own_ref[...])


def times_transposed(left, right):
    return lax.dot_general(left, right, (((1,), (1,)), ((), ())), preferred_element_type=F32)


def pack_grad(
    dests, rank_ref, other_ref, weight_ref, part_ref, post_ref, gated_ref, out_ref, away_ref
):
    width = out_ref.shape[1]
    weight = weight_ref[...]
    away_ref[...] = weight
    grad_gated = part_ref[...] + times_transposed(weight, other_ref[...])
    gated_ref[...] = grad_gated
    mixed = grad_gated * post_ref[...].T.astype(F32)
    for k in range(dests):
        out_ref[k] = mixed[k * width : (k + 1) * width].astype(BF16)


def group_order(n):
    return [*range(n // 2, n), *range(n // 2 - 1, -1, -1)]


def group_places(n):
    return [int(place) for place in np.argsort(group_order(n))]


def started(*copies):
    made = [pltpu.make_async_copy(*copy) for copy in copies]
    for copy in made:
        copy.start()
    return made


def forward_blocks(n, blocks, twist_ref, mid_ref, rows):
    length = mid_ref.shape[2] // 2
    for m, (real, imag) in enumerate(real_dft([x.astype(F32) for x in blocks], 2 * n)):
        cos, sin = twist_ref[m : m + 1], twist_ref[n + 1 + m : n + 2 + m]
        if m == 0:
            imag = jnp.zeros_like(real)
        elif imag is None:
            real, imag = real * cos, -(real * sin)
        else:
            real, imag = real * cos + imag * sin, imag * cos - real * sin
        mid_ref[m, rows, :length] = real.astype(mid_ref.dtype)
        mid_ref[m, rows, length:] = imag.astype(mid_ref.dtype)


def inverse_blocks(n, back, twist_ref):
    length = back.shape[1] // 2
    rows = back.shape[0] // (n + 1)
    spectrum = []
    for m in range(n + 1):
        cos, sin = twist_ref[m : m + 1], twist_ref[n + 1 + m : n + 2 + m]
        at = slice(m * rows, (m + 1) * rows)
        real, imag = back[at, :length], back[at, length:]
        if m == 0:
            spectrum.append((0.5 * real, None))
        elif m == n:
            spectrum.append((0.5 * (real * cos - imag * sin), None))
        else:
            spectrum.append((real * cos - imag * sin, real * sin + imag * cos))
    return [x.astype(BF16) for x in real_dft_transposed(spectrum, 2 * n, True)]


def inner_product(values_ref, matrix):
    count, rows, wide = values_ref.shape
    values = values_ref[...].reshape(count * rows, wide).astype(BF16)
    return jnp.dot(values, matrix, preferred_element_type=F32)


def dft_matrices(dft_ref, points):
    length = dft_ref.shape[0]
    cos, sin = dft_ref[:, :length], dft_ref[:, length:]
    forward = jnp.concatenate(
        [jnp.concatenate([cos, -sin], axis=1), jnp.concatenate([sin, cos], axis=1)], axis=0
    )
    cos, sin = cos * (1.0 / points), sin * (1.0 / points)
    back = jnp.concatenate(
        [jnp.concatenate([cos, sin], axis=1), jnp.concatenate([-sin, cos], axis=1)], axis=0
    )
    return forward, back


def row_chunks(rows):
    return max(1, rows // 16)


def mix_forward(
    n,
    pair_ref,
    grad_ref,
    twist_ref,
    dft_ref,
    both_ref,
    filt_ref,
    mid_ref,
    prod_ref,
):
    length = twist_ref.shape[1]
    width = grad_ref.shape[1]
    chunks = row_chunks(width)
    step = width // chunks
    forward, back = dft_matrices(dft_ref, n * length)
    both_ref[:, :, length:] = grad_ref[...]

    def transform(c):
        for kind in range(2):
            start = kind * width + c * step
            blocks = [pair_ref[b, start : start + step] for b in group_places(n)]
            forward_blocks(
                n, blocks, twist_ref, mid_ref.at[c], slice(kind * step, (kind + 1) * step)
            )

    transform(0)
    for c in range(chunks):
        at = slice(c * step, (c + 1) * step)
        if c + 1 < chunks:
            transform(c + 1)
        spec = inner_product(mid_ref.at[c], forward)
        for m in range(n + 1):
            first = 2 * m * step
            signal, filt = spec[first : first + step], spec[first + step : first + 2 * step]
            filt_ref[m, at] = filt.astype(filt_ref.dtype)
            real, imag = signal[:, :length], signal[:, length:]
            filt_real, filt_imag = filt[:, :length], filt[:, length:]
            prod_ref[c, m, :, :length] = (real * filt_real - imag * filt_imag).astype(
                prod_ref.dtype
            )
            prod_ref[c, m, :, length:] = (real * filt_imag + imag * filt_real).astype(
                prod_ref.dtype
            )
        mid = inner_product(prod_ref.at[c], back)
        for b, value in zip(group_places(n), inverse_blocks(n, mid, twist_ref)):
            both_ref[b, at, :length] = value


def mix_backward(
    n,
    both_ref,
    post_ref,
    twist_ref,
    dft_ref,
    filt_ref,
    weight_ref,
    out_hbm,
    gated_hbm,
    away_hbm,
    mid_ref,
    prod_ref,
    out_ref,
    gated_ref,
    away_ref,
    sems,
):
    length = twist_ref.shape[1]
    width = out_ref.shape[1]
    forward, back = dft_matrices(dft_ref, n * length)
    mixed = channel_rows(both_ref, length).T.astype(F32)
    gated = (post_ref[...].astype(F32) * mixed).astype(BF16)
    gated_ref[...] = gated
    away_ref[...] = jnp.dot(gated, weight_ref[...], preferred_element_type=F32).astype(BF16)
    copies = started((away_ref, away_hbm, sems.at[0]), (gated_ref, gated_hbm, sems.at[1]))
    chunks = row_chunks(width)
    step = width // chunks

    def transform(c):
        blocks = [both_ref[b, c * step : (c + 1) * step, length:] for b in group_places(n)]
        forward_blocks(n, blocks, twist_ref, mid_ref.at[c], slice(0, step))

    transform(0)
    for c in range(chunks):
        at = slice(c * step, (c + 1) * step)
        if c + 1 < chunks:
            transform(c + 1)
        spec = inner_product(mid_ref.at[c], forward)
        for m in range(n + 1):
            signal, filt = spec[m * step : (m + 1) * step], filt_ref[m, at].astype(F32)
            real, imag = signal[:, :length], signal[:, length:]
            filt_real, filt_imag = filt[:, :length], filt[:, length:]
            prod_ref[c, m, :, :length] = (filt_real * real + filt_imag * imag).astype(
                prod_ref.dtype
            )
            prod_ref[c, m, :, length:] = (filt_real * imag - filt_imag * real).astype(
                prod_ref.dtype
            )
        mid = inner_product(prod_ref.at[c], back)
        for b, value in zip(group_places(n), inverse_blocks(n, mid, twist_ref)):
            out_ref[b, at] = value
        if chunks == 1:
            copies += started((out_ref, out_hbm, sems.at[2]))
        else:
            rows = pl.ds(c * step, step)
            copies += started((out_ref.at[:, rows], out_hbm.at[:, rows], sems.at[2 + c]))
    for copy in copies:
        copy.wait()


def channel_rows(blocks_ref, length):
    return jnp.concatenate(
        [blocks_ref[k, :, :length] for k in range(blocks_ref.shape[0])], axis=0
    )


def weight_copies(parts, side, weight_hbm, weight_ref, sems):
    channels, columns = weight_ref.shape
    rows = channels // parts
    start = pl.multiple_of(side * columns, LANES)
    return started(
        *(
            (
                weight_hbm.at[pl.ds(k * rows, rows), pl.ds(start, columns)],
                weight_ref.at[pl.ds(k * rows, rows)],
                sems[k],
            )
            for k in range(parts)
        )
    )


def part_products(copies, gated, weight_ref):
    rows = weight_ref.shape[0] // len(copies)
    total = None
    for k, copy in enumerate(copies):
        copy.wait()
        at = slice(k * rows, (k + 1) * rows)
        product = jnp.dot(gated[:, at], weight_ref[at], preferred_element_type=F32)
        total = product if total is None else total + product
    return total


def project_home(
    parts,
    rank_ref,
    gated_ref,
    both_ref,
    grad_ref,
    weight_hbm,
    home_ref,
    post_grad_ref,
    weight_ref,
    sems,
):
    copies = weight_copies(
        parts, rank_ref[0], weight_hbm, weight_ref, [sems.at[k] for k in range(parts)]
    )
    mixed = channel_rows(both_ref, grad_ref.shape[1]).astype(F32)
    post_grad_ref[...] = (grad_ref[...] * mixed).astype(BF16).T
    home_ref[...] = part_products(copies, gated_ref[...], weight_ref)


def input_grads(
    parts,
    token_ref,
    packed_ref,
    pre_ref,
    feat_ref,
    pre_grad_hbm,
    feat_grad_hbm,
    pre_grad_ref,
    feat_grad_ref,
    sems,
):
    keep = (token_ref[...] < BASES).astype(BF16)
    dests = packed_ref.shape[0] // parts
    cut = pre_ref.shape[1] // parts
    copies = []
    for k in range(parts):
        at = pl.ds(k * cut, cut)
        blocks = packed_ref.at[pl.ds(k * dests, dests)]
        grad = (channel_rows(blocks, blocks.shape[2]) * keep).T.astype(F32)
        pre_grad_ref[:, at] = (grad * feat_ref[:, at].astype(F32)).astype(BF16)
        feat_grad_ref[:, at] = (grad * pre_ref[:, at].astype(F32)).astype(BF16)
        copies += started(
            (pre_grad_ref.at[:, at], pre_grad_hbm.at[:, at], sems.at[0, k]),
            (feat_grad_ref.at[:, at], feat_grad_hbm.at[:, at], sems.at[1, k]),
        )
    for copy in copies:
        copy.wait()


def add_halves(home_ref, other_ref, after_hbm, out_ref):
    out_ref[...] = (home_ref[...] + other_ref[...].astype(F32)).astype(BF16)


def dft_tables(n, length):
    index = np.arange(length)
    angle = index[:, None] * index[None, :] % length * (2.0 * math.pi / length)
    dft = np.concatenate([np.cos(angle), np.sin(angle)], axis=1).astype(jnp.bfloat16)
    angle = np.arange(n + 1)[:, None] * index[None, :] * (math.pi / (n * length))
    twist = np.concatenate([np.cos(angle), np.sin(angle)], axis=0).astype(np.float32)
    return twist, dft


def call(kernel, outs, args, grid=None, blocks=None, out_blocks=None, flops=0, scratch=(), prefetch=0, from_hbm=()):
    leaves = jax.tree.leaves(outs)
    args = [
        pltpu.with_memory_space_constraint(x, pltpu.HBM) if k in from_hbm else x
        for k, x in enumerate(args)
    ]
    tensors = args[prefetch:]

    def spec(array, block):
        if block == "hbm":
            return pl.BlockSpec(memory_space=pltpu.HBM)
        if block is None:
            rank = len(array.shape)
            if grid is None:
                return pl.BlockSpec(memory_space=pltpu.VMEM)
            return pl.BlockSpec(array.shape, lambda *_: (0,) * rank)
        return pl.BlockSpec(*block)

    blocks = blocks or [None] * len(tensors)
    out_blocks = out_blocks or [None] * len(leaves)
    in_specs = [spec(x, b) for x, b in zip(tensors, blocks)]
    out_specs = [spec(x, b) for x, b in zip(leaves, out_blocks)]
    moved = sum(math.prod(x.shape) * np.dtype(x.dtype).itemsize for x in [*tensors, *leaves])
    return pl.pallas_call(
        kernel,
        out_shape=outs,
        grid_spec=pltpu.PrefetchScalarGridSpec(
            num_scalar_prefetch=prefetch,
            grid=grid or (),
            in_specs=in_specs,
            out_specs=out_specs if isinstance(outs, tuple) else out_specs[0],
            scratch_shapes=list(scratch),
        ),
        compiler_params=pltpu.CompilerParams(vmem_limit_bytes=VMEM_GRANT),
        cost_estimate=pl.CostEstimate(flops=flops, bytes_accessed=moved, transcendentals=0),
    )(*args)


def exchange(block):
    return lax.all_to_all(
        block,
        "ctx",
        split_axis=0,
        concat_axis=0,
        tiled=True,
        axis_index_groups=[group_order(block.shape[0])],
    )


def swap_tp(block):
    count = lax.axis_size("tp")
    assert count == 2
    return lax.ppermute(block, "tp", [(0, 1), (1, 0)])


def on_device(
    tables, post_gate, pre_gate, features, filters, token_ids, out_weight, out_grad
):
    n = lax.axis_size("ctx")
    length, channels = post_gate.shape
    columns = out_grad.shape[1]
    width = channels // n
    shape = jax.ShapeDtypeStruct
    one = (n, width, length)
    pair = (n, 2 * width, length)
    both = (n, width, 2 * length)
    twist, dft = tables
    tokens = token_ids.reshape(1, length)
    rank = lax.axis_index("tp").astype(jnp.int32).reshape(1)
    inner_flops = 2 * (n + 1) * (2 * length) ** 2 * width
    spec_shape = (n + 1, width, 2 * length)
    narrow = BF16 if width >= 16 else F32
    chunks = row_chunks(width)
    narrow_scratch = pltpu.VMEM((chunks, n + 1, width // chunks, 2 * length), narrow)

    def by_channels(steps):
        cut, dests = channels // steps, n // steps
        return (
            ((length, cut), lambda i, *_: (0, i)),
            ((cut, length), lambda i, *_: (i, 0)),
            ((dests, *one[1:]), lambda i, *_: (i, 0, 0)),
        )

    other_grad = swap_tp(out_grad)
    steps = 2
    flat, _, _ = by_channels(steps)
    pair_out = call(
        functools.partial(pack_inputs, n // steps),
        pltpu.HBM(pair, BF16),
        (tokens, pre_gate, features, filters),
        grid=(steps,),
        blocks=[None, flat, flat, flat],
        out_blocks=[((n // steps, *pair[1:]), lambda i, *_: (i, 0, 0))],
        from_hbm=range(4),
    )
    pair_in = exchange(pair_out)
    steps = 4
    flat, turned, packed = by_channels(steps)
    weight_block = (channels // steps, columns)
    grad_part = call(
        own_grad,
        pltpu.VMEM((channels, length), F32),
        (rank, out_grad, out_weight),
        grid=(steps,),
        blocks=[None, (weight_block, lambda i, rank: (i, rank[0]))],
        out_blocks=[turned],
        flops=2 * length * channels * columns,
        prefetch=1,
        from_hbm=(1, 2),
    )
    grad_gated, grad_out, away_weight = call(
        functools.partial(pack_grad, n // steps),
        (
            pltpu.HBM((channels, length), F32),
            pltpu.VMEM(one, BF16),
            pltpu.VMEM((channels, columns), BF16),
        ),
        (rank, other_grad, out_weight, grad_part, post_gate),
        grid=(steps,),
        blocks=[None, (weight_block, lambda i, rank: (i, 1 - rank[0])), turned, flat],
        out_blocks=[turned, packed, (weight_block, lambda i, *_: (i, 0))],
        flops=2 * length * channels * columns,
        prefetch=1,
        from_hbm=(2, 4),
    )
    both_out, filt_spec = call(
        functools.partial(mix_forward, n),
        (
            shape(both, BF16),
            pltpu.VMEM(spec_shape, narrow),
        ),
        (pair_in, grad_out, twist, dft),
        flops=3 * inner_flops,
        scratch=[
            pltpu.VMEM((chunks, n + 1, 2 * width // chunks, 2 * length), BF16),
            narrow_scratch,
        ],
    )
    both_in = exchange(both_out)
    grad_back_out, gated, away = call(
        functools.partial(mix_backward, n),
        (
            pltpu.HBM(one, BF16),
            pltpu.HBM((length, channels), BF16),
            pltpu.HBM((length, columns), BF16),
        ),
        (both_in, post_gate, twist, dft, filt_spec, away_weight),
        out_blocks=["hbm", "hbm", "hbm"],
        flops=2 * inner_flops + 2 * length * channels * columns,
        scratch=[
            narrow_scratch,
            narrow_scratch,
            pltpu.VMEM(one, BF16),
            pltpu.VMEM((length, channels), BF16),
            pltpu.VMEM((length, columns), BF16),
            pltpu.SemaphoreType.DMA((2 + chunks,)),
        ],
    )
    grad_back_in = exchange(grad_back_out)
    other_part = swap_tp(away)
    parts = 2
    home, grad_post = call(
        functools.partial(project_home, parts),
        (shape((length, columns), F32), shape((length, channels), BF16)),
        (rank, gated, both_in, grad_gated, out_weight),
        grid=(1,),
        blocks=[None, (one, lambda *_: (0, 0, 0)), None, "hbm"],
        flops=2 * length * channels * columns,
        scratch=[pltpu.VMEM((channels, columns), BF16), pltpu.SemaphoreType.DMA((parts,))],
        prefetch=1,
    )
    flat = (length, channels)
    grad_pre, grad_features = call(
        functools.partial(input_grads, parts),
        (pltpu.HBM(flat, BF16), pltpu.HBM(flat, BF16)),
        (tokens, grad_back_in, pre_gate, features),
        out_blocks=["hbm"] * 2,
        scratch=[
            pltpu.VMEM(flat, BF16),
            pltpu.VMEM(flat, BF16),
            pltpu.SemaphoreType.DMA((2, parts)),
        ],
    )
    output = call(
        add_halves,
        pltpu.HBM((length, columns), BF16),
        (home, other_part, grad_features),
        blocks=[None, None, "hbm"],
        from_hbm=(2,),
    )
    return (output, grad_post, grad_pre, grad_features)


def solution(mesh):
    in_specs = (
        P("ctx", "tp"),
        P("ctx", "tp"),
        P("ctx", "tp"),
        P("ctx", "tp"),
        P("ctx"),
        P("tp", None),
        P("ctx", "tp"),
    )
    out_specs = (P("ctx", "tp"), P("ctx", "tp"), P("ctx", "tp"), P("ctx", "tp"))

    def run(*args):
        n = mesh.shape["ctx"]
        tables = tuple(jnp.asarray(x) for x in dft_tables(n, args[0].shape[0] // n))
        return jax.shard_map(
            functools.partial(on_device, tables),
            mesh=mesh,
            in_specs=in_specs,
            out_specs=out_specs,
            check_vma=False,
        )(*args)

    return run
```

```python
import functools
import math

import jax
import jax.numpy as jnp
import numpy as np
from jax import lax
from jax.experimental import pallas as pl
from jax.experimental.pallas import tpu as pltpu
from jax.sharding import PartitionSpec as P

BASES = 4
LANES = 128
VMEM_GRANT = 24 * 2**20
F32 = jnp.float32
BF16 = jnp.bfloat16


def complex_dft(values, sign):
    length = len(values)
    if length == 1:
        return values
    half = length // 2
    even = [
        (values[b][0] + values[b + half][0], values[b][1] + values[b + half][1])
        for b in range(half)
    ]
    odd = [
        twist(
            (values[b][0] - values[b + half][0], values[b][1] - values[b + half][1]),
            sign * b,
            length,
        )
        for b in range(half)
    ]
    even = complex_dft(even, sign)
    odd = complex_dft(odd, sign)
    return [part for pair in zip(even, odd) for part in pair]


def twist(value, step, length):
    real, imag = value
    step = step % length
    if step == 0:
        return real, imag
    if 4 * step == length:
        return -imag, real
    if 2 * step == length:
        return -real, -imag
    if 4 * step == 3 * length:
        return imag, -real
    cos = math.cos(2.0 * math.pi * step / length)
    sin = math.sin(2.0 * math.pi * step / length)
    if 8 * step % length == 0:
        root = math.sqrt(0.5)
        signed_cos = 1.0 if cos > 0 else -1.0
        signed_sin = 1.0 if sin > 0 else -1.0
        a = real * root
        b = imag * root
        if signed_cos == signed_sin:
            return (a - b, a + b) if signed_cos > 0 else (b - a, -a - b)
        return (a + b, b - a) if signed_cos > 0 else (-a - b, a - b)
    return real * cos - imag * sin, real * sin + imag * cos


def real_dft(values, length):
    if length == 2:
        if len(values) == 1:
            return [(values[0], None), (values[0], None)]
        return [(values[0] + values[1], None), (values[0] - values[1], None)]
    half, quarter = length // 2, length // 4
    if len(values) == length:
        total = [values[b] + values[b + half] for b in range(half)]
        rest = [values[b] - values[b + half] for b in range(half)]
    else:
        total = values
        rest = values
    out = [None] * (half + 1)
    for index, value in enumerate(real_dft(total, half)):
        out[2 * index] = value
    turned = [
        twist((rest[b], -rest[b + quarter]), -b, length) for b in range(quarter)
    ]
    for index, (real, imag) in enumerate(complex_dft(turned, -1)):
        place = 4 * index + 1
        if place <= half:
            out[place] = (real, imag)
        else:
            out[length - place] = (real, -imag)
    return out


def real_dft_transposed(spectrum, length, padded):
    if length == 2:
        first, second = spectrum[0][0], spectrum[1][0]
        return [first + second] if padded else [first + second, first - second]
    half, quarter = length // 2, length // 4
    total = real_dft_transposed(
        [spectrum[2 * index] for index in range(quarter + 1)], half, False
    )
    odd = []
    for index in range(quarter):
        place = 4 * index + 1
        if place <= half:
            odd.append(spectrum[place])
        else:
            real, imag = spectrum[length - place]
            odd.append((real, -imag))
    rest = [None] * half
    for b, value in enumerate(complex_dft(odd, 1)):
        real, imag = twist(value, b, length)
        rest[b] = real
        rest[b + quarter] = -imag
    low = [total[b] + rest[b] for b in range(half)]
    if padded:
        return low
    return low + [total[b] - rest[b] for b in range(half)]


def pack_inputs(dests, token_ref, pre_ref, feat_ref, filt_ref, out_ref):
    width = out_ref.shape[1] // 2
    keep = (token_ref[...] < BASES).astype(BF16)
    mixer = (pre_ref[...].astype(F32) * feat_ref[...].astype(F32)).astype(BF16).T * keep
    filt = filt_ref[...].astype(BF16).T
    for k in range(dests):
        at = slice(k * width, (k + 1) * width)
        out_ref[k] = jnp.concatenate([mixer[at], filt[at]], axis=0)


def own_grad(rank_ref, own_ref, weight_ref, out_ref):
    out_ref[...] = times_transposed(weight_ref[...], own_ref[...])


def times_transposed(left, right):
    return lax.dot_general(left, right, (((1,), (1,)), ((), ())), preferred_element_type=F32)


def pack_grad(
    dests, rank_ref, other_ref, weight_ref, part_ref, post_ref, gated_ref, out_ref, away_ref
):
    width = out_ref.shape[1]
    weight = weight_ref[...]
    away_ref[...] = weight
    grad_gated = part_ref[...] + times_transposed(weight, other_ref[...])
    gated_ref[...] = grad_gated
    mixed = grad_gated * post_ref[...].T.astype(F32)
    for k in range(dests):
        out_ref[k] = mixed[k * width : (k + 1) * width].astype(BF16)


def group_order(n):
    half = n // 2
    return [rank for i in range(half) for rank in (half + i, half - 1 - i)]


def group_places(n):
    return [int(place) for place in np.argsort(group_order(n))]


def started(*copies):
    made = [pltpu.make_async_copy(*copy) for copy in copies]
    for copy in made:
        copy.start()
    return made


def forward_blocks(n, blocks, twist_ref, mid_ref, rows):
    length = mid_ref.shape[2] // 2
    for m, (real, imag) in enumerate(real_dft([x.astype(F32) for x in blocks], 2 * n)):
        cos, sin = twist_ref[m : m + 1], twist_ref[n + 1 + m : n + 2 + m]
        if m == 0:
            imag = jnp.zeros_like(real)
        elif imag is None:
            real, imag = real * cos, -(real * sin)
        else:
            real, imag = real * cos + imag * sin, imag * cos - real * sin
        mid_ref[m, rows, :length] = real.astype(mid_ref.dtype)
        mid_ref[m, rows, length:] = imag.astype(mid_ref.dtype)


def inverse_blocks(n, back, twist_ref):
    length = back.shape[1] // 2
    rows = back.shape[0] // (n + 1)
    spectrum = []
    for m in range(n + 1):
        cos, sin = twist_ref[m : m + 1], twist_ref[n + 1 + m : n + 2 + m]
        at = slice(m * rows, (m + 1) * rows)
        real, imag = back[at, :length], back[at, length:]
        if m == 0:
            spectrum.append((0.5 * real, None))
        elif m == n:
            spectrum.append((0.5 * (real * cos - imag * sin), None))
        else:
            spectrum.append((real * cos - imag * sin, real * sin + imag * cos))
    return [x.astype(BF16) for x in real_dft_transposed(spectrum, 2 * n, True)]


def inner_product(values_ref, matrix):
    count, rows, wide = values_ref.shape
    values = values_ref[...].reshape(count * rows, wide).astype(BF16)
    return jnp.dot(values, matrix, preferred_element_type=F32)


def dft_matrices(dft_ref, points):
    length = dft_ref.shape[0]
    cos, sin = dft_ref[:, :length], dft_ref[:, length:]
    forward = jnp.concatenate(
        [jnp.concatenate([cos, -sin], axis=1), jnp.concatenate([sin, cos], axis=1)], axis=0
    )
    cos, sin = cos * (1.0 / points), sin * (1.0 / points)
    back = jnp.concatenate(
        [jnp.concatenate([cos, sin], axis=1), jnp.concatenate([-sin, cos], axis=1)], axis=0
    )
    return forward, back


def row_chunks(rows):
    return max(1, rows // 16)


def mix_forward(
    n,
    pair_ref,
    grad_ref,
    twist_ref,
    dft_ref,
    both_ref,
    filt_ref,
    mid_ref,
    prod_ref,
):
    length = twist_ref.shape[1]
    width = grad_ref.shape[1]
    chunks = row_chunks(width)
    step = width // chunks
    forward, back = dft_matrices(dft_ref, n * length)
    both_ref[:, :, length:] = grad_ref[...]

    def transform(c):
        for kind in range(2):
            start = kind * width + c * step
            blocks = [pair_ref[b, start : start + step] for b in group_places(n)]
            forward_blocks(
                n, blocks, twist_ref, mid_ref.at[c], slice(kind * step, (kind + 1) * step)
            )

    transform(0)
    for c in range(chunks):
        at = slice(c * step, (c + 1) * step)
        if c + 1 < chunks:
            transform(c + 1)
        spec = inner_product(mid_ref.at[c], forward)
        for m in range(n + 1):
            first = 2 * m * step
            signal, filt = spec[first : first + step], spec[first + step : first + 2 * step]
            filt_ref[m, at] = filt.astype(filt_ref.dtype)
            real, imag = signal[:, :length], signal[:, length:]
            filt_real, filt_imag = filt[:, :length], filt[:, length:]
            prod_ref[c, m, :, :length] = (real * filt_real - imag * filt_imag).astype(
                prod_ref.dtype
            )
            prod_ref[c, m, :, length:] = (real * filt_imag + imag * filt_real).astype(
                prod_ref.dtype
            )
        mid = inner_product(prod_ref.at[c], back)
        for b, value in zip(group_places(n), inverse_blocks(n, mid, twist_ref)):
            both_ref[b, at, :length] = value


def mix_backward(
    n,
    both_ref,
    post_ref,
    twist_ref,
    dft_ref,
    filt_ref,
    weight_ref,
    out_hbm,
    gated_hbm,
    away_hbm,
    mid_ref,
    prod_ref,
    out_ref,
    gated_ref,
    away_ref,
    sems,
):
    length = twist_ref.shape[1]
    width = out_ref.shape[1]
    forward, back = dft_matrices(dft_ref, n * length)
    mixed = channel_rows(both_ref, length).T.astype(F32)
    gated = (post_ref[...].astype(F32) * mixed).astype(BF16)
    gated_ref[...] = gated
    away_ref[...] = jnp.dot(gated, weight_ref[...], preferred_element_type=F32).astype(BF16)
    copies = started((away_ref, away_hbm, sems.at[0]), (gated_ref, gated_hbm, sems.at[1]))
    chunks = row_chunks(width)
    step = width // chunks

    def transform(c):
        blocks = [both_ref[b, c * step : (c + 1) * step, length:] for b in group_places(n)]
        forward_blocks(n, blocks, twist_ref, mid_ref.at[c], slice(0, step))

    transform(0)
    for c in range(chunks):
        at = slice(c * step, (c + 1) * step)
        if c + 1 < chunks:
            transform(c + 1)
        spec = inner_product(mid_ref.at[c], forward)
        for m in range(n + 1):
            signal, filt = spec[m * step : (m + 1) * step], filt_ref[m, at].astype(F32)
            real, imag = signal[:, :length], signal[:, length:]
            filt_real, filt_imag = filt[:, :length], filt[:, length:]
            prod_ref[c, m, :, :length] = (filt_real * real + filt_imag * imag).astype(
                prod_ref.dtype
            )
            prod_ref[c, m, :, length:] = (filt_real * imag - filt_imag * real).astype(
                prod_ref.dtype
            )
        mid = inner_product(prod_ref.at[c], back)
        for b, value in zip(group_places(n), inverse_blocks(n, mid, twist_ref)):
            out_ref[b, at] = value
        if chunks == 1:
            copies += started((out_ref, out_hbm, sems.at[2]))
        else:
            rows = pl.ds(c * step, step)
            copies += started((out_ref.at[:, rows], out_hbm.at[:, rows], sems.at[2 + c]))
    for copy in copies:
        copy.wait()


def channel_rows(blocks_ref, length):
    return jnp.concatenate(
        [blocks_ref[k, :, :length] for k in range(blocks_ref.shape[0])], axis=0
    )


def weight_copies(parts, side, weight_hbm, weight_ref, sems):
    channels, columns = weight_ref.shape
    rows = channels // parts
    start = pl.multiple_of(side * columns, LANES)
    return started(
        *(
            (
                weight_hbm.at[pl.ds(k * rows, rows), pl.ds(start, columns)],
                weight_ref.at[pl.ds(k * rows, rows)],
                sems[k],
            )
            for k in range(parts)
        )
    )


def part_products(copies, gated, weight_ref):
    rows = weight_ref.shape[0] // len(copies)
    total = None
    for k, copy in enumerate(copies):
        copy.wait()
        at = slice(k * rows, (k + 1) * rows)
        product = jnp.dot(gated[:, at], weight_ref[at], preferred_element_type=F32)
        total = product if total is None else total + product
    return total


def project_home(
    parts,
    rank_ref,
    gated_ref,
    both_ref,
    grad_ref,
    weight_hbm,
    home_ref,
    post_grad_ref,
    weight_ref,
    sems,
):
    copies = weight_copies(
        parts, rank_ref[0], weight_hbm, weight_ref, [sems.at[k] for k in range(parts)]
    )
    mixed = channel_rows(both_ref, grad_ref.shape[1]).astype(F32)
    post_grad_ref[...] = (grad_ref[...] * mixed).astype(BF16).T
    home_ref[...] = part_products(copies, gated_ref[...], weight_ref)


def finish(
    parts,
    token_ref,
    packed_ref,
    pre_ref,
    feat_ref,
    home_ref,
    other_ref,
    pre_grad_hbm,
    feat_grad_hbm,
    out_hbm,
    pre_grad_ref,
    feat_grad_ref,
    out_ref,
    sems,
):
    out_ref[...] = (home_ref[...] + other_ref[...].astype(F32)).astype(BF16)
    copies = started((out_ref, out_hbm, sems.at[2, 0]))
    keep = (token_ref[...] < BASES).astype(BF16)
    dests = packed_ref.shape[0] // parts
    cut = pre_ref.shape[1] // parts
    for k in range(parts):
        at = pl.ds(k * cut, cut)
        blocks = packed_ref.at[pl.ds(k * dests, dests)]
        grad = (channel_rows(blocks, blocks.shape[2]) * keep).T.astype(F32)
        pre_grad_ref[:, at] = (grad * feat_ref[:, at].astype(F32)).astype(BF16)
        feat_grad_ref[:, at] = (grad * pre_ref[:, at].astype(F32)).astype(BF16)
        copies += started(
            (pre_grad_ref.at[:, at], pre_grad_hbm.at[:, at], sems.at[0, k]),
            (feat_grad_ref.at[:, at], feat_grad_hbm.at[:, at], sems.at[1, k]),
        )
    for copy in copies:
        copy.wait()


def dft_tables(n, length):
    index = np.arange(length)
    angle = index[:, None] * index[None, :] % length * (2.0 * math.pi / length)
    dft = np.concatenate([np.cos(angle), np.sin(angle)], axis=1).astype(jnp.bfloat16)
    angle = np.arange(n + 1)[:, None] * index[None, :] * (math.pi / (n * length))
    twist = np.concatenate([np.cos(angle), np.sin(angle)], axis=0).astype(np.float32)
    return twist, dft


def call(kernel, outs, args, grid=None, blocks=None, out_blocks=None, flops=0, scratch=(), prefetch=0, from_hbm=()):
    leaves = jax.tree.leaves(outs)
    args = [
        pltpu.with_memory_space_constraint(x, pltpu.HBM) if k in from_hbm else x
        for k, x in enumerate(args)
    ]
    tensors = args[prefetch:]

    def spec(array, block):
        if block == "hbm":
            return pl.BlockSpec(memory_space=pltpu.HBM)
        if block is None:
            rank = len(array.shape)
            if grid is None:
                return pl.BlockSpec(memory_space=pltpu.VMEM)
            return pl.BlockSpec(array.shape, lambda *_: (0,) * rank)
        return pl.BlockSpec(*block)

    blocks = blocks or [None] * len(tensors)
    out_blocks = out_blocks or [None] * len(leaves)
    in_specs = [spec(x, b) for x, b in zip(tensors, blocks)]
    out_specs = [spec(x, b) for x, b in zip(leaves, out_blocks)]
    moved = sum(math.prod(x.shape) * np.dtype(x.dtype).itemsize for x in [*tensors, *leaves])
    return pl.pallas_call(
        kernel,
        out_shape=outs,
        grid_spec=pltpu.PrefetchScalarGridSpec(
            num_scalar_prefetch=prefetch,
            grid=grid or (),
            in_specs=in_specs,
            out_specs=out_specs if isinstance(outs, tuple) else out_specs[0],
            scratch_shapes=list(scratch),
        ),
        compiler_params=pltpu.CompilerParams(vmem_limit_bytes=VMEM_GRANT),
        cost_estimate=pl.CostEstimate(flops=flops, bytes_accessed=moved, transcendentals=0),
    )(*args)


def exchange(block):
    return lax.all_to_all(
        block,
        "ctx",
        split_axis=0,
        concat_axis=0,
        tiled=True,
        axis_index_groups=[group_order(block.shape[0])],
    )


def swap_tp(block):
    count = lax.axis_size("tp")
    assert count == 2
    return lax.ppermute(block, "tp", [(0, 1), (1, 0)])


def on_device(
    tables, post_gate, pre_gate, features, filters, token_ids, out_weight, out_grad
):
    n = lax.axis_size("ctx")
    length, channels = post_gate.shape
    columns = out_grad.shape[1]
    width = channels // n
    shape = jax.ShapeDtypeStruct
    one = (n, width, length)
    pair = (n, 2 * width, length)
    both = (n, width, 2 * length)
    twist, dft = tables
    tokens = token_ids.reshape(1, length)
    rank = lax.axis_index("tp").astype(jnp.int32).reshape(1)
    inner_flops = 2 * (n + 1) * (2 * length) ** 2 * width
    spec_shape = (n + 1, width, 2 * length)
    narrow = BF16 if width >= 16 else F32
    chunks = row_chunks(width)
    narrow_scratch = pltpu.VMEM((chunks, n + 1, width // chunks, 2 * length), narrow)

    def by_channels(steps):
        cut, dests = channels // steps, n // steps
        return (
            ((length, cut), lambda i, *_: (0, i)),
            ((cut, length), lambda i, *_: (i, 0)),
            ((dests, *one[1:]), lambda i, *_: (i, 0, 0)),
        )

    other_grad = swap_tp(out_grad)
    steps = 2
    flat, _, _ = by_channels(steps)
    pair_out = call(
        functools.partial(pack_inputs, n // steps),
        pltpu.HBM(pair, BF16),
        (tokens, pre_gate, features, filters),
        grid=(steps,),
        blocks=[None, flat, flat, flat],
        out_blocks=[((n // steps, *pair[1:]), lambda i, *_: (i, 0, 0))],
        from_hbm=range(4),
    )
    pair_in = exchange(pair_out)
    steps = 4
    flat, turned, packed = by_channels(steps)
    weight_block = (channels // steps, columns)
    grad_part = call(
        own_grad,
        pltpu.VMEM((channels, length), F32),
        (rank, out_grad, out_weight),
        grid=(steps,),
        blocks=[None, (weight_block, lambda i, rank: (i, rank[0]))],
        out_blocks=[turned],
        flops=2 * length * channels * columns,
        prefetch=1,
        from_hbm=(1, 2),
    )
    grad_gated, grad_out, away_weight = call(
        functools.partial(pack_grad, n // steps),
        (
            pltpu.HBM((channels, length), F32),
            pltpu.VMEM(one, BF16),
            pltpu.VMEM((channels, columns), BF16),
        ),
        (rank, other_grad, out_weight, grad_part, post_gate),
        grid=(steps,),
        blocks=[None, (weight_block, lambda i, rank: (i, 1 - rank[0])), turned, flat],
        out_blocks=[turned, packed, (weight_block, lambda i, *_: (i, 0))],
        flops=2 * length * channels * columns,
        prefetch=1,
        from_hbm=(2, 4),
    )
    both_out, filt_spec = call(
        functools.partial(mix_forward, n),
        (
            shape(both, BF16),
            pltpu.VMEM(spec_shape, narrow),
        ),
        (pair_in, grad_out, twist, dft),
        flops=3 * inner_flops,
        scratch=[
            pltpu.VMEM((chunks, n + 1, 2 * width // chunks, 2 * length), BF16),
            narrow_scratch,
        ],
    )
    both_in = exchange(both_out)
    grad_back_out, gated, away = call(
        functools.partial(mix_backward, n),
        (
            pltpu.HBM(one, BF16),
            pltpu.HBM((length, channels), BF16),
            pltpu.HBM((length, columns), BF16),
        ),
        (both_in, post_gate, twist, dft, filt_spec, away_weight),
        out_blocks=["hbm", "hbm", "hbm"],
        flops=2 * inner_flops + 2 * length * channels * columns,
        scratch=[
            narrow_scratch,
            narrow_scratch,
            pltpu.VMEM(one, BF16),
            pltpu.VMEM((length, channels), BF16),
            pltpu.VMEM((length, columns), BF16),
            pltpu.SemaphoreType.DMA((2 + chunks,)),
        ],
    )
    grad_back_in = exchange(grad_back_out)
    other_part = swap_tp(away)
    parts = 2
    home, grad_post = call(
        functools.partial(project_home, parts),
        (shape((length, columns), F32), shape((length, channels), BF16)),
        (rank, gated, both_in, grad_gated, out_weight),
        grid=(1,),
        blocks=[None, (one, lambda *_: (0, 0, 0)), None, "hbm"],
        flops=2 * length * channels * columns,
        scratch=[pltpu.VMEM((channels, columns), BF16), pltpu.SemaphoreType.DMA((parts,))],
        prefetch=1,
    )
    flat = (length, channels)
    grad_pre, grad_features, output = call(
        functools.partial(finish, parts),
        (pltpu.HBM(flat, BF16), pltpu.HBM(flat, BF16), pltpu.HBM((length, columns), BF16)),
        (tokens, grad_back_in, pre_gate, features, home, other_part),
        out_blocks=["hbm"] * 3,
        scratch=[
            pltpu.VMEM(flat, BF16),
            pltpu.VMEM(flat, BF16),
            pltpu.VMEM((length, columns), BF16),
            pltpu.SemaphoreType.DMA((3, parts)),
        ],
    )
    return (output, grad_post, grad_pre, grad_features)


def solution(mesh):
    in_specs = (
        P("ctx", "tp"),
        P("ctx", "tp"),
        P("ctx", "tp"),
        P("ctx", "tp"),
        P("ctx"),
        P("tp", None),
        P("ctx", "tp"),
    )
    out_specs = (P("ctx", "tp"), P("ctx", "tp"), P("ctx", "tp"), P("ctx", "tp"))

    def run(*args):
        n = mesh.shape["ctx"]
        tables = tuple(jnp.asarray(x) for x in dft_tables(n, args[0].shape[0] // n))
        return jax.shard_map(
            functools.partial(on_device, tables),
            mesh=mesh,
            in_specs=in_specs,
            out_specs=out_specs,
            check_vma=False,
        )(*args)

    return run
```

```python
import functools
import math

import jax
import jax.numpy as jnp
import numpy as np
from jax import lax
from jax.experimental import pallas as pl
from jax.experimental.pallas import tpu as pltpu
from jax.sharding import PartitionSpec as P

BASES = 4
LANES = 128
VMEM_GRANT = 24 * 2**20
F32 = jnp.float32
BF16 = jnp.bfloat16


def complex_dft(values, sign):
    length = len(values)
    if length == 1:
        return values
    half = length // 2
    even = [
        (values[b][0] + values[b + half][0], values[b][1] + values[b + half][1])
        for b in range(half)
    ]
    odd = [
        twist(
            (values[b][0] - values[b + half][0], values[b][1] - values[b + half][1]),
            sign * b,
            length,
        )
        for b in range(half)
    ]
    even = complex_dft(even, sign)
    odd = complex_dft(odd, sign)
    return [part for pair in zip(even, odd) for part in pair]


def twist(value, step, length):
    real, imag = value
    step = step % length
    if step == 0:
        return real, imag
    if 4 * step == length:
        return -imag, real
    if 2 * step == length:
        return -real, -imag
    if 4 * step == 3 * length:
        return imag, -real
    cos = math.cos(2.0 * math.pi * step / length)
    sin = math.sin(2.0 * math.pi * step / length)
    if 8 * step % length == 0:
        root = math.sqrt(0.5)
        signed_cos = 1.0 if cos > 0 else -1.0
        signed_sin = 1.0 if sin > 0 else -1.0
        a = real * root
        b = imag * root
        if signed_cos == signed_sin:
            return (a - b, a + b) if signed_cos > 0 else (b - a, -a - b)
        return (a + b, b - a) if signed_cos > 0 else (-a - b, a - b)
    return real * cos - imag * sin, real * sin + imag * cos


def real_dft(values, length):
    if length == 2:
        if len(values) == 1:
            return [(values[0], None), (values[0], None)]
        return [(values[0] + values[1], None), (values[0] - values[1], None)]
    half, quarter = length // 2, length // 4
    if len(values) == length:
        total = [values[b] + values[b + half] for b in range(half)]
        rest = [values[b] - values[b + half] for b in range(half)]
    else:
        total = values
        rest = values
    out = [None] * (half + 1)
    for index, value in enumerate(real_dft(total, half)):
        out[2 * index] = value
    turned = [
        twist((rest[b], -rest[b + quarter]), -b, length) for b in range(quarter)
    ]
    for index, (real, imag) in enumerate(complex_dft(turned, -1)):
        place = 4 * index + 1
        if place <= half:
            out[place] = (real, imag)
        else:
            out[length - place] = (real, -imag)
    return out


def real_dft_transposed(spectrum, length, padded):
    if length == 2:
        first, second = spectrum[0][0], spectrum[1][0]
        return [first + second] if padded else [first + second, first - second]
    half, quarter = length // 2, length // 4
    total = real_dft_transposed(
        [spectrum[2 * index] for index in range(quarter + 1)], half, False
    )
    odd = []
    for index in range(quarter):
        place = 4 * index + 1
        if place <= half:
            odd.append(spectrum[place])
        else:
            real, imag = spectrum[length - place]
            odd.append((real, -imag))
    rest = [None] * half
    for b, value in enumerate(complex_dft(odd, 1)):
        real, imag = twist(value, b, length)
        rest[b] = real
        rest[b + quarter] = -imag
    low = [total[b] + rest[b] for b in range(half)]
    if padded:
        return low
    return low + [total[b] - rest[b] for b in range(half)]


def pack_inputs(dests, token_ref, pre_ref, feat_ref, filt_ref, out_ref):
    width = out_ref.shape[1] // 2
    keep = (token_ref[...] < BASES).astype(BF16)
    mixer = (pre_ref[...].astype(F32) * feat_ref[...].astype(F32)).astype(BF16).T * keep
    filt = filt_ref[...].astype(BF16).T
    for k in range(dests):
        at = slice(k * width, (k + 1) * width)
        out_ref[k] = jnp.concatenate([mixer[at], filt[at]], axis=0)


def own_grad(rank_ref, own_ref, weight_ref, out_ref):
    out_ref[...] = times_transposed(weight_ref[...], own_ref[...])


def times_transposed(left, right):
    return lax.dot_general(left, right, (((1,), (1,)), ((), ())), preferred_element_type=F32)


def pack_grad(
    dests, rank_ref, other_ref, weight_ref, part_ref, post_ref, gated_ref, out_ref, away_ref
):
    width = out_ref.shape[1]
    weight = weight_ref[...]
    away_ref[...] = weight
    grad_gated = part_ref[...] + times_transposed(weight, other_ref[...])
    gated_ref[...] = grad_gated
    mixed = grad_gated * post_ref[...].T.astype(F32)
    for k in range(dests):
        out_ref[k] = mixed[k * width : (k + 1) * width].astype(BF16)


def group_order(n):
    first = n // 4
    order = []
    for i in range(first):
        order += [first + 3 * i, first + 3 * i + 1, first + 3 * i + 2, first - 1 - i]
    return order


def group_places(n):
    return [int(place) for place in np.argsort(group_order(n))]


def started(*copies):
    made = [pltpu.make_async_copy(*copy) for copy in copies]
    for copy in made:
        copy.start()
    return made


def forward_blocks(n, blocks, twist_ref, mid_ref, rows):
    length = mid_ref.shape[2] // 2
    for m, (real, imag) in enumerate(real_dft([x.astype(F32) for x in blocks], 2 * n)):
        cos, sin = twist_ref[m : m + 1], twist_ref[n + 1 + m : n + 2 + m]
        if m == 0:
            imag = jnp.zeros_like(real)
        elif imag is None:
            real, imag = real * cos, -(real * sin)
        else:
            real, imag = real * cos + imag * sin, imag * cos - real * sin
        mid_ref[m, rows, :length] = real.astype(mid_ref.dtype)
        mid_ref[m, rows, length:] = imag.astype(mid_ref.dtype)


def inverse_blocks(n, back, twist_ref):
    length = back.shape[1] // 2
    rows = back.shape[0] // (n + 1)
    spectrum = []
    for m in range(n + 1):
        cos, sin = twist_ref[m : m + 1], twist_ref[n + 1 + m : n + 2 + m]
        at = slice(m * rows, (m + 1) * rows)
        real, imag = back[at, :length], back[at, length:]
        if m == 0:
            spectrum.append((0.5 * real, None))
        elif m == n:
            spectrum.append((0.5 * (real * cos - imag * sin), None))
        else:
            spectrum.append((real * cos - imag * sin, real * sin + imag * cos))
    return [x.astype(BF16) for x in real_dft_transposed(spectrum, 2 * n, True)]


def inner_product(values_ref, matrix):
    count, rows, wide = values_ref.shape
    values = values_ref[...].reshape(count * rows, wide).astype(BF16)
    return jnp.dot(values, matrix, preferred_element_type=F32)


def dft_matrices(dft_ref, points):
    length = dft_ref.shape[0]
    cos, sin = dft_ref[:, :length], dft_ref[:, length:]
    forward = jnp.concatenate(
        [jnp.concatenate([cos, -sin], axis=1), jnp.concatenate([sin, cos], axis=1)], axis=0
    )
    cos, sin = cos * (1.0 / points), sin * (1.0 / points)
    back = jnp.concatenate(
        [jnp.concatenate([cos, sin], axis=1), jnp.concatenate([-sin, cos], axis=1)], axis=0
    )
    return forward, back


def row_chunks(rows):
    return max(1, rows // 16)


def mix_forward(
    n,
    pair_ref,
    grad_ref,
    twist_ref,
    dft_ref,
    both_ref,
    filt_ref,
    mid_ref,
    prod_ref,
):
    length = twist_ref.shape[1]
    width = grad_ref.shape[1]
    chunks = row_chunks(width)
    step = width // chunks
    forward, back = dft_matrices(dft_ref, n * length)
    both_ref[:, :, length:] = grad_ref[...]

    def transform(c):
        for kind in range(2):
            start = kind * width + c * step
            blocks = [pair_ref[b, start : start + step] for b in group_places(n)]
            forward_blocks(
                n, blocks, twist_ref, mid_ref.at[c], slice(kind * step, (kind + 1) * step)
            )

    transform(0)
    for c in range(chunks):
        at = slice(c * step, (c + 1) * step)
        if c + 1 < chunks:
            transform(c + 1)
        spec = inner_product(mid_ref.at[c], forward)
        for m in range(n + 1):
            first = 2 * m * step
            signal, filt = spec[first : first + step], spec[first + step : first + 2 * step]
            filt_ref[m, at] = filt.astype(filt_ref.dtype)
            real, imag = signal[:, :length], signal[:, length:]
            filt_real, filt_imag = filt[:, :length], filt[:, length:]
            prod_ref[c, m, :, :length] = (real * filt_real - imag * filt_imag).astype(
                prod_ref.dtype
            )
            prod_ref[c, m, :, length:] = (real * filt_imag + imag * filt_real).astype(
                prod_ref.dtype
            )
        mid = inner_product(prod_ref.at[c], back)
        for b, value in zip(group_places(n), inverse_blocks(n, mid, twist_ref)):
            both_ref[b, at, :length] = value


def mix_backward(
    n,
    both_ref,
    post_ref,
    twist_ref,
    dft_ref,
    filt_ref,
    weight_ref,
    out_hbm,
    gated_hbm,
    away_hbm,
    mid_ref,
    prod_ref,
    out_ref,
    gated_ref,
    away_ref,
    sems,
):
    length = twist_ref.shape[1]
    width = out_ref.shape[1]
    forward, back = dft_matrices(dft_ref, n * length)
    mixed = channel_rows(both_ref, length).T.astype(F32)
    gated = (post_ref[...].astype(F32) * mixed).astype(BF16)
    gated_ref[...] = gated
    away_ref[...] = jnp.dot(gated, weight_ref[...], preferred_element_type=F32).astype(BF16)
    copies = started((away_ref, away_hbm, sems.at[0]), (gated_ref, gated_hbm, sems.at[1]))
    chunks = row_chunks(width)
    step = width // chunks

    def transform(c):
        blocks = [both_ref[b, c * step : (c + 1) * step, length:] for b in group_places(n)]
        forward_blocks(n, blocks, twist_ref, mid_ref.at[c], slice(0, step))

    transform(0)
    for c in range(chunks):
        at = slice(c * step, (c + 1) * step)
        if c + 1 < chunks:
            transform(c + 1)
        spec = inner_product(mid_ref.at[c], forward)
        for m in range(n + 1):
            signal, filt = spec[m * step : (m + 1) * step], filt_ref[m, at].astype(F32)
            real, imag = signal[:, :length], signal[:, length:]
            filt_real, filt_imag = filt[:, :length], filt[:, length:]
            prod_ref[c, m, :, :length] = (filt_real * real + filt_imag * imag).astype(
                prod_ref.dtype
            )
            prod_ref[c, m, :, length:] = (filt_real * imag - filt_imag * real).astype(
                prod_ref.dtype
            )
        mid = inner_product(prod_ref.at[c], back)
        for b, value in zip(group_places(n), inverse_blocks(n, mid, twist_ref)):
            out_ref[b, at] = value
        if chunks == 1:
            copies += started((out_ref, out_hbm, sems.at[2]))
        else:
            rows = pl.ds(c * step, step)
            copies += started((out_ref.at[:, rows], out_hbm.at[:, rows], sems.at[2 + c]))
    for copy in copies:
        copy.wait()


def channel_rows(blocks_ref, length):
    return jnp.concatenate(
        [blocks_ref[k, :, :length] for k in range(blocks_ref.shape[0])], axis=0
    )


def weight_copies(parts, side, weight_hbm, weight_ref, sems):
    channels, columns = weight_ref.shape
    rows = channels // parts
    start = pl.multiple_of(side * columns, LANES)
    return started(
        *(
            (
                weight_hbm.at[pl.ds(k * rows, rows), pl.ds(start, columns)],
                weight_ref.at[pl.ds(k * rows, rows)],
                sems[k],
            )
            for k in range(parts)
        )
    )


def part_products(copies, gated, weight_ref):
    rows = weight_ref.shape[0] // len(copies)
    total = None
    for k, copy in enumerate(copies):
        copy.wait()
        at = slice(k * rows, (k + 1) * rows)
        product = jnp.dot(gated[:, at], weight_ref[at], preferred_element_type=F32)
        total = product if total is None else total + product
    return total


def project_home(
    parts,
    rank_ref,
    gated_ref,
    both_ref,
    grad_ref,
    weight_hbm,
    home_ref,
    post_grad_ref,
    weight_ref,
    sems,
):
    copies = weight_copies(
        parts, rank_ref[0], weight_hbm, weight_ref, [sems.at[k] for k in range(parts)]
    )
    mixed = channel_rows(both_ref, grad_ref.shape[1]).astype(F32)
    post_grad_ref[...] = (grad_ref[...] * mixed).astype(BF16).T
    home_ref[...] = part_products(copies, gated_ref[...], weight_ref)


def finish(
    parts,
    token_ref,
    packed_ref,
    pre_ref,
    feat_ref,
    home_ref,
    other_ref,
    pre_grad_hbm,
    feat_grad_hbm,
    out_hbm,
    pre_grad_ref,
    feat_grad_ref,
    out_ref,
    sems,
):
    out_ref[...] = (home_ref[...] + other_ref[...].astype(F32)).astype(BF16)
    copies = started((out_ref, out_hbm, sems.at[2, 0]))
    keep = (token_ref[...] < BASES).astype(BF16)
    dests = packed_ref.shape[0] // parts
    cut = pre_ref.shape[1] // parts
    for k in range(parts):
        at = pl.ds(k * cut, cut)
        blocks = packed_ref.at[pl.ds(k * dests, dests)]
        grad = (channel_rows(blocks, blocks.shape[2]) * keep).T.astype(F32)
        pre_grad_ref[:, at] = (grad * feat_ref[:, at].astype(F32)).astype(BF16)
        feat_grad_ref[:, at] = (grad * pre_ref[:, at].astype(F32)).astype(BF16)
        copies += started(
            (pre_grad_ref.at[:, at], pre_grad_hbm.at[:, at], sems.at[0, k]),
            (feat_grad_ref.at[:, at], feat_grad_hbm.at[:, at], sems.at[1, k]),
        )
    for copy in copies:
        copy.wait()


def dft_tables(n, length):
    index = np.arange(length)
    angle = index[:, None] * index[None, :] % length * (2.0 * math.pi / length)
    dft = np.concatenate([np.cos(angle), np.sin(angle)], axis=1).astype(jnp.bfloat16)
    angle = np.arange(n + 1)[:, None] * index[None, :] * (math.pi / (n * length))
    twist = np.concatenate([np.cos(angle), np.sin(angle)], axis=0).astype(np.float32)
    return twist, dft


def call(kernel, outs, args, grid=None, blocks=None, out_blocks=None, flops=0, scratch=(), prefetch=0, from_hbm=()):
    leaves = jax.tree.leaves(outs)
    args = [
        pltpu.with_memory_space_constraint(x, pltpu.HBM) if k in from_hbm else x
        for k, x in enumerate(args)
    ]
    tensors = args[prefetch:]

    def spec(array, block):
        if block == "hbm":
            return pl.BlockSpec(memory_space=pltpu.HBM)
        if block is None:
            rank = len(array.shape)
            if grid is None:
                return pl.BlockSpec(memory_space=pltpu.VMEM)
            return pl.BlockSpec(array.shape, lambda *_: (0,) * rank)
        return pl.BlockSpec(*block)

    blocks = blocks or [None] * len(tensors)
    out_blocks = out_blocks or [None] * len(leaves)
    in_specs = [spec(x, b) for x, b in zip(tensors, blocks)]
    out_specs = [spec(x, b) for x, b in zip(leaves, out_blocks)]
    moved = sum(math.prod(x.shape) * np.dtype(x.dtype).itemsize for x in [*tensors, *leaves])
    return pl.pallas_call(
        kernel,
        out_shape=outs,
        grid_spec=pltpu.PrefetchScalarGridSpec(
            num_scalar_prefetch=prefetch,
            grid=grid or (),
            in_specs=in_specs,
            out_specs=out_specs if isinstance(outs, tuple) else out_specs[0],
            scratch_shapes=list(scratch),
        ),
        compiler_params=pltpu.CompilerParams(vmem_limit_bytes=VMEM_GRANT),
        cost_estimate=pl.CostEstimate(flops=flops, bytes_accessed=moved, transcendentals=0),
    )(*args)


def exchange(block):
    return lax.all_to_all(
        block,
        "ctx",
        split_axis=0,
        concat_axis=0,
        tiled=True,
        axis_index_groups=[group_order(block.shape[0])],
    )


def swap_tp(block):
    count = lax.axis_size("tp")
    assert count == 2
    return lax.ppermute(block, "tp", [(0, 1), (1, 0)])


def on_device(
    tables, post_gate, pre_gate, features, filters, token_ids, out_weight, out_grad
):
    n = lax.axis_size("ctx")
    length, channels = post_gate.shape
    columns = out_grad.shape[1]
    width = channels // n
    shape = jax.ShapeDtypeStruct
    one = (n, width, length)
    pair = (n, 2 * width, length)
    both = (n, width, 2 * length)
    twist, dft = tables
    tokens = token_ids.reshape(1, length)
    rank = lax.axis_index("tp").astype(jnp.int32).reshape(1)
    inner_flops = 2 * (n + 1) * (2 * length) ** 2 * width
    spec_shape = (n + 1, width, 2 * length)
    narrow = BF16 if width >= 16 else F32
    chunks = row_chunks(width)
    narrow_scratch = pltpu.VMEM((chunks, n + 1, width // chunks, 2 * length), narrow)

    def by_channels(steps):
        cut, dests = channels // steps, n // steps
        return (
            ((length, cut), lambda i, *_: (0, i)),
            ((cut, length), lambda i, *_: (i, 0)),
            ((dests, *one[1:]), lambda i, *_: (i, 0, 0)),
        )

    other_grad = swap_tp(out_grad)
    steps = 2
    flat, _, _ = by_channels(steps)
    pair_out = call(
        functools.partial(pack_inputs, n // steps),
        pltpu.HBM(pair, BF16),
        (tokens, pre_gate, features, filters),
        grid=(steps,),
        blocks=[None, flat, flat, flat],
        out_blocks=[((n // steps, *pair[1:]), lambda i, *_: (i, 0, 0))],
        from_hbm=range(4),
    )
    pair_in = exchange(pair_out)
    steps = 4
    flat, turned, packed = by_channels(steps)
    weight_block = (channels // steps, columns)
    grad_part = call(
        own_grad,
        pltpu.VMEM((channels, length), F32),
        (rank, out_grad, out_weight),
        grid=(steps,),
        blocks=[None, (weight_block, lambda i, rank: (i, rank[0]))],
        out_blocks=[turned],
        flops=2 * length * channels * columns,
        prefetch=1,
        from_hbm=(1, 2),
    )
    grad_gated, grad_out, away_weight = call(
        functools.partial(pack_grad, n // steps),
        (
            pltpu.HBM((channels, length), F32),
            pltpu.VMEM(one, BF16),
            pltpu.VMEM((channels, columns), BF16),
        ),
        (rank, other_grad, out_weight, grad_part, post_gate),
        grid=(steps,),
        blocks=[None, (weight_block, lambda i, rank: (i, 1 - rank[0])), turned, flat],
        out_blocks=[turned, packed, (weight_block, lambda i, *_: (i, 0))],
        flops=2 * length * channels * columns,
        prefetch=1,
        from_hbm=(2, 4),
    )
    both_out, filt_spec = call(
        functools.partial(mix_forward, n),
        (
            shape(both, BF16),
            pltpu.VMEM(spec_shape, narrow),
        ),
        (pair_in, grad_out, twist, dft),
        flops=3 * inner_flops,
        scratch=[
            pltpu.VMEM((chunks, n + 1, 2 * width // chunks, 2 * length), BF16),
            narrow_scratch,
        ],
    )
    both_in = exchange(both_out)
    grad_back_out, gated, away = call(
        functools.partial(mix_backward, n),
        (
            pltpu.HBM(one, BF16),
            pltpu.HBM((length, channels), BF16),
            pltpu.HBM((length, columns), BF16),
        ),
        (both_in, post_gate, twist, dft, filt_spec, away_weight),
        out_blocks=["hbm", "hbm", "hbm"],
        flops=2 * inner_flops + 2 * length * channels * columns,
        scratch=[
            narrow_scratch,
            narrow_scratch,
            pltpu.VMEM(one, BF16),
            pltpu.VMEM((length, channels), BF16),
            pltpu.VMEM((length, columns), BF16),
            pltpu.SemaphoreType.DMA((2 + chunks,)),
        ],
    )
    grad_back_in = exchange(grad_back_out)
    other_part = swap_tp(away)
    parts = 2
    home, grad_post = call(
        functools.partial(project_home, parts),
        (shape((length, columns), F32), shape((length, channels), BF16)),
        (rank, gated, both_in, grad_gated, out_weight),
        grid=(1,),
        blocks=[None, (one, lambda *_: (0, 0, 0)), None, "hbm"],
        flops=2 * length * channels * columns,
        scratch=[pltpu.VMEM((channels, columns), BF16), pltpu.SemaphoreType.DMA((parts,))],
        prefetch=1,
    )
    flat = (length, channels)
    grad_pre, grad_features, output = call(
        functools.partial(finish, parts),
        (pltpu.HBM(flat, BF16), pltpu.HBM(flat, BF16), pltpu.HBM((length, columns), BF16)),
        (tokens, grad_back_in, pre_gate, features, home, other_part),
        out_blocks=["hbm"] * 3,
        scratch=[
            pltpu.VMEM(flat, BF16),
            pltpu.VMEM(flat, BF16),
            pltpu.VMEM((length, columns), BF16),
            pltpu.SemaphoreType.DMA((3, parts)),
        ],
    )
    return (output, grad_post, grad_pre, grad_features)


def solution(mesh):
    in_specs = (
        P("ctx", "tp"),
        P("ctx", "tp"),
        P("ctx", "tp"),
        P("ctx", "tp"),
        P("ctx"),
        P("tp", None),
        P("ctx", "tp"),
    )
    out_specs = (P("ctx", "tp"), P("ctx", "tp"), P("ctx", "tp"), P("ctx", "tp"))

    def run(*args):
        n = mesh.shape["ctx"]
        tables = tuple(jnp.asarray(x) for x in dft_tables(n, args[0].shape[0] // n))
        return jax.shard_map(
            functools.partial(on_device, tables),
            mesh=mesh,
            in_specs=in_specs,
            out_specs=out_specs,
            check_vma=False,
        )(*args)

    return run
```

```python
import functools
import math

import jax
import jax.numpy as jnp
import numpy as np
from jax import lax
from jax.experimental import pallas as pl
from jax.experimental.pallas import tpu as pltpu
from jax.sharding import PartitionSpec as P

BASES = 4
LANES = 128
VMEM_GRANT = 24 * 2**20
F32 = jnp.float32
BF16 = jnp.bfloat16


def complex_dft(values, sign):
    length = len(values)
    if length == 1:
        return values
    half = length // 2
    even = [
        (values[b][0] + values[b + half][0], values[b][1] + values[b + half][1])
        for b in range(half)
    ]
    odd = [
        twist(
            (values[b][0] - values[b + half][0], values[b][1] - values[b + half][1]),
            sign * b,
            length,
        )
        for b in range(half)
    ]
    even = complex_dft(even, sign)
    odd = complex_dft(odd, sign)
    return [part for pair in zip(even, odd) for part in pair]


def twist(value, step, length):
    real, imag = value
    step = step % length
    if step == 0:
        return real, imag
    if 4 * step == length:
        return -imag, real
    if 2 * step == length:
        return -real, -imag
    if 4 * step == 3 * length:
        return imag, -real
    cos = math.cos(2.0 * math.pi * step / length)
    sin = math.sin(2.0 * math.pi * step / length)
    if 8 * step % length == 0:
        root = math.sqrt(0.5)
        signed_cos = 1.0 if cos > 0 else -1.0
        signed_sin = 1.0 if sin > 0 else -1.0
        a = real * root
        b = imag * root
        if signed_cos == signed_sin:
            return (a - b, a + b) if signed_cos > 0 else (b - a, -a - b)
        return (a + b, b - a) if signed_cos > 0 else (-a - b, a - b)
    return real * cos - imag * sin, real * sin + imag * cos


def real_dft(values, length):
    if length == 2:
        if len(values) == 1:
            return [(values[0], None), (values[0], None)]
        return [(values[0] + values[1], None), (values[0] - values[1], None)]
    half, quarter = length // 2, length // 4
    if len(values) == length:
        total = [values[b] + values[b + half] for b in range(half)]
        rest = [values[b] - values[b + half] for b in range(half)]
    else:
        total = values
        rest = values
    out = [None] * (half + 1)
    for index, value in enumerate(real_dft(total, half)):
        out[2 * index] = value
    turned = [
        twist((rest[b], -rest[b + quarter]), -b, length) for b in range(quarter)
    ]
    for index, (real, imag) in enumerate(complex_dft(turned, -1)):
        place = 4 * index + 1
        if place <= half:
            out[place] = (real, imag)
        else:
            out[length - place] = (real, -imag)
    return out


def real_dft_transposed(spectrum, length, padded):
    if length == 2:
        first, second = spectrum[0][0], spectrum[1][0]
        return [first + second] if padded else [first + second, first - second]
    half, quarter = length // 2, length // 4
    total = real_dft_transposed(
        [spectrum[2 * index] for index in range(quarter + 1)], half, False
    )
    odd = []
    for index in range(quarter):
        place = 4 * index + 1
        if place <= half:
            odd.append(spectrum[place])
        else:
            real, imag = spectrum[length - place]
            odd.append((real, -imag))
    rest = [None] * half
    for b, value in enumerate(complex_dft(odd, 1)):
        real, imag = twist(value, b, length)
        rest[b] = real
        rest[b + quarter] = -imag
    low = [total[b] + rest[b] for b in range(half)]
    if padded:
        return low
    return low + [total[b] - rest[b] for b in range(half)]


def pack_inputs(dests, token_ref, pre_ref, feat_ref, filt_ref, out_ref):
    width = out_ref.shape[1] // 2
    keep = (token_ref[...] < BASES).astype(BF16)
    mixer = (pre_ref[...].astype(F32) * feat_ref[...].astype(F32)).astype(BF16).T * keep
    filt = filt_ref[...].astype(BF16).T
    for k in range(dests):
        at = slice(k * width, (k + 1) * width)
        out_ref[k] = jnp.concatenate([mixer[at], filt[at]], axis=0)


def own_grad(rank_ref, own_ref, weight_ref, out_ref):
    out_ref[...] = times_transposed(weight_ref[...], own_ref[...])


def times_transposed(left, right):
    return lax.dot_general(left, right, (((1,), (1,)), ((), ())), preferred_element_type=F32)


def pack_grad(
    dests, rank_ref, other_ref, weight_ref, part_ref, post_ref, gated_ref, out_ref, away_ref
):
    width = out_ref.shape[1]
    weight = weight_ref[...]
    away_ref[...] = weight
    grad_gated = part_ref[...] + times_transposed(weight, other_ref[...])
    gated_ref[...] = grad_gated
    mixed = grad_gated * post_ref[...].T.astype(F32)
    for k in range(dests):
        out_ref[k] = mixed[k * width : (k + 1) * width].astype(BF16)


def group_order(n):
    half = n // 2
    return [rank for i in range(half) for rank in (half + i, half - 1 - i)]


def group_places(n):
    return [int(place) for place in np.argsort(group_order(n))]


def started(*copies):
    made = [pltpu.make_async_copy(*copy) for copy in copies]
    for copy in made:
        copy.start()
    return made


def forward_blocks(n, blocks, twist_ref, mid_ref, rows):
    length = mid_ref.shape[2] // 2
    for m, (real, imag) in enumerate(real_dft([x.astype(F32) for x in blocks], 2 * n)):
        cos, sin = twist_ref[m : m + 1], twist_ref[n + 1 + m : n + 2 + m]
        if m == 0:
            imag = jnp.zeros_like(real)
        elif imag is None:
            real, imag = real * cos, -(real * sin)
        else:
            real, imag = real * cos + imag * sin, imag * cos - real * sin
        mid_ref[m, rows, :length] = real.astype(mid_ref.dtype)
        mid_ref[m, rows, length:] = imag.astype(mid_ref.dtype)


def inverse_blocks(n, back, twist_ref):
    length = back.shape[1] // 2
    rows = back.shape[0] // (n + 1)
    spectrum = []
    for m in range(n + 1):
        cos, sin = twist_ref[m : m + 1], twist_ref[n + 1 + m : n + 2 + m]
        at = slice(m * rows, (m + 1) * rows)
        real, imag = back[at, :length], back[at, length:]
        if m == 0:
            spectrum.append((0.5 * real, None))
        elif m == n:
            spectrum.append((0.5 * (real * cos - imag * sin), None))
        else:
            spectrum.append((real * cos - imag * sin, real * sin + imag * cos))
    return [x.astype(BF16) for x in real_dft_transposed(spectrum, 2 * n, True)]


def inner_product(values_ref, matrix):
    count, rows, wide = values_ref.shape
    values = values_ref[...].reshape(count * rows, wide).astype(BF16)
    return jnp.dot(values, matrix, preferred_element_type=F32)


def dft_matrices(dft_ref, points):
    length = dft_ref.shape[0]
    cos, sin = dft_ref[:, :length], dft_ref[:, length:]
    forward = jnp.concatenate(
        [jnp.concatenate([cos, -sin], axis=1), jnp.concatenate([sin, cos], axis=1)], axis=0
    )
    cos, sin = cos * (1.0 / points), sin * (1.0 / points)
    back = jnp.concatenate(
        [jnp.concatenate([cos, sin], axis=1), jnp.concatenate([-sin, cos], axis=1)], axis=0
    )
    return forward, back


def row_chunks(rows):
    return max(1, rows // 16)


def mix_forward(
    n,
    pair_ref,
    grad_ref,
    twist_ref,
    dft_ref,
    both_ref,
    filt_ref,
    mid_ref,
    prod_ref,
):
    length = twist_ref.shape[1]
    width = grad_ref.shape[1]
    chunks = row_chunks(width)
    step = width // chunks
    forward, back = dft_matrices(dft_ref, n * length)
    both_ref[:, :, length:] = grad_ref[...]

    def transform(c):
        for kind in range(2):
            start = kind * width + c * step
            blocks = [pair_ref[b, start : start + step] for b in group_places(n)]
            forward_blocks(
                n, blocks, twist_ref, mid_ref.at[c], slice(kind * step, (kind + 1) * step)
            )

    transform(0)
    for c in range(chunks):
        at = slice(c * step, (c + 1) * step)
        if c + 1 < chunks:
            transform(c + 1)
        spec = inner_product(mid_ref.at[c], forward)
        for m in range(n + 1):
            first = 2 * m * step
            signal, filt = spec[first : first + step], spec[first + step : first + 2 * step]
            filt_ref[m, at] = filt.astype(filt_ref.dtype)
            real, imag = signal[:, :length], signal[:, length:]
            filt_real, filt_imag = filt[:, :length], filt[:, length:]
            prod_ref[c, m, :, :length] = (real * filt_real - imag * filt_imag).astype(
                prod_ref.dtype
            )
            prod_ref[c, m, :, length:] = (real * filt_imag + imag * filt_real).astype(
                prod_ref.dtype
            )
        mid = inner_product(prod_ref.at[c], back)
        for b, value in zip(group_places(n), inverse_blocks(n, mid, twist_ref)):
            both_ref[b, at, :length] = value


def mix_backward(
    n,
    both_ref,
    post_ref,
    twist_ref,
    dft_ref,
    filt_ref,
    weight_ref,
    out_hbm,
    gated_hbm,
    away_hbm,
    mid_ref,
    prod_ref,
    out_ref,
    gated_ref,
    away_ref,
    sems,
):
    length = twist_ref.shape[1]
    width = out_ref.shape[1]
    forward, back = dft_matrices(dft_ref, n * length)
    mixed = channel_rows(both_ref, length).T.astype(F32)
    gated = (post_ref[...].astype(F32) * mixed).astype(BF16)
    gated_ref[...] = gated
    away_ref[...] = jnp.dot(gated, weight_ref[...], preferred_element_type=F32).astype(BF16)
    copies = started((away_ref, away_hbm, sems.at[0]), (gated_ref, gated_hbm, sems.at[1]))
    chunks = row_chunks(width)
    step = width // chunks

    def transform(c):
        blocks = [both_ref[b, c * step : (c + 1) * step, length:] for b in group_places(n)]
        forward_blocks(n, blocks, twist_ref, mid_ref.at[c], slice(0, step))

    transform(0)
    for c in range(chunks):
        at = slice(c * step, (c + 1) * step)
        if c + 1 < chunks:
            transform(c + 1)
        spec = inner_product(mid_ref.at[c], forward)
        for m in range(n + 1):
            signal, filt = spec[m * step : (m + 1) * step], filt_ref[m, at].astype(F32)
            real, imag = signal[:, :length], signal[:, length:]
            filt_real, filt_imag = filt[:, :length], filt[:, length:]
            prod_ref[c, m, :, :length] = (filt_real * real + filt_imag * imag).astype(
                prod_ref.dtype
            )
            prod_ref[c, m, :, length:] = (filt_real * imag - filt_imag * real).astype(
                prod_ref.dtype
            )
        mid = inner_product(prod_ref.at[c], back)
        for b, value in zip(group_places(n), inverse_blocks(n, mid, twist_ref)):
            out_ref[b, at] = value
        if chunks == 1:
            copies += started((out_ref, out_hbm, sems.at[2]))
        else:
            rows = pl.ds(c * step, step)
            copies += started((out_ref.at[:, rows], out_hbm.at[:, rows], sems.at[2 + c]))
    for copy in copies:
        copy.wait()


def channel_rows(blocks_ref, length):
    return jnp.concatenate(
        [blocks_ref[k, :, :length] for k in range(blocks_ref.shape[0])], axis=0
    )


def weight_copies(parts, side, weight_hbm, weight_ref, sems):
    channels, columns = weight_ref.shape
    rows = channels // parts
    start = pl.multiple_of(side * columns, LANES)
    return started(
        *(
            (
                weight_hbm.at[pl.ds(k * rows, rows), pl.ds(start, columns)],
                weight_ref.at[pl.ds(k * rows, rows)],
                sems[k],
            )
            for k in range(parts)
        )
    )


def part_products(copies, gated, weight_ref):
    rows = weight_ref.shape[0] // len(copies)
    total = None
    for k, copy in enumerate(copies):
        copy.wait()
        at = slice(k * rows, (k + 1) * rows)
        product = jnp.dot(gated[:, at], weight_ref[at], preferred_element_type=F32)
        total = product if total is None else total + product
    return total


def project_home(
    parts,
    rank_ref,
    gated_ref,
    both_ref,
    grad_ref,
    weight_hbm,
    home_ref,
    post_grad_ref,
    weight_ref,
    sems,
):
    copies = weight_copies(
        parts, rank_ref[0], weight_hbm, weight_ref, [sems.at[k] for k in range(parts)]
    )
    mixed = channel_rows(both_ref, grad_ref.shape[1]).astype(F32)
    post_grad_ref[...] = (grad_ref[...] * mixed).astype(BF16).T
    home_ref[...] = part_products(copies, gated_ref[...], weight_ref)


def input_grads(
    parts,
    token_ref,
    packed_ref,
    pre_ref,
    feat_ref,
    pre_grad_hbm,
    feat_grad_hbm,
    pre_grad_ref,
    feat_grad_ref,
    sems,
):
    keep = (token_ref[...] < BASES).astype(BF16)
    dests = packed_ref.shape[0] // parts
    cut = pre_ref.shape[1] // parts
    copies = []
    for k in range(parts):
        at = pl.ds(k * cut, cut)
        blocks = packed_ref.at[pl.ds(k * dests, dests)]
        grad = (channel_rows(blocks, blocks.shape[2]) * keep).T.astype(F32)
        pre_grad_ref[:, at] = (grad * feat_ref[:, at].astype(F32)).astype(BF16)
        feat_grad_ref[:, at] = (grad * pre_ref[:, at].astype(F32)).astype(BF16)
        copies += started(
            (pre_grad_ref.at[:, at], pre_grad_hbm.at[:, at], sems.at[0, k]),
            (feat_grad_ref.at[:, at], feat_grad_hbm.at[:, at], sems.at[1, k]),
        )
    for copy in copies:
        copy.wait()


def add_halves(home_ref, other_ref, after_hbm, out_ref):
    out_ref[...] = (home_ref[...] + other_ref[...].astype(F32)).astype(BF16)


def dft_tables(n, length):
    index = np.arange(length)
    angle = index[:, None] * index[None, :] % length * (2.0 * math.pi / length)
    dft = np.concatenate([np.cos(angle), np.sin(angle)], axis=1).astype(jnp.bfloat16)
    angle = np.arange(n + 1)[:, None] * index[None, :] * (math.pi / (n * length))
    twist = np.concatenate([np.cos(angle), np.sin(angle)], axis=0).astype(np.float32)
    return twist, dft


def call(kernel, outs, args, grid=None, blocks=None, out_blocks=None, flops=0, scratch=(), prefetch=0, from_hbm=()):
    leaves = jax.tree.leaves(outs)
    args = [
        pltpu.with_memory_space_constraint(x, pltpu.HBM) if k in from_hbm else x
        for k, x in enumerate(args)
    ]
    tensors = args[prefetch:]

    def spec(array, block):
        if block == "hbm":
            return pl.BlockSpec(memory_space=pltpu.HBM)
        if block is None:
            rank = len(array.shape)
            if grid is None:
                return pl.BlockSpec(memory_space=pltpu.VMEM)
            return pl.BlockSpec(array.shape, lambda *_: (0,) * rank)
        return pl.BlockSpec(*block)

    blocks = blocks or [None] * len(tensors)
    out_blocks = out_blocks or [None] * len(leaves)
    in_specs = [spec(x, b) for x, b in zip(tensors, blocks)]
    out_specs = [spec(x, b) for x, b in zip(leaves, out_blocks)]
    moved = sum(math.prod(x.shape) * np.dtype(x.dtype).itemsize for x in [*tensors, *leaves])
    return pl.pallas_call(
        kernel,
        out_shape=outs,
        grid_spec=pltpu.PrefetchScalarGridSpec(
            num_scalar_prefetch=prefetch,
            grid=grid or (),
            in_specs=in_specs,
            out_specs=out_specs if isinstance(outs, tuple) else out_specs[0],
            scratch_shapes=list(scratch),
        ),
        compiler_params=pltpu.CompilerParams(vmem_limit_bytes=VMEM_GRANT),
        cost_estimate=pl.CostEstimate(flops=flops, bytes_accessed=moved, transcendentals=0),
    )(*args)


def exchange(block):
    return lax.all_to_all(
        block,
        "ctx",
        split_axis=0,
        concat_axis=0,
        tiled=True,
        axis_index_groups=[group_order(block.shape[0])],
    )


def swap_tp(block):
    count = lax.axis_size("tp")
    assert count == 2
    return lax.ppermute(block, "tp", [(0, 1), (1, 0)])


def on_device(
    tables, post_gate, pre_gate, features, filters, token_ids, out_weight, out_grad
):
    n = lax.axis_size("ctx")
    length, channels = post_gate.shape
    columns = out_grad.shape[1]
    width = channels // n
    shape = jax.ShapeDtypeStruct
    one = (n, width, length)
    pair = (n, 2 * width, length)
    both = (n, width, 2 * length)
    twist, dft = tables
    tokens = token_ids.reshape(1, length)
    rank = lax.axis_index("tp").astype(jnp.int32).reshape(1)
    inner_flops = 2 * (n + 1) * (2 * length) ** 2 * width
    spec_shape = (n + 1, width, 2 * length)
    narrow = BF16 if width >= 16 else F32
    chunks = row_chunks(width)
    narrow_scratch = pltpu.VMEM((chunks, n + 1, width // chunks, 2 * length), narrow)

    def by_channels(steps):
        cut, dests = channels // steps, n // steps
        return (
            ((length, cut), lambda i, *_: (0, i)),
            ((cut, length), lambda i, *_: (i, 0)),
            ((dests, *one[1:]), lambda i, *_: (i, 0, 0)),
        )

    other_grad = swap_tp(out_grad)
    steps = 2
    flat, _, _ = by_channels(steps)
    pair_out = call(
        functools.partial(pack_inputs, n // steps),
        pltpu.HBM(pair, BF16),
        (tokens, pre_gate, features, filters),
        grid=(steps,),
        blocks=[None, flat, flat, flat],
        out_blocks=[((n // steps, *pair[1:]), lambda i, *_: (i, 0, 0))],
        from_hbm=range(4),
    )
    pair_in = exchange(pair_out)
    steps = 4
    flat, turned, packed = by_channels(steps)
    weight_block = (channels // steps, columns)
    grad_part = call(
        own_grad,
        pltpu.VMEM((channels, length), F32),
        (rank, out_grad, out_weight),
        grid=(steps,),
        blocks=[None, (weight_block, lambda i, rank: (i, rank[0]))],
        out_blocks=[turned],
        flops=2 * length * channels * columns,
        prefetch=1,
        from_hbm=(1, 2),
    )
    grad_gated, grad_out, away_weight = call(
        functools.partial(pack_grad, n // steps),
        (
            pltpu.HBM((channels, length), F32),
            pltpu.VMEM(one, BF16),
            pltpu.VMEM((channels, columns), BF16),
        ),
        (rank, other_grad, out_weight, grad_part, post_gate),
        grid=(steps,),
        blocks=[None, (weight_block, lambda i, rank: (i, 1 - rank[0])), turned, flat],
        out_blocks=[turned, packed, (weight_block, lambda i, *_: (i, 0))],
        flops=2 * length * channels * columns,
        prefetch=1,
        from_hbm=(2, 4),
    )
    both_out, filt_spec = call(
        functools.partial(mix_forward, n),
        (
            shape(both, BF16),
            pltpu.VMEM(spec_shape, narrow),
        ),
        (pair_in, grad_out, twist, dft),
        flops=3 * inner_flops,
        scratch=[
            pltpu.VMEM((chunks, n + 1, 2 * width // chunks, 2 * length), BF16),
            narrow_scratch,
        ],
    )
    both_in = exchange(both_out)
    grad_back_out, gated, away = call(
        functools.partial(mix_backward, n),
        (
            pltpu.HBM(one, BF16),
            pltpu.HBM((length, channels), BF16),
            pltpu.HBM((length, columns), BF16),
        ),
        (both_in, post_gate, twist, dft, filt_spec, away_weight),
        out_blocks=["hbm", "hbm", "hbm"],
        flops=2 * inner_flops + 2 * length * channels * columns,
        scratch=[
            narrow_scratch,
            narrow_scratch,
            pltpu.VMEM(one, BF16),
            pltpu.VMEM((length, channels), BF16),
            pltpu.VMEM((length, columns), BF16),
            pltpu.SemaphoreType.DMA((2 + chunks,)),
        ],
    )
    grad_back_in = exchange(grad_back_out)
    other_part = swap_tp(away)
    parts = 2
    home, grad_post = call(
        functools.partial(project_home, parts),
        (shape((length, columns), F32), shape((length, channels), BF16)),
        (rank, gated, both_in, grad_gated, out_weight),
        grid=(1,),
        blocks=[None, (one, lambda *_: (0, 0, 0)), None, "hbm"],
        flops=2 * length * channels * columns,
        scratch=[pltpu.VMEM((channels, columns), BF16), pltpu.SemaphoreType.DMA((parts,))],
        prefetch=1,
    )
    flat = (length, channels)
    grad_pre, grad_features = call(
        functools.partial(input_grads, parts),
        (pltpu.HBM(flat, BF16), pltpu.HBM(flat, BF16)),
        (tokens, grad_back_in, pre_gate, features),
        out_blocks=["hbm"] * 2,
        scratch=[
            pltpu.VMEM(flat, BF16),
            pltpu.VMEM(flat, BF16),
            pltpu.SemaphoreType.DMA((2, parts)),
        ],
    )
    output = call(
        add_halves,
        pltpu.HBM((length, columns), BF16),
        (home, other_part, grad_features),
        blocks=[None, None, "hbm"],
        from_hbm=(2,),
    )
    return (output, grad_post, grad_pre, grad_features)


def solution(mesh):
    in_specs = (
        P("ctx", "tp"),
        P("ctx", "tp"),
        P("ctx", "tp"),
        P("ctx", "tp"),
        P("ctx"),
        P("tp", None),
        P("ctx", "tp"),
    )
    out_specs = (P("ctx", "tp"), P("ctx", "tp"), P("ctx", "tp"), P("ctx", "tp"))

    def run(*args):
        n = mesh.shape["ctx"]
        tables = tuple(jnp.asarray(x) for x in dft_tables(n, args[0].shape[0] // n))
        return jax.shard_map(
            functools.partial(on_device, tables),
            mesh=mesh,
            in_specs=in_specs,
            out_specs=out_specs,
            check_vma=False,
        )(*args)

    return run
```

```python
import functools
import math

import jax
import jax.numpy as jnp
import numpy as np
from jax import lax
from jax.experimental import pallas as pl
from jax.experimental.pallas import tpu as pltpu
from jax.sharding import PartitionSpec as P

BASES = 4
LANES = 128
VMEM_GRANT = 24 * 2**20
F32 = jnp.float32
BF16 = jnp.bfloat16


def complex_dft(values, sign):
    length = len(values)
    if length == 1:
        return values
    half = length // 2
    even = [
        (values[b][0] + values[b + half][0], values[b][1] + values[b + half][1])
        for b in range(half)
    ]
    odd = [
        twist(
            (values[b][0] - values[b + half][0], values[b][1] - values[b + half][1]),
            sign * b,
            length,
        )
        for b in range(half)
    ]
    even = complex_dft(even, sign)
    odd = complex_dft(odd, sign)
    return [part for pair in zip(even, odd) for part in pair]


def twist(value, step, length):
    real, imag = value
    step = step % length
    if step == 0:
        return real, imag
    if 4 * step == length:
        return -imag, real
    if 2 * step == length:
        return -real, -imag
    if 4 * step == 3 * length:
        return imag, -real
    cos = math.cos(2.0 * math.pi * step / length)
    sin = math.sin(2.0 * math.pi * step / length)
    if 8 * step % length == 0:
        root = math.sqrt(0.5)
        signed_cos = 1.0 if cos > 0 else -1.0
        signed_sin = 1.0 if sin > 0 else -1.0
        a = real * root
        b = imag * root
        if signed_cos == signed_sin:
            return (a - b, a + b) if signed_cos > 0 else (b - a, -a - b)
        return (a + b, b - a) if signed_cos > 0 else (-a - b, a - b)
    return real * cos - imag * sin, real * sin + imag * cos


def real_dft(values, length):
    if length == 2:
        if len(values) == 1:
            return [(values[0], None), (values[0], None)]
        return [(values[0] + values[1], None), (values[0] - values[1], None)]
    half, quarter = length // 2, length // 4
    if len(values) == length:
        total = [values[b] + values[b + half] for b in range(half)]
        rest = [values[b] - values[b + half] for b in range(half)]
    else:
        total = values
        rest = values
    out = [None] * (half + 1)
    for index, value in enumerate(real_dft(total, half)):
        out[2 * index] = value
    turned = [
        twist((rest[b], -rest[b + quarter]), -b, length) for b in range(quarter)
    ]
    for index, (real, imag) in enumerate(complex_dft(turned, -1)):
        place = 4 * index + 1
        if place <= half:
            out[place] = (real, imag)
        else:
            out[length - place] = (real, -imag)
    return out


def real_dft_transposed(spectrum, length, padded):
    if length == 2:
        first, second = spectrum[0][0], spectrum[1][0]
        return [first + second] if padded else [first + second, first - second]
    half, quarter = length // 2, length // 4
    total = real_dft_transposed(
        [spectrum[2 * index] for index in range(quarter + 1)], half, False
    )
    odd = []
    for index in range(quarter):
        place = 4 * index + 1
        if place <= half:
            odd.append(spectrum[place])
        else:
            real, imag = spectrum[length - place]
            odd.append((real, -imag))
    rest = [None] * half
    for b, value in enumerate(complex_dft(odd, 1)):
        real, imag = twist(value, b, length)
        rest[b] = real
        rest[b + quarter] = -imag
    low = [total[b] + rest[b] for b in range(half)]
    if padded:
        return low
    return low + [total[b] - rest[b] for b in range(half)]


def pack_inputs(dests, token_ref, pre_ref, feat_ref, filt_ref, out_ref):
    width = out_ref.shape[1] // 2
    keep = (token_ref[...] < BASES).astype(BF16)
    mixer = (pre_ref[...].astype(F32) * feat_ref[...].astype(F32)).astype(BF16).T * keep
    filt = filt_ref[...].astype(BF16).T
    for k in range(dests):
        at = slice(k * width, (k + 1) * width)
        out_ref[k] = jnp.concatenate([mixer[at], filt[at]], axis=0)


def own_grad(rank_ref, own_ref, weight_ref, out_ref):
    out_ref[...] = times_transposed(weight_ref[...], own_ref[...])


def times_transposed(left, right):
    return lax.dot_general(left, right, (((1,), (1,)), ((), ())), preferred_element_type=F32)


def pack_grad(
    dests, rank_ref, other_ref, weight_ref, part_ref, post_ref, gated_ref, out_ref, away_ref
):
    width = out_ref.shape[1]
    weight = weight_ref[...]
    away_ref[...] = weight
    grad_gated = part_ref[...] + times_transposed(weight, other_ref[...])
    gated_ref[...] = grad_gated
    mixed = grad_gated * post_ref[...].T.astype(F32)
    for k in range(dests):
        out_ref[k] = mixed[k * width : (k + 1) * width].astype(BF16)


def group_order(n, turn):
    first = (3 * n // 4, 3 * n // 4, 3 * n // 4)[turn]
    return sorted(range(n), key=lambda rank: (abs(rank - first), rank))


def block_places(n, turn):
    return [int(place) for place in np.argsort(group_order(n, turn))]


def channel_places(n, turn):
    places = block_places(n, turn)
    return [places[rank] for rank in group_order(n, 0)]


def started(*copies):
    made = [pltpu.make_async_copy(*copy) for copy in copies]
    for copy in made:
        copy.start()
    return made


def forward_blocks(n, blocks, twist_ref, mid_ref, rows):
    length = mid_ref.shape[2] // 2
    for m, (real, imag) in enumerate(real_dft([x.astype(F32) for x in blocks], 2 * n)):
        cos, sin = twist_ref[m : m + 1], twist_ref[n + 1 + m : n + 2 + m]
        if m == 0:
            imag = jnp.zeros_like(real)
        elif imag is None:
            real, imag = real * cos, -(real * sin)
        else:
            real, imag = real * cos + imag * sin, imag * cos - real * sin
        mid_ref[m, rows, :length] = real.astype(mid_ref.dtype)
        mid_ref[m, rows, length:] = imag.astype(mid_ref.dtype)


def inverse_blocks(n, back, twist_ref):
    length = back.shape[1] // 2
    rows = back.shape[0] // (n + 1)
    spectrum = []
    for m in range(n + 1):
        cos, sin = twist_ref[m : m + 1], twist_ref[n + 1 + m : n + 2 + m]
        at = slice(m * rows, (m + 1) * rows)
        real, imag = back[at, :length], back[at, length:]
        if m == 0:
            spectrum.append((0.5 * real, None))
        elif m == n:
            spectrum.append((0.5 * (real * cos - imag * sin), None))
        else:
            spectrum.append((real * cos - imag * sin, real * sin + imag * cos))
    return [x.astype(BF16) for x in real_dft_transposed(spectrum, 2 * n, True)]


def inner_product(values_ref, matrix):
    count, rows, wide = values_ref.shape
    values = values_ref[...].reshape(count * rows, wide).astype(BF16)
    return jnp.dot(values, matrix, preferred_element_type=F32)


def dft_matrices(dft_ref, points):
    length = dft_ref.shape[0]
    cos, sin = dft_ref[:, :length], dft_ref[:, length:]
    forward = jnp.concatenate(
        [jnp.concatenate([cos, -sin], axis=1), jnp.concatenate([sin, cos], axis=1)], axis=0
    )
    cos, sin = cos * (1.0 / points), sin * (1.0 / points)
    back = jnp.concatenate(
        [jnp.concatenate([cos, sin], axis=1), jnp.concatenate([-sin, cos], axis=1)], axis=0
    )
    return forward, back


def row_chunks(rows):
    return max(1, rows // 16)


def mix_forward(
    n,
    pair_ref,
    grad_ref,
    twist_ref,
    dft_ref,
    both_ref,
    filt_ref,
    mid_ref,
    prod_ref,
):
    length = twist_ref.shape[1]
    width = grad_ref.shape[1]
    chunks = row_chunks(width)
    step = width // chunks
    forward, back = dft_matrices(dft_ref, n * length)
    for group, place in enumerate(channel_places(n, 1)):
        both_ref[place, :, length:] = grad_ref[group]

    def transform(c):
        for kind in range(2):
            start = kind * width + c * step
            blocks = [pair_ref[b, start : start + step] for b in block_places(n, 0)]
            forward_blocks(
                n, blocks, twist_ref, mid_ref.at[c], slice(kind * step, (kind + 1) * step)
            )

    transform(0)
    for c in range(chunks):
        at = slice(c * step, (c + 1) * step)
        if c + 1 < chunks:
            transform(c + 1)
        spec = inner_product(mid_ref.at[c], forward)
        for m in range(n + 1):
            first = 2 * m * step
            signal, filt = spec[first : first + step], spec[first + step : first + 2 * step]
            filt_ref[m, at] = filt.astype(filt_ref.dtype)
            real, imag = signal[:, :length], signal[:, length:]
            filt_real, filt_imag = filt[:, :length], filt[:, length:]
            prod_ref[c, m, :, :length] = (real * filt_real - imag * filt_imag).astype(
                prod_ref.dtype
            )
            prod_ref[c, m, :, length:] = (real * filt_imag + imag * filt_real).astype(
                prod_ref.dtype
            )
        mid = inner_product(prod_ref.at[c], back)
        for b, value in zip(block_places(n, 1), inverse_blocks(n, mid, twist_ref)):
            both_ref[b, at, :length] = value


def mix_backward(
    n,
    both_ref,
    post_ref,
    twist_ref,
    dft_ref,
    filt_ref,
    weight_ref,
    out_hbm,
    gated_hbm,
    away_hbm,
    mid_ref,
    prod_ref,
    out_ref,
    gated_ref,
    away_ref,
    sems,
):
    length = twist_ref.shape[1]
    width = out_ref.shape[1]
    forward, back = dft_matrices(dft_ref, n * length)
    mixed = channel_rows(both_ref, length, channel_places(n, 1)).T.astype(F32)
    gated = (post_ref[...].astype(F32) * mixed).astype(BF16)
    gated_ref[...] = gated
    away_ref[...] = jnp.dot(gated, weight_ref[...], preferred_element_type=F32).astype(BF16)
    copies = started((away_ref, away_hbm, sems.at[0]), (gated_ref, gated_hbm, sems.at[1]))
    chunks = row_chunks(width)
    step = width // chunks

    def transform(c):
        blocks = [both_ref[b, c * step : (c + 1) * step, length:] for b in block_places(n, 1)]
        forward_blocks(n, blocks, twist_ref, mid_ref.at[c], slice(0, step))

    transform(0)
    for c in range(chunks):
        at = slice(c * step, (c + 1) * step)
        if c + 1 < chunks:
            transform(c + 1)
        spec = inner_product(mid_ref.at[c], forward)
        for m in range(n + 1):
            signal, filt = spec[m * step : (m + 1) * step], filt_ref[m, at].astype(F32)
            real, imag = signal[:, :length], signal[:, length:]
            filt_real, filt_imag = filt[:, :length], filt[:, length:]
            prod_ref[c, m, :, :length] = (filt_real * real + filt_imag * imag).astype(
                prod_ref.dtype
            )
            prod_ref[c, m, :, length:] = (filt_real * imag - filt_imag * real).astype(
                prod_ref.dtype
            )
        mid = inner_product(prod_ref.at[c], back)
        for b, value in zip(block_places(n, 2), inverse_blocks(n, mid, twist_ref)):
            out_ref[b, at] = value
        if chunks == 1:
            copies += started((out_ref, out_hbm, sems.at[2]))
        else:
            rows = pl.ds(c * step, step)
            copies += started((out_ref.at[:, rows], out_hbm.at[:, rows], sems.at[2 + c]))
    for copy in copies:
        copy.wait()


def channel_rows(blocks_ref, length, places):
    return jnp.concatenate([blocks_ref[k, :, :length] for k in places], axis=0)


def weight_copies(parts, side, weight_hbm, weight_ref, sems):
    channels, columns = weight_ref.shape
    rows = channels // parts
    start = pl.multiple_of(side * columns, LANES)
    return started(
        *(
            (
                weight_hbm.at[pl.ds(k * rows, rows), pl.ds(start, columns)],
                weight_ref.at[pl.ds(k * rows, rows)],
                sems[k],
            )
            for k in range(parts)
        )
    )


def part_products(copies, gated, weight_ref):
    rows = weight_ref.shape[0] // len(copies)
    total = None
    for k, copy in enumerate(copies):
        copy.wait()
        at = slice(k * rows, (k + 1) * rows)
        product = jnp.dot(gated[:, at], weight_ref[at], preferred_element_type=F32)
        total = product if total is None else total + product
    return total


def project_home(
    parts,
    rank_ref,
    gated_ref,
    both_ref,
    grad_ref,
    weight_hbm,
    home_ref,
    post_grad_ref,
    weight_ref,
    sems,
):
    copies = weight_copies(
        parts, rank_ref[0], weight_hbm, weight_ref, [sems.at[k] for k in range(parts)]
    )
    places = channel_places(both_ref.shape[0], 1)
    mixed = channel_rows(both_ref, grad_ref.shape[1], places).astype(F32)
    post_grad_ref[...] = (grad_ref[...] * mixed).astype(BF16).T
    home_ref[...] = part_products(copies, gated_ref[...], weight_ref)


def input_grads(
    parts,
    token_ref,
    packed_ref,
    pre_ref,
    feat_ref,
    pre_grad_hbm,
    feat_grad_hbm,
    pre_grad_ref,
    feat_grad_ref,
    sems,
):
    keep = (token_ref[...] < BASES).astype(BF16)
    places = channel_places(packed_ref.shape[0], 2)
    dests = len(places) // parts
    cut = pre_ref.shape[1] // parts
    copies = []
    for k in range(parts):
        at = pl.ds(k * cut, cut)
        here = places[k * dests : (k + 1) * dests]
        grad = (channel_rows(packed_ref, packed_ref.shape[2], here) * keep).T.astype(F32)
        pre_grad_ref[:, at] = (grad * feat_ref[:, at].astype(F32)).astype(BF16)
        feat_grad_ref[:, at] = (grad * pre_ref[:, at].astype(F32)).astype(BF16)
        copies += started(
            (pre_grad_ref.at[:, at], pre_grad_hbm.at[:, at], sems.at[0, k]),
            (feat_grad_ref.at[:, at], feat_grad_hbm.at[:, at], sems.at[1, k]),
        )
    for copy in copies:
        copy.wait()


def add_halves(home_ref, other_ref, after_hbm, out_ref):
    out_ref[...] = (home_ref[...] + other_ref[...].astype(F32)).astype(BF16)


def dft_tables(n, length):
    index = np.arange(length)
    angle = index[:, None] * index[None, :] % length * (2.0 * math.pi / length)
    dft = np.concatenate([np.cos(angle), np.sin(angle)], axis=1).astype(jnp.bfloat16)
    angle = np.arange(n + 1)[:, None] * index[None, :] * (math.pi / (n * length))
    twist = np.concatenate([np.cos(angle), np.sin(angle)], axis=0).astype(np.float32)
    return twist, dft


def call(kernel, outs, args, grid=None, blocks=None, out_blocks=None, flops=0, scratch=(), prefetch=0, from_hbm=()):
    leaves = jax.tree.leaves(outs)
    args = [
        pltpu.with_memory_space_constraint(x, pltpu.HBM) if k in from_hbm else x
        for k, x in enumerate(args)
    ]
    tensors = args[prefetch:]

    def spec(array, block):
        if block == "hbm":
            return pl.BlockSpec(memory_space=pltpu.HBM)
        if block is None:
            rank = len(array.shape)
            if grid is None:
                return pl.BlockSpec(memory_space=pltpu.VMEM)
            return pl.BlockSpec(array.shape, lambda *_: (0,) * rank)
        return pl.BlockSpec(*block)

    blocks = blocks or [None] * len(tensors)
    out_blocks = out_blocks or [None] * len(leaves)
    in_specs = [spec(x, b) for x, b in zip(tensors, blocks)]
    out_specs = [spec(x, b) for x, b in zip(leaves, out_blocks)]
    moved = sum(math.prod(x.shape) * np.dtype(x.dtype).itemsize for x in [*tensors, *leaves])
    return pl.pallas_call(
        kernel,
        out_shape=outs,
        grid_spec=pltpu.PrefetchScalarGridSpec(
            num_scalar_prefetch=prefetch,
            grid=grid or (),
            in_specs=in_specs,
            out_specs=out_specs if isinstance(outs, tuple) else out_specs[0],
            scratch_shapes=list(scratch),
        ),
        compiler_params=pltpu.CompilerParams(vmem_limit_bytes=VMEM_GRANT),
        cost_estimate=pl.CostEstimate(flops=flops, bytes_accessed=moved, transcendentals=0),
    )(*args)


def exchange(block, turn):
    return lax.all_to_all(
        block,
        "ctx",
        split_axis=0,
        concat_axis=0,
        tiled=True,
        axis_index_groups=[group_order(block.shape[0], turn)],
    )


def swap_tp(block):
    count = lax.axis_size("tp")
    assert count == 2
    return lax.ppermute(block, "tp", [(0, 1), (1, 0)])


def on_device(
    tables, post_gate, pre_gate, features, filters, token_ids, out_weight, out_grad
):
    n = lax.axis_size("ctx")
    length, channels = post_gate.shape
    columns = out_grad.shape[1]
    width = channels // n
    shape = jax.ShapeDtypeStruct
    one = (n, width, length)
    pair = (n, 2 * width, length)
    both = (n, width, 2 * length)
    twist, dft = tables
    tokens = token_ids.reshape(1, length)
    rank = lax.axis_index("tp").astype(jnp.int32).reshape(1)
    inner_flops = 2 * (n + 1) * (2 * length) ** 2 * width
    spec_shape = (n + 1, width, 2 * length)
    narrow = BF16 if width >= 16 else F32
    chunks = row_chunks(width)
    narrow_scratch = pltpu.VMEM((chunks, n + 1, width // chunks, 2 * length), narrow)

    def by_channels(steps):
        cut, dests = channels // steps, n // steps
        return (
            ((length, cut), lambda i, *_: (0, i)),
            ((cut, length), lambda i, *_: (i, 0)),
            ((dests, *one[1:]), lambda i, *_: (i, 0, 0)),
        )

    other_grad = swap_tp(out_grad)
    steps = 2
    flat, _, _ = by_channels(steps)
    pair_out = call(
        functools.partial(pack_inputs, n // steps),
        pltpu.HBM(pair, BF16),
        (tokens, pre_gate, features, filters),
        grid=(steps,),
        blocks=[None, flat, flat, flat],
        out_blocks=[((n // steps, *pair[1:]), lambda i, *_: (i, 0, 0))],
        from_hbm=range(4),
    )
    pair_in = exchange(pair_out, 0)
    steps = 4
    flat, turned, packed = by_channels(steps)
    weight_block = (channels // steps, columns)
    grad_part = call(
        own_grad,
        pltpu.VMEM((channels, length), F32),
        (rank, out_grad, out_weight),
        grid=(steps,),
        blocks=[None, (weight_block, lambda i, rank: (i, rank[0]))],
        out_blocks=[turned],
        flops=2 * length * channels * columns,
        prefetch=1,
        from_hbm=(1, 2),
    )
    grad_gated, grad_out, away_weight = call(
        functools.partial(pack_grad, n // steps),
        (
            pltpu.HBM((channels, length), F32),
            pltpu.VMEM(one, BF16),
            pltpu.VMEM((channels, columns), BF16),
        ),
        (rank, other_grad, out_weight, grad_part, post_gate),
        grid=(steps,),
        blocks=[None, (weight_block, lambda i, rank: (i, 1 - rank[0])), turned, flat],
        out_blocks=[turned, packed, (weight_block, lambda i, *_: (i, 0))],
        flops=2 * length * channels * columns,
        prefetch=1,
        from_hbm=(2, 4),
    )
    both_out, filt_spec = call(
        functools.partial(mix_forward, n),
        (
            shape(both, BF16),
            pltpu.VMEM(spec_shape, narrow),
        ),
        (pair_in, grad_out, twist, dft),
        flops=3 * inner_flops,
        scratch=[
            pltpu.VMEM((chunks, n + 1, 2 * width // chunks, 2 * length), BF16),
            narrow_scratch,
        ],
    )
    both_in = exchange(both_out, 1)
    grad_back_out, gated, away = call(
        functools.partial(mix_backward, n),
        (
            pltpu.HBM(one, BF16),
            pltpu.HBM((length, channels), BF16),
            pltpu.HBM((length, columns), BF16),
        ),
        (both_in, post_gate, twist, dft, filt_spec, away_weight),
        out_blocks=["hbm", "hbm", "hbm"],
        flops=2 * inner_flops + 2 * length * channels * columns,
        scratch=[
            narrow_scratch,
            narrow_scratch,
            pltpu.VMEM(one, BF16),
            pltpu.VMEM((length, channels), BF16),
            pltpu.VMEM((length, columns), BF16),
            pltpu.SemaphoreType.DMA((2 + chunks,)),
        ],
    )
    grad_back_in = exchange(grad_back_out, 2)
    other_part = swap_tp(away)
    parts = 2
    home, grad_post = call(
        functools.partial(project_home, parts),
        (shape((length, columns), F32), shape((length, channels), BF16)),
        (rank, gated, both_in, grad_gated, out_weight),
        grid=(1,),
        blocks=[None, (one, lambda *_: (0, 0, 0)), None, "hbm"],
        flops=2 * length * channels * columns,
        scratch=[pltpu.VMEM((channels, columns), BF16), pltpu.SemaphoreType.DMA((parts,))],
        prefetch=1,
    )
    flat = (length, channels)
    grad_pre, grad_features = call(
        functools.partial(input_grads, parts),
        (pltpu.HBM(flat, BF16), pltpu.HBM(flat, BF16)),
        (tokens, grad_back_in, pre_gate, features),
        out_blocks=["hbm"] * 2,
        scratch=[
            pltpu.VMEM(flat, BF16),
            pltpu.VMEM(flat, BF16),
            pltpu.SemaphoreType.DMA((2, parts)),
        ],
    )
    output = call(
        add_halves,
        pltpu.HBM((length, columns), BF16),
        (home, other_part, grad_features),
        blocks=[None, None, "hbm"],
        from_hbm=(2,),
    )
    return (output, grad_post, grad_pre, grad_features)


def solution(mesh):
    in_specs = (
        P("ctx", "tp"),
        P("ctx", "tp"),
        P("ctx", "tp"),
        P("ctx", "tp"),
        P("ctx"),
        P("tp", None),
        P("ctx", "tp"),
    )
    out_specs = (P("ctx", "tp"), P("ctx", "tp"), P("ctx", "tp"), P("ctx", "tp"))

    def run(*args):
        n = mesh.shape["ctx"]
        tables = tuple(jnp.asarray(x) for x in dft_tables(n, args[0].shape[0] // n))
        return jax.shard_map(
            functools.partial(on_device, tables),
            mesh=mesh,
            in_specs=in_specs,
            out_specs=out_specs,
            check_vma=False,
        )(*args)

    return run
```

```python
import functools
import math

import jax
import jax.numpy as jnp
import numpy as np
from jax import lax
from jax.experimental import pallas as pl
from jax.experimental.pallas import tpu as pltpu
from jax.sharding import PartitionSpec as P

BASES = 4
LANES = 128
VMEM_GRANT = 24 * 2**20
F32 = jnp.float32
BF16 = jnp.bfloat16


def complex_dft(values, sign):
    length = len(values)
    if length == 1:
        return values
    half = length // 2
    even = [
        (values[b][0] + values[b + half][0], values[b][1] + values[b + half][1])
        for b in range(half)
    ]
    odd = [
        twist(
            (values[b][0] - values[b + half][0], values[b][1] - values[b + half][1]),
            sign * b,
            length,
        )
        for b in range(half)
    ]
    even = complex_dft(even, sign)
    odd = complex_dft(odd, sign)
    return [part for pair in zip(even, odd) for part in pair]


def twist(value, step, length):
    real, imag = value
    step = step % length
    if step == 0:
        return real, imag
    if 4 * step == length:
        return -imag, real
    if 2 * step == length:
        return -real, -imag
    if 4 * step == 3 * length:
        return imag, -real
    cos = math.cos(2.0 * math.pi * step / length)
    sin = math.sin(2.0 * math.pi * step / length)
    if 8 * step % length == 0:
        root = math.sqrt(0.5)
        signed_cos = 1.0 if cos > 0 else -1.0
        signed_sin = 1.0 if sin > 0 else -1.0
        a = real * root
        b = imag * root
        if signed_cos == signed_sin:
            return (a - b, a + b) if signed_cos > 0 else (b - a, -a - b)
        return (a + b, b - a) if signed_cos > 0 else (-a - b, a - b)
    return real * cos - imag * sin, real * sin + imag * cos


def real_dft(values, length):
    if length == 2:
        if len(values) == 1:
            return [(values[0], None), (values[0], None)]
        return [(values[0] + values[1], None), (values[0] - values[1], None)]
    half, quarter = length // 2, length // 4
    if len(values) == length:
        total = [values[b] + values[b + half] for b in range(half)]
        rest = [values[b] - values[b + half] for b in range(half)]
    else:
        total = values
        rest = values
    out = [None] * (half + 1)
    for index, value in enumerate(real_dft(total, half)):
        out[2 * index] = value
    turned = [
        twist((rest[b], -rest[b + quarter]), -b, length) for b in range(quarter)
    ]
    for index, (real, imag) in enumerate(complex_dft(turned, -1)):
        place = 4 * index + 1
        if place <= half:
            out[place] = (real, imag)
        else:
            out[length - place] = (real, -imag)
    return out


def real_dft_transposed(spectrum, length, padded):
    if length == 2:
        first, second = spectrum[0][0], spectrum[1][0]
        return [first + second] if padded else [first + second, first - second]
    half, quarter = length // 2, length // 4
    total = real_dft_transposed(
        [spectrum[2 * index] for index in range(quarter + 1)], half, False
    )
    odd = []
    for index in range(quarter):
        place = 4 * index + 1
        if place <= half:
            odd.append(spectrum[place])
        else:
            real, imag = spectrum[length - place]
            odd.append((real, -imag))
    rest = [None] * half
    for b, value in enumerate(complex_dft(odd, 1)):
        real, imag = twist(value, b, length)
        rest[b] = real
        rest[b + quarter] = -imag
    low = [total[b] + rest[b] for b in range(half)]
    if padded:
        return low
    return low + [total[b] - rest[b] for b in range(half)]


def pack_inputs(dests, token_ref, pre_ref, feat_ref, filt_ref, out_ref):
    width = out_ref.shape[1] // 2
    keep = (token_ref[...] < BASES).astype(BF16)
    mixer = (pre_ref[...].astype(F32) * feat_ref[...].astype(F32)).astype(BF16).T * keep
    filt = filt_ref[...].astype(BF16).T
    for k in range(dests):
        at = slice(k * width, (k + 1) * width)
        out_ref[k] = jnp.concatenate([mixer[at], filt[at]], axis=0)


def own_grad(rank_ref, own_ref, weight_ref, out_ref):
    out_ref[...] = times_transposed(weight_ref[...], own_ref[...])


def times_transposed(left, right):
    return lax.dot_general(left, right, (((1,), (1,)), ((), ())), preferred_element_type=F32)


def pack_grad(
    dests, rank_ref, other_ref, weight_ref, part_ref, post_ref, gated_ref, out_ref, away_ref
):
    width = out_ref.shape[1]
    weight = weight_ref[...]
    away_ref[...] = weight
    grad_gated = part_ref[...] + times_transposed(weight, other_ref[...])
    gated_ref[...] = grad_gated
    mixed = grad_gated * post_ref[...].T.astype(F32)
    for k in range(dests):
        out_ref[k] = mixed[k * width : (k + 1) * width].astype(BF16)


def group_order(n):
    half = n // 2
    order = [rank for i in range(half) for rank in (half + i, half - 1 - i)]
    return [order[1], order[0], *order[2:]]


def group_places(n):
    return [int(place) for place in np.argsort(group_order(n))]


def started(*copies):
    made = [pltpu.make_async_copy(*copy) for copy in copies]
    for copy in made:
        copy.start()
    return made


def forward_blocks(n, blocks, twist_ref, mid_ref, rows):
    length = mid_ref.shape[2] // 2
    for m, (real, imag) in enumerate(real_dft([x.astype(F32) for x in blocks], 2 * n)):
        cos, sin = twist_ref[m : m + 1], twist_ref[n + 1 + m : n + 2 + m]
        if m == 0:
            imag = jnp.zeros_like(real)
        elif imag is None:
            real, imag = real * cos, -(real * sin)
        else:
            real, imag = real * cos + imag * sin, imag * cos - real * sin
        mid_ref[m, rows, :length] = real.astype(mid_ref.dtype)
        mid_ref[m, rows, length:] = imag.astype(mid_ref.dtype)


def inverse_blocks(n, back, twist_ref):
    length = back.shape[1] // 2
    rows = back.shape[0] // (n + 1)
    spectrum = []
    for m in range(n + 1):
        cos, sin = twist_ref[m : m + 1], twist_ref[n + 1 + m : n + 2 + m]
        at = slice(m * rows, (m + 1) * rows)
        real, imag = back[at, :length], back[at, length:]
        if m == 0:
            spectrum.append((0.5 * real, None))
        elif m == n:
            spectrum.append((0.5 * (real * cos - imag * sin), None))
        else:
            spectrum.append((real * cos - imag * sin, real * sin + imag * cos))
    return [x.astype(BF16) for x in real_dft_transposed(spectrum, 2 * n, True)]


def inner_product(values_ref, matrix):
    count, rows, wide = values_ref.shape
    values = values_ref[...].reshape(count * rows, wide).astype(BF16)
    return jnp.dot(values, matrix, preferred_element_type=F32)


def dft_matrices(dft_ref, points):
    length = dft_ref.shape[0]
    cos, sin = dft_ref[:, :length], dft_ref[:, length:]
    forward = jnp.concatenate(
        [jnp.concatenate([cos, -sin], axis=1), jnp.concatenate([sin, cos], axis=1)], axis=0
    )
    cos, sin = cos * (1.0 / points), sin * (1.0 / points)
    back = jnp.concatenate(
        [jnp.concatenate([cos, sin], axis=1), jnp.concatenate([-sin, cos], axis=1)], axis=0
    )
    return forward, back


def row_chunks(rows):
    return max(1, rows // 16)


def mix_forward(
    n,
    pair_ref,
    grad_ref,
    twist_ref,
    dft_ref,
    both_ref,
    filt_ref,
    mid_ref,
    prod_ref,
):
    length = twist_ref.shape[1]
    width = grad_ref.shape[1]
    chunks = row_chunks(width)
    step = width // chunks
    forward, back = dft_matrices(dft_ref, n * length)
    both_ref[:, :, length:] = grad_ref[...]

    def transform(c):
        for kind in range(2):
            start = kind * width + c * step
            blocks = [pair_ref[b, start : start + step] for b in group_places(n)]
            forward_blocks(
                n, blocks, twist_ref, mid_ref.at[c], slice(kind * step, (kind + 1) * step)
            )

    transform(0)
    for c in range(chunks):
        at = slice(c * step, (c + 1) * step)
        if c + 1 < chunks:
            transform(c + 1)
        spec = inner_product(mid_ref.at[c], forward)
        for m in range(n + 1):
            first = 2 * m * step
            signal, filt = spec[first : first + step], spec[first + step : first + 2 * step]
            filt_ref[m, at] = filt.astype(filt_ref.dtype)
            real, imag = signal[:, :length], signal[:, length:]
            filt_real, filt_imag = filt[:, :length], filt[:, length:]
            prod_ref[c, m, :, :length] = (real * filt_real - imag * filt_imag).astype(
                prod_ref.dtype
            )
            prod_ref[c, m, :, length:] = (real * filt_imag + imag * filt_real).astype(
                prod_ref.dtype
            )
        mid = inner_product(prod_ref.at[c], back)
        for b, value in zip(group_places(n), inverse_blocks(n, mid, twist_ref)):
            both_ref[b, at, :length] = value


def mix_backward(
    n,
    both_ref,
    post_ref,
    twist_ref,
    dft_ref,
    filt_ref,
    weight_ref,
    out_hbm,
    gated_hbm,
    away_hbm,
    mid_ref,
    prod_ref,
    out_ref,
    gated_ref,
    away_ref,
    sems,
):
    length = twist_ref.shape[1]
    width = out_ref.shape[1]
    forward, back = dft_matrices(dft_ref, n * length)
    mixed = channel_rows(both_ref, length).T.astype(F32)
    gated = (post_ref[...].astype(F32) * mixed).astype(BF16)
    gated_ref[...] = gated
    away_ref[...] = jnp.dot(gated, weight_ref[...], preferred_element_type=F32).astype(BF16)
    copies = started((away_ref, away_hbm, sems.at[0]), (gated_ref, gated_hbm, sems.at[1]))
    chunks = row_chunks(width)
    step = width // chunks

    def transform(c):
        blocks = [both_ref[b, c * step : (c + 1) * step, length:] for b in group_places(n)]
        forward_blocks(n, blocks, twist_ref, mid_ref.at[c], slice(0, step))

    transform(0)
    for c in range(chunks):
        at = slice(c * step, (c + 1) * step)
        if c + 1 < chunks:
            transform(c + 1)
        spec = inner_product(mid_ref.at[c], forward)
        for m in range(n + 1):
            signal, filt = spec[m * step : (m + 1) * step], filt_ref[m, at].astype(F32)
            real, imag = signal[:, :length], signal[:, length:]
            filt_real, filt_imag = filt[:, :length], filt[:, length:]
            prod_ref[c, m, :, :length] = (filt_real * real + filt_imag * imag).astype(
                prod_ref.dtype
            )
            prod_ref[c, m, :, length:] = (filt_real * imag - filt_imag * real).astype(
                prod_ref.dtype
            )
        mid = inner_product(prod_ref.at[c], back)
        for b, value in zip(group_places(n), inverse_blocks(n, mid, twist_ref)):
            out_ref[b, at] = value
        if chunks == 1:
            copies += started((out_ref, out_hbm, sems.at[2]))
        else:
            rows = pl.ds(c * step, step)
            copies += started((out_ref.at[:, rows], out_hbm.at[:, rows], sems.at[2 + c]))
    for copy in copies:
        copy.wait()


def channel_rows(blocks_ref, length):
    return jnp.concatenate(
        [blocks_ref[k, :, :length] for k in range(blocks_ref.shape[0])], axis=0
    )


def weight_copies(parts, side, weight_hbm, weight_ref, sems):
    channels, columns = weight_ref.shape
    rows = channels // parts
    start = pl.multiple_of(side * columns, LANES)
    return started(
        *(
            (
                weight_hbm.at[pl.ds(k * rows, rows), pl.ds(start, columns)],
                weight_ref.at[pl.ds(k * rows, rows)],
                sems[k],
            )
            for k in range(parts)
        )
    )


def part_products(copies, gated, weight_ref):
    rows = weight_ref.shape[0] // len(copies)
    total = None
    for k, copy in enumerate(copies):
        copy.wait()
        at = slice(k * rows, (k + 1) * rows)
        product = jnp.dot(gated[:, at], weight_ref[at], preferred_element_type=F32)
        total = product if total is None else total + product
    return total


def project_home(
    parts,
    rank_ref,
    gated_ref,
    both_ref,
    grad_ref,
    weight_hbm,
    home_ref,
    post_grad_ref,
    weight_ref,
    sems,
):
    copies = weight_copies(
        parts, rank_ref[0], weight_hbm, weight_ref, [sems.at[k] for k in range(parts)]
    )
    mixed = channel_rows(both_ref, grad_ref.shape[1]).astype(F32)
    post_grad_ref[...] = (grad_ref[...] * mixed).astype(BF16).T
    home_ref[...] = part_products(copies, gated_ref[...], weight_ref)


def input_grads(
    parts,
    token_ref,
    packed_ref,
    pre_ref,
    feat_ref,
    pre_grad_hbm,
    feat_grad_hbm,
    pre_grad_ref,
    feat_grad_ref,
    sems,
):
    keep = (token_ref[...] < BASES).astype(BF16)
    dests = packed_ref.shape[0] // parts
    cut = pre_ref.shape[1] // parts
    copies = []
    for k in range(parts):
        at = pl.ds(k * cut, cut)
        blocks = packed_ref.at[pl.ds(k * dests, dests)]
        grad = (channel_rows(blocks, blocks.shape[2]) * keep).T.astype(F32)
        pre_grad_ref[:, at] = (grad * feat_ref[:, at].astype(F32)).astype(BF16)
        feat_grad_ref[:, at] = (grad * pre_ref[:, at].astype(F32)).astype(BF16)
        copies += started(
            (pre_grad_ref.at[:, at], pre_grad_hbm.at[:, at], sems.at[0, k]),
            (feat_grad_ref.at[:, at], feat_grad_hbm.at[:, at], sems.at[1, k]),
        )
    for copy in copies:
        copy.wait()


def add_halves(home_ref, other_ref, after_hbm, out_ref):
    out_ref[...] = (home_ref[...] + other_ref[...].astype(F32)).astype(BF16)


def dft_tables(n, length):
    index = np.arange(length)
    angle = index[:, None] * index[None, :] % length * (2.0 * math.pi / length)
    dft = np.concatenate([np.cos(angle), np.sin(angle)], axis=1).astype(jnp.bfloat16)
    angle = np.arange(n + 1)[:, None] * index[None, :] * (math.pi / (n * length))
    twist = np.concatenate([np.cos(angle), np.sin(angle)], axis=0).astype(np.float32)
    return twist, dft


def call(kernel, outs, args, grid=None, blocks=None, out_blocks=None, flops=0, scratch=(), prefetch=0, from_hbm=()):
    leaves = jax.tree.leaves(outs)
    args = [
        pltpu.with_memory_space_constraint(x, pltpu.HBM) if k in from_hbm else x
        for k, x in enumerate(args)
    ]
    tensors = args[prefetch:]

    def spec(array, block):
        if block == "hbm":
            return pl.BlockSpec(memory_space=pltpu.HBM)
        if block is None:
            rank = len(array.shape)
            if grid is None:
                return pl.BlockSpec(memory_space=pltpu.VMEM)
            return pl.BlockSpec(array.shape, lambda *_: (0,) * rank)
        return pl.BlockSpec(*block)

    blocks = blocks or [None] * len(tensors)
    out_blocks = out_blocks or [None] * len(leaves)
    in_specs = [spec(x, b) for x, b in zip(tensors, blocks)]
    out_specs = [spec(x, b) for x, b in zip(leaves, out_blocks)]
    moved = sum(math.prod(x.shape) * np.dtype(x.dtype).itemsize for x in [*tensors, *leaves])
    return pl.pallas_call(
        kernel,
        out_shape=outs,
        grid_spec=pltpu.PrefetchScalarGridSpec(
            num_scalar_prefetch=prefetch,
            grid=grid or (),
            in_specs=in_specs,
            out_specs=out_specs if isinstance(outs, tuple) else out_specs[0],
            scratch_shapes=list(scratch),
        ),
        compiler_params=pltpu.CompilerParams(vmem_limit_bytes=VMEM_GRANT),
        cost_estimate=pl.CostEstimate(flops=flops, bytes_accessed=moved, transcendentals=0),
    )(*args)


def exchange(block):
    return lax.all_to_all(
        block,
        "ctx",
        split_axis=0,
        concat_axis=0,
        tiled=True,
        axis_index_groups=[group_order(block.shape[0])],
    )


def swap_tp(block):
    count = lax.axis_size("tp")
    assert count == 2
    return lax.ppermute(block, "tp", [(0, 1), (1, 0)])


def on_device(
    tables, post_gate, pre_gate, features, filters, token_ids, out_weight, out_grad
):
    n = lax.axis_size("ctx")
    length, channels = post_gate.shape
    columns = out_grad.shape[1]
    width = channels // n
    shape = jax.ShapeDtypeStruct
    one = (n, width, length)
    pair = (n, 2 * width, length)
    both = (n, width, 2 * length)
    twist, dft = tables
    tokens = token_ids.reshape(1, length)
    rank = lax.axis_index("tp").astype(jnp.int32).reshape(1)
    inner_flops = 2 * (n + 1) * (2 * length) ** 2 * width
    spec_shape = (n + 1, width, 2 * length)
    narrow = BF16 if width >= 16 else F32
    chunks = row_chunks(width)
    narrow_scratch = pltpu.VMEM((chunks, n + 1, width // chunks, 2 * length), narrow)

    def by_channels(steps):
        cut, dests = channels // steps, n // steps
        return (
            ((length, cut), lambda i, *_: (0, i)),
            ((cut, length), lambda i, *_: (i, 0)),
            ((dests, *one[1:]), lambda i, *_: (i, 0, 0)),
        )

    other_grad = swap_tp(out_grad)
    steps = 2
    flat, _, _ = by_channels(steps)
    pair_out = call(
        functools.partial(pack_inputs, n // steps),
        pltpu.HBM(pair, BF16),
        (tokens, pre_gate, features, filters),
        grid=(steps,),
        blocks=[None, flat, flat, flat],
        out_blocks=[((n // steps, *pair[1:]), lambda i, *_: (i, 0, 0))],
        from_hbm=range(4),
    )
    pair_in = exchange(pair_out)
    steps = 4
    flat, turned, packed = by_channels(steps)
    weight_block = (channels // steps, columns)
    grad_part = call(
        own_grad,
        pltpu.VMEM((channels, length), F32),
        (rank, out_grad, out_weight),
        grid=(steps,),
        blocks=[None, (weight_block, lambda i, rank: (i, rank[0]))],
        out_blocks=[turned],
        flops=2 * length * channels * columns,
        prefetch=1,
        from_hbm=(1, 2),
    )
    grad_gated, grad_out, away_weight = call(
        functools.partial(pack_grad, n // steps),
        (
            pltpu.HBM((channels, length), F32),
            pltpu.VMEM(one, BF16),
            pltpu.VMEM((channels, columns), BF16),
        ),
        (rank, other_grad, out_weight, grad_part, post_gate),
        grid=(steps,),
        blocks=[None, (weight_block, lambda i, rank: (i, 1 - rank[0])), turned, flat],
        out_blocks=[turned, packed, (weight_block, lambda i, *_: (i, 0))],
        flops=2 * length * channels * columns,
        prefetch=1,
        from_hbm=(2, 4),
    )
    both_out, filt_spec = call(
        functools.partial(mix_forward, n),
        (
            shape(both, BF16),
            pltpu.VMEM(spec_shape, narrow),
        ),
        (pair_in, grad_out, twist, dft),
        flops=3 * inner_flops,
        scratch=[
            pltpu.VMEM((chunks, n + 1, 2 * width // chunks, 2 * length), BF16),
            narrow_scratch,
        ],
    )
    both_in = exchange(both_out)
    grad_back_out, gated, away = call(
        functools.partial(mix_backward, n),
        (
            pltpu.HBM(one, BF16),
            pltpu.HBM((length, channels), BF16),
            pltpu.HBM((length, columns), BF16),
        ),
        (both_in, post_gate, twist, dft, filt_spec, away_weight),
        out_blocks=["hbm", "hbm", "hbm"],
        flops=2 * inner_flops + 2 * length * channels * columns,
        scratch=[
            narrow_scratch,
            narrow_scratch,
            pltpu.VMEM(one, BF16),
            pltpu.VMEM((length, channels), BF16),
            pltpu.VMEM((length, columns), BF16),
            pltpu.SemaphoreType.DMA((2 + chunks,)),
        ],
    )
    grad_back_in = exchange(grad_back_out)
    other_part = swap_tp(away)
    parts = 2
    home, grad_post = call(
        functools.partial(project_home, parts),
        (shape((length, columns), F32), shape((length, channels), BF16)),
        (rank, gated, both_in, grad_gated, out_weight),
        grid=(1,),
        blocks=[None, (one, lambda *_: (0, 0, 0)), None, "hbm"],
        flops=2 * length * channels * columns,
        scratch=[pltpu.VMEM((channels, columns), BF16), pltpu.SemaphoreType.DMA((parts,))],
        prefetch=1,
    )
    flat = (length, channels)
    grad_pre, grad_features = call(
        functools.partial(input_grads, parts),
        (pltpu.HBM(flat, BF16), pltpu.HBM(flat, BF16)),
        (tokens, grad_back_in, pre_gate, features),
        out_blocks=["hbm"] * 2,
        scratch=[
            pltpu.VMEM(flat, BF16),
            pltpu.VMEM(flat, BF16),
            pltpu.SemaphoreType.DMA((2, parts)),
        ],
    )
    output = call(
        add_halves,
        pltpu.HBM((length, columns), BF16),
        (home, other_part, grad_features),
        blocks=[None, None, "hbm"],
        from_hbm=(2,),
    )
    return (output, grad_post, grad_pre, grad_features)


def solution(mesh):
    in_specs = (
        P("ctx", "tp"),
        P("ctx", "tp"),
        P("ctx", "tp"),
        P("ctx", "tp"),
        P("ctx"),
        P("tp", None),
        P("ctx", "tp"),
    )
    out_specs = (P("ctx", "tp"), P("ctx", "tp"), P("ctx", "tp"), P("ctx", "tp"))

    def run(*args):
        n = mesh.shape["ctx"]
        tables = tuple(jnp.asarray(x) for x in dft_tables(n, args[0].shape[0] // n))
        return jax.shard_map(
            functools.partial(on_device, tables),
            mesh=mesh,
            in_specs=in_specs,
            out_specs=out_specs,
            check_vma=False,
        )(*args)

    return run
```

```python
import functools
import math

import jax
import jax.numpy as jnp
import numpy as np
from jax import lax
from jax.experimental import pallas as pl
from jax.experimental.pallas import tpu as pltpu
from jax.sharding import PartitionSpec as P

BASES = 4
LANES = 128
VMEM_GRANT = 24 * 2**20
F32 = jnp.float32
BF16 = jnp.bfloat16


def complex_dft(values, sign):
    length = len(values)
    if length == 1:
        return values
    half = length // 2
    even = [
        (values[b][0] + values[b + half][0], values[b][1] + values[b + half][1])
        for b in range(half)
    ]
    odd = [
        twist(
            (values[b][0] - values[b + half][0], values[b][1] - values[b + half][1]),
            sign * b,
            length,
        )
        for b in range(half)
    ]
    even = complex_dft(even, sign)
    odd = complex_dft(odd, sign)
    return [part for pair in zip(even, odd) for part in pair]


def twist(value, step, length):
    real, imag = value
    step = step % length
    if step == 0:
        return real, imag
    if 4 * step == length:
        return -imag, real
    if 2 * step == length:
        return -real, -imag
    if 4 * step == 3 * length:
        return imag, -real
    cos = math.cos(2.0 * math.pi * step / length)
    sin = math.sin(2.0 * math.pi * step / length)
    if 8 * step % length == 0:
        root = math.sqrt(0.5)
        signed_cos = 1.0 if cos > 0 else -1.0
        signed_sin = 1.0 if sin > 0 else -1.0
        a = real * root
        b = imag * root
        if signed_cos == signed_sin:
            return (a - b, a + b) if signed_cos > 0 else (b - a, -a - b)
        return (a + b, b - a) if signed_cos > 0 else (-a - b, a - b)
    return real * cos - imag * sin, real * sin + imag * cos


def real_dft(values, length):
    if length == 2:
        if len(values) == 1:
            return [(values[0], None), (values[0], None)]
        return [(values[0] + values[1], None), (values[0] - values[1], None)]
    half, quarter = length // 2, length // 4
    if len(values) == length:
        total = [values[b] + values[b + half] for b in range(half)]
        rest = [values[b] - values[b + half] for b in range(half)]
    else:
        total = values
        rest = values
    out = [None] * (half + 1)
    for index, value in enumerate(real_dft(total, half)):
        out[2 * index] = value
    turned = [
        twist((rest[b], -rest[b + quarter]), -b, length) for b in range(quarter)
    ]
    for index, (real, imag) in enumerate(complex_dft(turned, -1)):
        place = 4 * index + 1
        if place <= half:
            out[place] = (real, imag)
        else:
            out[length - place] = (real, -imag)
    return out


def real_dft_transposed(spectrum, length, padded):
    if length == 2:
        first, second = spectrum[0][0], spectrum[1][0]
        return [first + second] if padded else [first + second, first - second]
    half, quarter = length // 2, length // 4
    total = real_dft_transposed(
        [spectrum[2 * index] for index in range(quarter + 1)], half, False
    )
    odd = []
    for index in range(quarter):
        place = 4 * index + 1
        if place <= half:
            odd.append(spectrum[place])
        else:
            real, imag = spectrum[length - place]
            odd.append((real, -imag))
    rest = [None] * half
    for b, value in enumerate(complex_dft(odd, 1)):
        real, imag = twist(value, b, length)
        rest[b] = real
        rest[b + quarter] = -imag
    low = [total[b] + rest[b] for b in range(half)]
    if padded:
        return low
    return low + [total[b] - rest[b] for b in range(half)]


def pack_inputs(dests, token_ref, pre_ref, feat_ref, filt_ref, out_ref):
    width = out_ref.shape[1] // 2
    keep = (token_ref[...] < BASES).astype(BF16)
    mixer = (pre_ref[...].astype(F32) * feat_ref[...].astype(F32)).astype(BF16).T * keep
    filt = filt_ref[...].astype(BF16).T
    for k in range(dests):
        at = slice(k * width, (k + 1) * width)
        out_ref[k] = jnp.concatenate([mixer[at], filt[at]], axis=0)


def own_grad(rank_ref, own_ref, weight_ref, out_ref):
    out_ref[...] = times_transposed(weight_ref[...], own_ref[...])


def times_transposed(left, right):
    return lax.dot_general(left, right, (((1,), (1,)), ((), ())), preferred_element_type=F32)


def pack_grad(
    dests, rank_ref, other_ref, weight_ref, part_ref, post_ref, gated_ref, out_ref, away_ref
):
    width = out_ref.shape[1]
    weight = weight_ref[...]
    away_ref[...] = weight
    grad_gated = part_ref[...] + times_transposed(weight, other_ref[...])
    gated_ref[...] = grad_gated
    mixed = grad_gated * post_ref[...].T.astype(F32)
    for k in range(dests):
        out_ref[k] = mixed[k * width : (k + 1) * width].astype(BF16)


def group_order(n):
    half = n // 2
    order = [rank for i in range(half) for rank in (half + i, half - 1 - i)]
    first = n // 4 - 1
    return [first, *(rank for rank in order if rank != first)]


def group_places(n):
    return [int(place) for place in np.argsort(group_order(n))]


def started(*copies):
    made = [pltpu.make_async_copy(*copy) for copy in copies]
    for copy in made:
        copy.start()
    return made


def forward_blocks(n, blocks, twist_ref, mid_ref, rows):
    length = mid_ref.shape[2] // 2
    for m, (real, imag) in enumerate(real_dft([x.astype(F32) for x in blocks], 2 * n)):
        cos, sin = twist_ref[m : m + 1], twist_ref[n + 1 + m : n + 2 + m]
        if m == 0:
            imag = jnp.zeros_like(real)
        elif imag is None:
            real, imag = real * cos, -(real * sin)
        else:
            real, imag = real * cos + imag * sin, imag * cos - real * sin
        mid_ref[m, rows, :length] = real.astype(mid_ref.dtype)
        mid_ref[m, rows, length:] = imag.astype(mid_ref.dtype)


def inverse_blocks(n, back, twist_ref):
    length = back.shape[1] // 2
    rows = back.shape[0] // (n + 1)
    spectrum = []
    for m in range(n + 1):
        cos, sin = twist_ref[m : m + 1], twist_ref[n + 1 + m : n + 2 + m]
        at = slice(m * rows, (m + 1) * rows)
        real, imag = back[at, :length], back[at, length:]
        if m == 0:
            spectrum.append((0.5 * real, None))
        elif m == n:
            spectrum.append((0.5 * (real * cos - imag * sin), None))
        else:
            spectrum.append((real * cos - imag * sin, real * sin + imag * cos))
    return [x.astype(BF16) for x in real_dft_transposed(spectrum, 2 * n, True)]


def inner_product(values_ref, matrix):
    count, rows, wide = values_ref.shape
    values = values_ref[...].reshape(count * rows, wide).astype(BF16)
    return jnp.dot(values, matrix, preferred_element_type=F32)


def dft_matrices(dft_ref, points):
    length = dft_ref.shape[0]
    cos, sin = dft_ref[:, :length], dft_ref[:, length:]
    forward = jnp.concatenate(
        [jnp.concatenate([cos, -sin], axis=1), jnp.concatenate([sin, cos], axis=1)], axis=0
    )
    cos, sin = cos * (1.0 / points), sin * (1.0 / points)
    back = jnp.concatenate(
        [jnp.concatenate([cos, sin], axis=1), jnp.concatenate([-sin, cos], axis=1)], axis=0
    )
    return forward, back


def row_chunks(rows):
    return max(1, rows // 16)


def mix_forward(
    n,
    pair_ref,
    grad_ref,
    twist_ref,
    dft_ref,
    both_ref,
    filt_ref,
    mid_ref,
    prod_ref,
):
    length = twist_ref.shape[1]
    width = grad_ref.shape[1]
    chunks = row_chunks(width)
    step = width // chunks
    forward, back = dft_matrices(dft_ref, n * length)
    both_ref[:, :, length:] = grad_ref[...]

    def transform(c):
        for kind in range(2):
            start = kind * width + c * step
            blocks = [pair_ref[b, start : start + step] for b in group_places(n)]
            forward_blocks(
                n, blocks, twist_ref, mid_ref.at[c], slice(kind * step, (kind + 1) * step)
            )

    transform(0)
    for c in range(chunks):
        at = slice(c * step, (c + 1) * step)
        if c + 1 < chunks:
            transform(c + 1)
        spec = inner_product(mid_ref.at[c], forward)
        for m in range(n + 1):
            first = 2 * m * step
            signal, filt = spec[first : first + step], spec[first + step : first + 2 * step]
            filt_ref[m, at] = filt.astype(filt_ref.dtype)
            real, imag = signal[:, :length], signal[:, length:]
            filt_real, filt_imag = filt[:, :length], filt[:, length:]
            prod_ref[c, m, :, :length] = (real * filt_real - imag * filt_imag).astype(
                prod_ref.dtype
            )
            prod_ref[c, m, :, length:] = (real * filt_imag + imag * filt_real).astype(
                prod_ref.dtype
            )
        mid = inner_product(prod_ref.at[c], back)
        for b, value in zip(group_places(n), inverse_blocks(n, mid, twist_ref)):
            both_ref[b, at, :length] = value


def mix_backward(
    n,
    both_ref,
    post_ref,
    twist_ref,
    dft_ref,
    filt_ref,
    weight_ref,
    out_hbm,
    gated_hbm,
    away_hbm,
    mid_ref,
    prod_ref,
    out_ref,
    gated_ref,
    away_ref,
    sems,
):
    length = twist_ref.shape[1]
    width = out_ref.shape[1]
    forward, back = dft_matrices(dft_ref, n * length)
    mixed = channel_rows(both_ref, length).T.astype(F32)
    gated = (post_ref[...].astype(F32) * mixed).astype(BF16)
    gated_ref[...] = gated
    away_ref[...] = jnp.dot(gated, weight_ref[...], preferred_element_type=F32).astype(BF16)
    copies = started((away_ref, away_hbm, sems.at[0]), (gated_ref, gated_hbm, sems.at[1]))
    chunks = row_chunks(width)
    step = width // chunks

    def transform(c):
        blocks = [both_ref[b, c * step : (c + 1) * step, length:] for b in group_places(n)]
        forward_blocks(n, blocks, twist_ref, mid_ref.at[c], slice(0, step))

    transform(0)
    for c in range(chunks):
        at = slice(c * step, (c + 1) * step)
        if c + 1 < chunks:
            transform(c + 1)
        spec = inner_product(mid_ref.at[c], forward)
        for m in range(n + 1):
            signal, filt = spec[m * step : (m + 1) * step], filt_ref[m, at].astype(F32)
            real, imag = signal[:, :length], signal[:, length:]
            filt_real, filt_imag = filt[:, :length], filt[:, length:]
            prod_ref[c, m, :, :length] = (filt_real * real + filt_imag * imag).astype(
                prod_ref.dtype
            )
            prod_ref[c, m, :, length:] = (filt_real * imag - filt_imag * real).astype(
                prod_ref.dtype
            )
        mid = inner_product(prod_ref.at[c], back)
        for b, value in zip(group_places(n), inverse_blocks(n, mid, twist_ref)):
            out_ref[b, at] = value
        if chunks == 1:
            copies += started((out_ref, out_hbm, sems.at[2]))
        else:
            rows = pl.ds(c * step, step)
            copies += started((out_ref.at[:, rows], out_hbm.at[:, rows], sems.at[2 + c]))
    for copy in copies:
        copy.wait()


def channel_rows(blocks_ref, length):
    return jnp.concatenate(
        [blocks_ref[k, :, :length] for k in range(blocks_ref.shape[0])], axis=0
    )


def weight_copies(parts, side, weight_hbm, weight_ref, sems):
    channels, columns = weight_ref.shape
    rows = channels // parts
    start = pl.multiple_of(side * columns, LANES)
    return started(
        *(
            (
                weight_hbm.at[pl.ds(k * rows, rows), pl.ds(start, columns)],
                weight_ref.at[pl.ds(k * rows, rows)],
                sems[k],
            )
            for k in range(parts)
        )
    )


def part_products(copies, gated, weight_ref):
    rows = weight_ref.shape[0] // len(copies)
    total = None
    for k, copy in enumerate(copies):
        copy.wait()
        at = slice(k * rows, (k + 1) * rows)
        product = jnp.dot(gated[:, at], weight_ref[at], preferred_element_type=F32)
        total = product if total is None else total + product
    return total


def project_home(
    parts,
    rank_ref,
    gated_ref,
    both_ref,
    grad_ref,
    weight_hbm,
    home_ref,
    post_grad_ref,
    weight_ref,
    sems,
):
    copies = weight_copies(
        parts, rank_ref[0], weight_hbm, weight_ref, [sems.at[k] for k in range(parts)]
    )
    mixed = channel_rows(both_ref, grad_ref.shape[1]).astype(F32)
    post_grad_ref[...] = (grad_ref[...] * mixed).astype(BF16).T
    home_ref[...] = part_products(copies, gated_ref[...], weight_ref)


def input_grads(
    parts,
    token_ref,
    packed_ref,
    pre_ref,
    feat_ref,
    pre_grad_hbm,
    feat_grad_hbm,
    pre_grad_ref,
    feat_grad_ref,
    sems,
):
    keep = (token_ref[...] < BASES).astype(BF16)
    dests = packed_ref.shape[0] // parts
    cut = pre_ref.shape[1] // parts
    copies = []
    for k in range(parts):
        at = pl.ds(k * cut, cut)
        blocks = packed_ref.at[pl.ds(k * dests, dests)]
        grad = (channel_rows(blocks, blocks.shape[2]) * keep).T.astype(F32)
        pre_grad_ref[:, at] = (grad * feat_ref[:, at].astype(F32)).astype(BF16)
        feat_grad_ref[:, at] = (grad * pre_ref[:, at].astype(F32)).astype(BF16)
        copies += started(
            (pre_grad_ref.at[:, at], pre_grad_hbm.at[:, at], sems.at[0, k]),
            (feat_grad_ref.at[:, at], feat_grad_hbm.at[:, at], sems.at[1, k]),
        )
    for copy in copies:
        copy.wait()


def add_halves(home_ref, other_ref, after_hbm, out_ref):
    out_ref[...] = (home_ref[...] + other_ref[...].astype(F32)).astype(BF16)


def dft_tables(n, length):
    index = np.arange(length)
    angle = index[:, None] * index[None, :] % length * (2.0 * math.pi / length)
    dft = np.concatenate([np.cos(angle), np.sin(angle)], axis=1).astype(jnp.bfloat16)
    angle = np.arange(n + 1)[:, None] * index[None, :] * (math.pi / (n * length))
    twist = np.concatenate([np.cos(angle), np.sin(angle)], axis=0).astype(np.float32)
    return twist, dft


def call(kernel, outs, args, grid=None, blocks=None, out_blocks=None, flops=0, scratch=(), prefetch=0, from_hbm=()):
    leaves = jax.tree.leaves(outs)
    args = [
        pltpu.with_memory_space_constraint(x, pltpu.HBM) if k in from_hbm else x
        for k, x in enumerate(args)
    ]
    tensors = args[prefetch:]

    def spec(array, block):
        if block == "hbm":
            return pl.BlockSpec(memory_space=pltpu.HBM)
        if block is None:
            rank = len(array.shape)
            if grid is None:
                return pl.BlockSpec(memory_space=pltpu.VMEM)
            return pl.BlockSpec(array.shape, lambda *_: (0,) * rank)
        return pl.BlockSpec(*block)

    blocks = blocks or [None] * len(tensors)
    out_blocks = out_blocks or [None] * len(leaves)
    in_specs = [spec(x, b) for x, b in zip(tensors, blocks)]
    out_specs = [spec(x, b) for x, b in zip(leaves, out_blocks)]
    moved = sum(math.prod(x.shape) * np.dtype(x.dtype).itemsize for x in [*tensors, *leaves])
    return pl.pallas_call(
        kernel,
        out_shape=outs,
        grid_spec=pltpu.PrefetchScalarGridSpec(
            num_scalar_prefetch=prefetch,
            grid=grid or (),
            in_specs=in_specs,
            out_specs=out_specs if isinstance(outs, tuple) else out_specs[0],
            scratch_shapes=list(scratch),
        ),
        compiler_params=pltpu.CompilerParams(vmem_limit_bytes=VMEM_GRANT),
        cost_estimate=pl.CostEstimate(flops=flops, bytes_accessed=moved, transcendentals=0),
    )(*args)


def exchange(block):
    return lax.all_to_all(
        block,
        "ctx",
        split_axis=0,
        concat_axis=0,
        tiled=True,
        axis_index_groups=[group_order(block.shape[0])],
    )


def swap_tp(block):
    count = lax.axis_size("tp")
    assert count == 2
    return lax.ppermute(block, "tp", [(0, 1), (1, 0)])


def on_device(
    tables, post_gate, pre_gate, features, filters, token_ids, out_weight, out_grad
):
    n = lax.axis_size("ctx")
    length, channels = post_gate.shape
    columns = out_grad.shape[1]
    width = channels // n
    shape = jax.ShapeDtypeStruct
    one = (n, width, length)
    pair = (n, 2 * width, length)
    both = (n, width, 2 * length)
    twist, dft = tables
    tokens = token_ids.reshape(1, length)
    rank = lax.axis_index("tp").astype(jnp.int32).reshape(1)
    inner_flops = 2 * (n + 1) * (2 * length) ** 2 * width
    spec_shape = (n + 1, width, 2 * length)
    narrow = BF16 if width >= 16 else F32
    chunks = row_chunks(width)
    narrow_scratch = pltpu.VMEM((chunks, n + 1, width // chunks, 2 * length), narrow)

    def by_channels(steps):
        cut, dests = channels // steps, n // steps
        return (
            ((length, cut), lambda i, *_: (0, i)),
            ((cut, length), lambda i, *_: (i, 0)),
            ((dests, *one[1:]), lambda i, *_: (i, 0, 0)),
        )

    other_grad = swap_tp(out_grad)
    steps = 2
    flat, _, _ = by_channels(steps)
    pair_out = call(
        functools.partial(pack_inputs, n // steps),
        pltpu.HBM(pair, BF16),
        (tokens, pre_gate, features, filters),
        grid=(steps,),
        blocks=[None, flat, flat, flat],
        out_blocks=[((n // steps, *pair[1:]), lambda i, *_: (i, 0, 0))],
        from_hbm=range(4),
    )
    pair_in = exchange(pair_out)
    steps = 4
    flat, turned, packed = by_channels(steps)
    weight_block = (channels // steps, columns)
    grad_part = call(
        own_grad,
        pltpu.VMEM((channels, length), F32),
        (rank, out_grad, out_weight),
        grid=(steps,),
        blocks=[None, (weight_block, lambda i, rank: (i, rank[0]))],
        out_blocks=[turned],
        flops=2 * length * channels * columns,
        prefetch=1,
        from_hbm=(1, 2),
    )
    grad_gated, grad_out, away_weight = call(
        functools.partial(pack_grad, n // steps),
        (
            pltpu.HBM((channels, length), F32),
            pltpu.VMEM(one, BF16),
            pltpu.VMEM((channels, columns), BF16),
        ),
        (rank, other_grad, out_weight, grad_part, post_gate),
        grid=(steps,),
        blocks=[None, (weight_block, lambda i, rank: (i, 1 - rank[0])), turned, flat],
        out_blocks=[turned, packed, (weight_block, lambda i, *_: (i, 0))],
        flops=2 * length * channels * columns,
        prefetch=1,
        from_hbm=(2, 4),
    )
    both_out, filt_spec = call(
        functools.partial(mix_forward, n),
        (
            shape(both, BF16),
            pltpu.VMEM(spec_shape, narrow),
        ),
        (pair_in, grad_out, twist, dft),
        flops=3 * inner_flops,
        scratch=[
            pltpu.VMEM((chunks, n + 1, 2 * width // chunks, 2 * length), BF16),
            narrow_scratch,
        ],
    )
    both_in = exchange(both_out)
    grad_back_out, gated, away = call(
        functools.partial(mix_backward, n),
        (
            pltpu.HBM(one, BF16),
            pltpu.HBM((length, channels), BF16),
            pltpu.HBM((length, columns), BF16),
        ),
        (both_in, post_gate, twist, dft, filt_spec, away_weight),
        out_blocks=["hbm", "hbm", "hbm"],
        flops=2 * inner_flops + 2 * length * channels * columns,
        scratch=[
            narrow_scratch,
            narrow_scratch,
            pltpu.VMEM(one, BF16),
            pltpu.VMEM((length, channels), BF16),
            pltpu.VMEM((length, columns), BF16),
            pltpu.SemaphoreType.DMA((2 + chunks,)),
        ],
    )
    grad_back_in = exchange(grad_back_out)
    other_part = swap_tp(away)
    parts = 2
    home, grad_post = call(
        functools.partial(project_home, parts),
        (shape((length, columns), F32), shape((length, channels), BF16)),
        (rank, gated, both_in, grad_gated, out_weight),
        grid=(1,),
        blocks=[None, (one, lambda *_: (0, 0, 0)), None, "hbm"],
        flops=2 * length * channels * columns,
        scratch=[pltpu.VMEM((channels, columns), BF16), pltpu.SemaphoreType.DMA((parts,))],
        prefetch=1,
    )
    flat = (length, channels)
    grad_pre, grad_features = call(
        functools.partial(input_grads, parts),
        (pltpu.HBM(flat, BF16), pltpu.HBM(flat, BF16)),
        (tokens, grad_back_in, pre_gate, features),
        out_blocks=["hbm"] * 2,
        scratch=[
            pltpu.VMEM(flat, BF16),
            pltpu.VMEM(flat, BF16),
            pltpu.SemaphoreType.DMA((2, parts)),
        ],
    )
    output = call(
        add_halves,
        pltpu.HBM((length, columns), BF16),
        (home, other_part, grad_features),
        blocks=[None, None, "hbm"],
        from_hbm=(2,),
    )
    return (output, grad_post, grad_pre, grad_features)


def solution(mesh):
    in_specs = (
        P("ctx", "tp"),
        P("ctx", "tp"),
        P("ctx", "tp"),
        P("ctx", "tp"),
        P("ctx"),
        P("tp", None),
        P("ctx", "tp"),
    )
    out_specs = (P("ctx", "tp"), P("ctx", "tp"), P("ctx", "tp"), P("ctx", "tp"))

    def run(*args):
        n = mesh.shape["ctx"]
        tables = tuple(jnp.asarray(x) for x in dft_tables(n, args[0].shape[0] // n))
        return jax.shard_map(
            functools.partial(on_device, tables),
            mesh=mesh,
            in_specs=in_specs,
            out_specs=out_specs,
            check_vma=False,
        )(*args)

    return run
```
